32 devices in a mesh: seq: 8 (over z, y), dp: 4 (over x, core).
Axes of the slice: x: 2, y: 2, z: 4, core: 2. Of those that a mesh axis runs over, the one named last changes fastest.
Arguments:
- tokens: int32 [16, 1056], P('dp', 'seq'), may hold values from 0 to 255
- next_targets: int32 [16, 1056], P('dp', 'seq'), may hold values from 0 to 255
- triple_targets: int32 [16, 352, 3], P('dp', 'seq'), may hold values from 0 to 255
- loss_mask: int32 [16, 1056], P('dp', 'seq'), may hold values from 0 to 1
- embedding: float32 [256, 512], P(None, ('seq', 'dp')), may hold values from -6 to 6
- attention: float32 [2, 512, 1536], P(None, ('seq', 'dp')), may hold values from -0.25 to 0.25
- projection: float32 [2, 512, 512], P(None, ('seq', 'dp')), may hold values from -1 to 1
- expansion: float32 [2, 512, 2048], P(None, ('seq', 'dp')), may hold values from -0.25 to 0.25
- contraction: float32 [2, 2048, 512], P(None, None, ('seq', 'dp')), may hold values from -0.125 to 0.125
- readout: float32 [512, 256], P(('seq', 'dp')), may hold values from -0.25 to 0.25
- trigram: float32 [512, 768], P(('seq', 'dp')), may hold values from -0.25 to 0.25
- scales: float32 [6, 512], P(None, ('seq', 'dp')), may hold values from 0.3 to 2.5
- embedding_first: float32 [256, 512], P(None, ('seq', 'dp')), may hold values from -1.9073486e-05 to 1.9073486e-05
- attention_first: float32 [2, 512, 1536], P(None, ('seq', 'dp')), may hold values from -6.1035156e-05 to 6.1035156e-05
- projection_first: float32 [2, 512, 512], P(None, ('seq', 'dp')), may hold values from -6.1035156e-05 to 6.1035156e-05
- expansion_first: float32 [2, 512, 2048], P(None, ('seq', 'dp')), may hold values from -6.1035156e-05 to 6.1035156e-05
- contraction_first: float32 [2, 2048, 512], P(None, None, ('seq', 'dp')), may hold values from -6.1035156e-05 to 6.1035156e-05
- readout_first: float32 [512, 256], P(('seq', 'dp')), may hold values from -6.1035156e-05 to 6.1035156e-05
- trigram_first: float32 [512, 768], P(('seq', 'dp')), may hold values from -6.1035156e-05 to 6.1035156e-05
- scales_first: float32 [6, 512], P(None, ('seq', 'dp')), may hold values from -0.00024414062 to 0.00024414062
- embedding_second: float32 [256, 512], P(None, ('seq', 'dp')), may hold values from 7.1943606e-12 to 2.8777442e-11
- attention_second: float32 [2, 512, 1536], P(None, ('seq', 'dp')), may hold values from 7.1943604e-11 to 2.8777442e-10
- projection_second: float32 [2, 512, 512], P(None, ('seq', 'dp')), may hold values from 7.1943604e-11 to 2.8777442e-10
- expansion_second: float32 [2, 512, 2048], P(None, ('seq', 'dp')), may hold values from 7.1943604e-11 to 2.8777442e-10
- contraction_second: float32 [2, 2048, 512], P(None, None, ('seq', 'dp')), may hold values from 7.1943604e-11 to 2.8777442e-10
- readout_second: float32 [512, 256], P(('seq', 'dp')), may hold values from 7.1943604e-11 to 2.8777442e-10
- trigram_second: float32 [512, 768], P(('seq', 'dp')), may hold values from 7.1943604e-11 to 2.8777442e-10
- scales_second: float32 [6, 512], P(None, ('seq', 'dp')), may hold values from 1.1510977e-09 to 4.6043906e-09
Outputs:
- loss_sum: float32 [], replicated
- loss_count: float32 [], replicated
- global_norm: float32 [], replicated
- updated_embedding: float32 [256, 512], P(None, ('seq', 'dp'))
- updated_attention: float32 [2, 512, 1536], P(None, ('seq', 'dp'))
- updated_projection: float32 [2, 512, 512], P(None, ('seq', 'dp'))
- updated_expansion: float32 [2, 512, 2048], P(None, ('seq', 'dp'))
- updated_contraction: float32 [2, 2048, 512], P(None, None, ('seq', 'dp'))
- updated_readout: float32 [512, 256], P(('seq', 'dp'))
- updated_trigram: float32 [512, 768], P(('seq', 'dp'))
- updated_scales: float32 [6, 512], P(None, ('seq', 'dp'))
- momentum_embedding: float32 [256, 512], P(None, ('seq', 'dp'))
- momentum_attention: float32 [2, 512, 1536], P(None, ('seq', 'dp'))
- momentum_projection: float32 [2, 512, 512], P(None, ('seq', 'dp'))
- momentum_expansion: float32 [2, 512, 2048], P(None, ('seq', 'dp'))
- momentum_contraction: float32 [2, 2048, 512], P(None, None, ('seq', 'dp'))
- momentum_readout: float32 [512, 256], P(('seq', 'dp'))
- momentum_trigram: float32 [512, 768], P(('seq', 'dp'))
- momentum_scales: float32 [6, 512], P(None, ('seq', 'dp'))
- variance_embedding: float32 [256, 512], P(None, ('seq', 'dp'))
- variance_attention: float32 [2, 512, 1536], P(None, ('seq', 'dp'))
- variance_projection: float32 [2, 512, 512], P(None, ('seq', 'dp'))
- variance_expansion: float32 [2, 512, 2048], P(None, ('seq', 'dp'))
- variance_contraction: float32 [2, 2048, 512], P(None, None, ('seq', 'dp'))
- variance_readout: float32 [512, 256], P(('seq', 'dp'))
- variance_trigram: float32 [512, 768], P(('seq', 'dp'))
- variance_scales: float32 [6, 512], P(None, ('seq', 'dp'))
The draws below stay inside these ranges and needn't reach their ends.
All inputs are finite; a program needn't handle non-finite values.
Results may differ from the reference program's by a relative error of at most 0.02.
Values may be sent and summed in bfloat16 or wider, within the bound.
No kernel may reach another device: no remote copies, remote signals or barrier semaphores. Data moves between devices by JAX's collectives and lax.ppermute only.
A program may use at most 512 MiB of HBM per device.

```python
import math
import jax
import jax.numpy as jnp
from jax import lax

D = 512
HEADS = 8
FF = 2048
V = 256
STEP = 10
LENGTH = 1056
SHORT = 352
SEQS = 16
NPARAM = 6949888


def draw_loss_mask(key, part):
    key = jax.random.fold_in(key, 11)
    picks = jax.random.randint(key, (SEQS, LENGTH), 0, 1000)
    place = jnp.arange(LENGTH, dtype=jnp.int32)
    limit = 250 + 500 * place // max(LENGTH - 1, 1)
    return (picks < limit[None, :]).astype(jnp.int32)


def draw_scales(key, part):
    key = jax.random.fold_in(key, 23)
    place = jnp.arange(D, dtype=jnp.float32) / (D - 1)
    base = 0.6 + 1.2 * place
    noise = jax.random.uniform(key, (6, D), jnp.float32, 0.85, 1.15)
    return base[None, :] * noise


def place_ends(array, own_key, smallest, top_value):
    shape = array.shape
    spot = [jax.random.randint(jax.random.fold_in(own_key, axis), (), 0, shape[axis]) for axis in range(len(shape))]
    array = array.at[tuple(spot)].set(smallest)
    longest = shape.index(max(shape))
    spot[longest] = (spot[longest] + 1) % shape[longest]
    return array.at[tuple(spot)].set(top_value)


def block_levels(rng, extent, shards, least, high):
    loudness, own = 1.0, jax.random.fold_in(rng, 6)
    for axis_at, blocks in shards:
        steps = jnp.exp(jax.random.uniform(jax.random.fold_in(own, axis_at), (blocks,), jnp.float32, least / len(shards), high / len(shards)))
        loudness = loudness * jnp.repeat(steps, extent[axis_at] // blocks).reshape([-1 if axis == axis_at else 1 for axis in range(len(extent))])
    return loudness


def centred(rng, extent, width, most, shards=(), kind=jnp.bfloat16):
    gain = block_levels(rng, extent, shards, -0.22, 0.18) if shards else 1.0
    result = jax.random.normal(rng, extent, jnp.float32) * width * gain
    return jnp.minimum(jnp.maximum(result, -most), most).astype(kind)


def setup_inputs(seed: int = 0) -> dict:
    keys = jax.random.split(jax.random.key(seed), 29)
    return {
        "tokens": place_ends(jax.random.randint(keys[0], (SEQS, LENGTH), 0, V), jax.random.fold_in(keys[0], 1), 0, V - 1).astype(jnp.int32),
        "next_targets": place_ends(jax.random.randint(keys[1], (SEQS, LENGTH), 0, V), jax.random.fold_in(keys[1], 1), 0, V - 1).astype(jnp.int32),
        "triple_targets": place_ends(jax.random.randint(keys[2], (SEQS, SHORT, 3), 0, V), jax.random.fold_in(keys[2], 1), 0, V - 1).astype(jnp.int32),
        "loss_mask": draw_loss_mask(jax.random.fold_in(keys[28], 71), 0),
        "embedding": centred(keys[4], (V, D), 1.0, 6.0, ((1, 32),), jnp.float32),
        "attention": centred(keys[5], (2, D, 3 * D), D ** -0.5, 0.25, ((1, 32),), jnp.float32),
        "projection": centred(keys[6], (2, D, D), (max(4, D * 64 // LENGTH)) ** -0.5, 1.0, ((1, 32),), jnp.float32),
        "expansion": centred(keys[7], (2, D, FF), D ** -0.5, 0.25, ((1, 32),), jnp.float32),
        "contraction": centred(keys[8], (2, FF, D), FF ** -0.5, 0.125, ((2, 32),), jnp.float32),
        "readout": centred(keys[9], (D, V), D ** -0.5, 0.25, ((0, 32),), jnp.float32),
        "trigram": centred(keys[10], (D, 3 * V), D ** -0.5, 0.25, ((0, 32),), jnp.float32),
        "scales": draw_scales(jax.random.fold_in(keys[28], 71), 0),
        "embedding_first": centred(keys[12], (V, D), (0.0032 * NPARAM ** -0.5), 1.9073486328125e-05, ((1, 32),), jnp.float32),
        "attention_first": centred(keys[13], (2, D, 3 * D), (0.011 * NPARAM ** -0.5), 6.103515625e-05, ((1, 32),), jnp.float32),
        "projection_first": centred(keys[14], (2, D, D), (0.011 * NPARAM ** -0.5), 6.103515625e-05, ((1, 32),), jnp.float32),
        "expansion_first": centred(keys[15], (2, D, FF), (0.011 * NPARAM ** -0.5), 6.103515625e-05, ((1, 32),), jnp.float32),
        "contraction_first": centred(keys[16], (2, FF, D), (0.011 * NPARAM ** -0.5), 6.103515625e-05, ((2, 32),), jnp.float32),
        "readout_first": centred(keys[17], (D, V), (0.011 * NPARAM ** -0.5), 6.103515625e-05, ((0, 32),), jnp.float32),
        "trigram_first": centred(keys[18], (D, 3 * V), (0.011 * NPARAM ** -0.5), 6.103515625e-05, ((0, 32),), jnp.float32),
        "scales_first": centred(keys[19], (6, D), (0.044 * NPARAM ** -0.5), 0.00024414062, ((1, 32),), jnp.float32),
        "embedding_second": jnp.clip(jnp.exp(math.log(2.8777442234728667e-11) - 1.3862944 * jax.random.uniform(keys[20], (V, D), jnp.float32) ** block_levels(keys[20], (V, D), ((1, 32),), -0.2, 0.2)), 7.194360558682167e-12, 2.8777442234728667e-11),
        "attention_second": jnp.clip(jnp.exp(math.log(2.8777441540839277e-10) - 1.3862944 * jax.random.uniform(keys[21], (2, D, 3 * D), jnp.float32) ** block_levels(keys[21], (2, D, 3 * D), ((1, 32),), -0.2, 0.2)), 7.194360385209819e-11, 2.8777441540839277e-10),
        "projection_second": jnp.clip(jnp.exp(math.log(2.8777441540839277e-10) - 1.3862944 * jax.random.uniform(keys[22], (2, D, D), jnp.float32) ** block_levels(keys[22], (2, D, D), ((1, 32),), -0.2, 0.2)), 7.194360385209819e-11, 2.8777441540839277e-10),
        "expansion_second": jnp.clip(jnp.exp(math.log(2.8777441540839277e-10) - 1.3862944 * jax.random.uniform(keys[23], (2, D, FF), jnp.float32) ** block_levels(keys[23], (2, D, FF), ((1, 32),), -0.2, 0.2)), 7.194360385209819e-11, 2.8777441540839277e-10),
        "contraction_second": jnp.clip(jnp.exp(math.log(2.8777441540839277e-10) - 1.3862944 * jax.random.uniform(keys[24], (2, FF, D), jnp.float32) ** block_levels(keys[24], (2, FF, D), ((2, 32),), -0.2, 0.2)), 7.194360385209819e-11, 2.8777441540839277e-10),
        "readout_second": jnp.clip(jnp.exp(math.log(2.8777441540839277e-10) - 1.3862944 * jax.random.uniform(keys[25], (D, V), jnp.float32) ** block_levels(keys[25], (D, V), ((0, 32),), -0.2, 0.2)), 7.194360385209819e-11, 2.8777441540839277e-10),
        "trigram_second": jnp.clip(jnp.exp(math.log(2.8777441540839277e-10) - 1.3862944 * jax.random.uniform(keys[26], (D, 3 * V), jnp.float32) ** block_levels(keys[26], (D, 3 * V), ((0, 32),), -0.2, 0.2)), 7.194360385209819e-11, 2.8777441540839277e-10),
        "scales_second": jnp.clip(jnp.exp(math.log(4.604390646534284e-09) - 1.3862944 * jax.random.uniform(keys[27], (6, D), jnp.float32) ** block_levels(keys[27], (6, D), ((1, 32),), -0.2, 0.2)), 1.151097661633571e-09, 4.604390646534284e-09),
    }


@jax.custom_vjp
def low(v):
    return lax.optimization_barrier(v.astype(jnp.bfloat16)).astype(jnp.float32)

@jax.custom_vjp
def low_back(v):
    return v

def low_keep(v):
    return (low(v), None)

def low_pass(kept, grad):
    return (grad,)

def back_keep(v):
    return (v, None)

def back_low(kept, grad):
    return (low(grad),)
low.defvjp(low_keep, low_pass)
low_back.defvjp(back_keep, back_low)
norm_epsilon = 1e-06
trigram_share = 0.5
clip_limit = 0.1
beta_first = 0.9
beta_second = 0.95
adam_epsilon = 1e-08
learning_rates = (0.6, 0.05, 0.2, 0.05, 0.03, 0.05, 0.05, 0.6)
weight_decays = (0.0, 0.1, 0.1, 0.1, 0.1, 0.1, 0.1, 0.0)
highest = lax.Precision.HIGHEST

def norm_rows(stream, scaling):
    return stream * lax.rsqrt(lax.optimization_barrier(jnp.mean(stream * stream, axis=-1, keepdims=True)) + norm_epsilon) * scaling

def product(left, right):
    return jnp.dot(left, right, precision=highest)

def attend(qkv_rows, head_count):
    length = qkv_rows.shape[0]
    features = qkv_rows.shape[1] // 3
    queries = qkv_rows[:, :features].reshape(length, head_count, -1)
    key_heads = qkv_rows[:, features:2 * features].reshape(length, head_count, -1)
    value_heads = qkv_rows[:, 2 * features:].reshape(length, head_count, -1)
    scaled = queries.shape[-1] ** (-0.5)
    block_rows = length // 8
    key_place = jnp.arange(length, dtype=jnp.int32)

    def one_block(first_row):
        chosen = lax.dynamic_slice_in_dim(queries, first_row, block_rows, 0)
        scores = low_back(jnp.einsum('rhd,khd->rhk', chosen, key_heads, precision=highest) * scaled)
        query_place = first_row + jnp.arange(block_rows, dtype=jnp.int32)
        visible = key_place[None, None, :] <= query_place[:, None, None]
        probability = jax.nn.softmax(jnp.where(visible, scores, -1e+30), axis=-1)
        mixture = jnp.einsum('rhk,khd->rhd', low(probability), value_heads, precision=highest)
        return mixture.reshape(block_rows, -1)
    starts = jnp.arange(8, dtype=jnp.int32) * block_rows
    return lax.map(jax.checkpoint(one_block), starts).reshape(length, -1)

def layer(stream, qkv_weight, out_weight, in_weight, down_weight, scale_attend, scale_feed):
    qkv_rows = low_back(low(product(low(norm_rows(stream, scale_attend)), qkv_weight)))
    attended = low_back(low(attend(qkv_rows, HEADS)))
    hidden = stream + low_back(product(attended, out_weight))
    before = low_back(product(low(norm_rows(hidden, scale_feed)), in_weight))
    return hidden + low_back(product(low(jax.nn.gelu(before)), down_weight))

def head_loss(stream, scaling, matrix, targets, weights):
    logits = low_back(product(low(norm_rows(stream, scaling)), matrix))
    logits = logits.reshape(stream.shape[0], targets.shape[1], -1)
    log_total = jax.nn.logsumexp(logits, axis=-1)
    matches = targets[..., None] == jnp.arange(logits.shape[-1], dtype=jnp.int32)
    picked = lax.optimization_barrier(jnp.sum(jnp.where(matches, logits, 0.0), axis=-1))
    return jnp.sum(weights * (log_total - picked))

def sequence_loss(params, sequence):
    embedding, attention, projection, expansion, contraction, readout, trigram, scales = params
    token_row, next_row, triple_rows, mask_row = sequence
    embedded = embedding[token_row]
    first_stream = layer(embedded, attention[0], projection[0], expansion[0], contraction[0], scales[0], scales[1])
    features = first_stream.shape[1]
    shifted = jnp.concatenate([jnp.zeros((2, features), jnp.float32), first_stream[:-2]], axis=0)
    pooled = lax.optimization_barrier(jnp.mean(shifted.reshape(-1, 3, features), axis=1))
    short_stream = layer(pooled, attention[1], projection[1], expansion[1], contraction[1], scales[2], scales[3])
    merged = first_stream + jnp.repeat(short_stream, 3, axis=0)
    weights = mask_row.astype(jnp.float32)
    main_sum = head_loss(merged, scales[4], readout, next_row[:, None], weights[:, None])
    extra_sum = head_loss(short_stream, scales[5], trigram, triple_rows, weights.reshape(-1, 3))
    return main_sum + trigram_share * extra_sum

def adam_step(master, prior_first, prior_second, gradient, factor, rate, decay):
    clipped = gradient * factor
    moment = beta_first * prior_first + (1.0 - beta_first) * clipped
    variance = beta_second * prior_second + (1.0 - beta_second) * clipped * clipped
    ratio = moment / (1.0 - beta_first ** STEP) / (jnp.sqrt(variance / (1.0 - beta_second ** STEP)) + adam_epsilon)
    return (master - rate * (ratio + decay * master), moment, variance)

def reference(tokens, next_targets, triple_targets, loss_mask, embedding, attention, projection, expansion, contraction, readout, trigram, scales, embedding_first, attention_first, projection_first, expansion_first, contraction_first, readout_first, trigram_first, scales_first, embedding_second, attention_second, projection_second, expansion_second, contraction_second, readout_second, trigram_second, scales_second):
    masters = (embedding, attention, projection, expansion, contraction, readout, trigram, scales)
    firsts = (embedding_first, attention_first, projection_first, expansion_first, contraction_first, readout_first, trigram_first, scales_first)
    seconds = (embedding_second, attention_second, projection_second, expansion_second, contraction_second, readout_second, trigram_second, scales_second)
    raw_count = jnp.sum(loss_mask.astype(jnp.float32))
    divisor = jnp.maximum(raw_count, 1.0)

    def objective(params):
        rounded = tuple((low(weight) for weight in params))

        def visit(running, sequence):
            return (running + jax.checkpoint(sequence_loss)(rounded, sequence), None)
        summed, _ = lax.scan(visit, jnp.zeros((), jnp.float32), (tokens, next_targets, triple_targets, loss_mask))
        return (summed / divisor, summed)
    _, pullback, loss_total = jax.vjp(objective, masters, has_aux=True)
    grads = pullback(jnp.ones((), jnp.float32))[0]
    norm_value = jnp.sqrt(sum((jnp.sum(gradient * gradient) for gradient in grads)))
    factor = clip_limit / jnp.maximum(norm_value, clip_limit)
    results = [adam_step(masters[place], firsts[place], seconds[place], grads[place], factor, learning_rates[place], weight_decays[place]) for place in range(8)]
    return (loss_total, raw_count, norm_value, results[0][0], results[1][0], results[2][0], results[3][0], results[4][0], results[5][0], results[6][0], results[7][0], results[0][1], results[1][1], results[2][1], results[3][1], results[4][1], results[5][1], results[6][1], results[7][1], results[0][2], results[1][2], results[2][2], results[3][2], results[4][2], results[5][2], results[6][2], results[7][2])
```

```python
import jax
import jax.numpy as jnp
from jax import lax
from jax.sharding import PartitionSpec as P

HEADS = 8
STEP = 10


norm_epsilon = 1e-06
trigram_share = 0.5
clip_limit = 0.1
beta_first = 0.9
beta_second = 0.95
adam_epsilon = 1e-08
learning_rates = (0.6, 0.05, 0.2, 0.05, 0.03, 0.05, 0.05, 0.6)
weight_decays = (0.0, 0.1, 0.1, 0.1, 0.1, 0.1, 0.1, 0.0)
exact_precision = lax.Precision.HIGHEST


def lowered(array):
    return array.astype(jnp.bfloat16)


def contract(left, right, form):
    return jnp.einsum(form, left, right, preferred_element_type=jnp.float32)


def exactly(left, right, form):
    return jnp.einsum(
        form, left, right, preferred_element_type=jnp.float32, precision=exact_precision
    )


def bits_of(axis):
    return [1 << k for k in range((lax.axis_size(axis) - 1).bit_length())]


def index_bits():
    return [("seq", b) for b in reversed(bits_of("seq"))] + [
        ("dp", b) for b in reversed(bits_of("dp"))
    ]


def own_bit(step):
    axis, weight = step
    return (lax.axis_index(axis) // weight) % 2


def swapped(x, step):
    axis, weight = step
    return lax.ppermute(x, axis, [(i, i ^ weight) for i in range(lax.axis_size(axis))])


def gather_blocks(block, bits, order):
    x = block.reshape((1,) * len(bits) + block.shape)
    for step in order:
        k = bits.index(step)
        other = swapped(x, step)
        mine = lax.broadcasted_iota(jnp.int32, (1,) * k + (2,) + (1,) * (x.ndim - k - 1), k)
        x = jnp.where(mine == own_bit(step), x, other)
    return x.reshape((-1,) + block.shape[1:])


def scatter_sums(terms, bits, order):
    count = 1 << len(bits)
    x = terms.reshape((2,) * len(bits) + (terms.shape[0] // count,) + terms.shape[1:])
    for place, step in enumerate(order):
        k = bits.index(step)
        bit = own_bit(step)
        kept = lax.dynamic_slice_in_dim(x, bit, 1, k)
        sent = lax.dynamic_slice_in_dim(x, 1 - bit, 1, k)
        x = kept.astype(jnp.float32) + swapped(sent, step).astype(jnp.float32)
        if place + 1 < len(order):
            x = lowered(x)
    return x.reshape(x.shape[len(bits):])


def rotated(bits, turn):
    rest = bits[1:-1]
    turn = turn % max(len(rest), 1)
    return [bits[0]] + rest[turn:] + rest[:turn] + [bits[-1]]


def norm_scale(stream):
    return lax.rsqrt(jnp.mean(stream * stream, axis=-1, keepdims=True) + norm_epsilon)


def norm_back(stream, inverse, scaling, gradient):
    unit = stream * inverse
    scaled = gradient * scaling
    scaling_grad = jnp.sum(gradient * unit, axis=0)
    stream_grad = inverse * (scaled - unit * jnp.mean(scaled * unit, axis=-1, keepdims=True))
    return stream_grad, scaling_grad


def heads_of(rows):
    return rows.reshape(rows.shape[0], HEADS, -1)


def weighted_attention(queries, keys, values, counts):
    scores = contract(queries, keys, "rhd,khd->hrk") * queries.shape[-1] ** (-0.5)
    seen = (counts > 0.0)[None]
    highest = jnp.max(jnp.where(seen, scores, -1e30), axis=-1, keepdims=True)
    exponent = jnp.where(seen, jnp.exp(jnp.where(seen, scores, -1e30) - highest), 0.0) * counts[None]
    shares = exponent / jnp.sum(exponent, axis=-1, keepdims=True)
    shares_low = lowered(shares)
    mixed = contract(shares_low, values, "hrk,khd->rhd")
    return mixed, shares


def weighted_attention_back(queries, keys, values, shares, mixed, mixed_grad):
    scaled = queries.shape[-1] ** (-0.5)
    row_dots = jnp.sum(mixed_grad.astype(jnp.float32) * mixed, axis=-1).T[..., None]
    share_grad = contract(mixed_grad, values, "rhd,khd->hrk")
    score_grad = lowered(shares * (share_grad - row_dots))
    query_grad = contract(score_grad, keys, "hrk,khd->rhd") * scaled
    key_grad = contract(score_grad, queries, "hrk,rhd->khd") * scaled
    value_grad = contract(lowered(shares), mixed_grad, "hrk,rhd->khd")
    return query_grad, key_grad, value_grad


def feed_forward(hidden, in_weight, down_weight, scaling):
    inverse = norm_scale(hidden)
    normed = lowered(hidden * inverse * scaling)
    before = contract(normed, in_weight, "rd,df->rf")
    activated = lowered(jax.nn.gelu(before))
    return hidden + contract(activated, down_weight, "rf,df->rd"), (inverse, normed, before, activated)


def feed_back(hidden, kept, gradient, in_weight, down_weight, scaling):
    inverse, normed, before, activated = kept
    grad_low = lowered(gradient)
    down_grad = contract(grad_low, activated, "rd,rf->df")
    act_grad = contract(grad_low, down_weight, "rd,df->rf")
    before_grad = lowered(jax.vjp(jax.nn.gelu, before)[1](act_grad)[0])
    in_grad = contract(normed, before_grad, "rd,rf->df")
    normed_grad = contract(before_grad, in_weight, "rf,df->rd")
    hidden_grad, scaling_grad = norm_back(hidden, inverse, scaling, normed_grad)
    return hidden_grad + gradient, lowered(in_grad), lowered(down_grad), scaling_grad


def head_back(stream, scaling, matrix, targets, weights, factor):
    inverse = norm_scale(stream)
    normed_low = lowered(stream * inverse * scaling)
    logits = contract(normed_low, matrix, "rd,dc->rc").reshape(
        stream.shape[0], targets.shape[1], -1
    )
    log_total = jax.nn.logsumexp(logits, axis=-1)
    matches = targets[..., None] == jnp.arange(logits.shape[-1], dtype=jnp.int32)
    picked = jnp.sum(jnp.where(matches, logits, 0.0), axis=-1)
    logit_grad = (
        jnp.exp(logits - log_total[..., None]) - matches.astype(jnp.float32)
    ) * (weights * factor)[..., None]
    logit_low = lowered(logit_grad.reshape(stream.shape[0], -1))
    matrix_grad = lowered(contract(normed_low, logit_low, "rd,rc->dc"))
    normed_grad = contract(logit_low, matrix, "rc,dc->rd")
    stream_grad, scaling_grad = norm_back(stream, inverse, scaling, normed_grad)
    return (jnp.sum(weights * (log_total - picked)), stream_grad, scaling_grad, matrix_grad)


def adam_step(master, prior_first, prior_second, gradient, factor, rate, decay):
    clipped = gradient * factor
    moment = beta_first * prior_first + (1.0 - beta_first) * clipped
    variance = beta_second * prior_second + (1.0 - beta_second) * clipped * clipped
    ratio = (
        moment
        / (1.0 - beta_first**STEP)
        / (jnp.sqrt(variance / (1.0 - beta_second**STEP)) + adam_epsilon)
    )
    return (master - rate * (ratio + decay * master), moment, variance)


def pad_columns(array, width):
    return jnp.pad(array, ((0, 0), (0, width - array.shape[1])))


def local(
    tokens,
    next_targets,
    triple_targets,
    loss_mask,
    embedding,
    attention,
    projection,
    expansion,
    contraction,
    readout,
    trigram,
    scales,
    *moments,
):
    masters = (embedding, attention, projection, expansion, contraction, readout, trigram, scales)
    firsts = moments[:8]
    seconds = moments[8:]
    bits = index_bits()
    seq_size, dp_size = lax.axis_size("seq"), lax.axis_size("dp")
    devices = seq_size * dp_size
    held, piece = tokens.shape
    length = piece * seq_size
    sequences = held * dp_size
    members = devices // sequences
    vocabulary, share = embedding.shape
    features = share * devices
    hidden_size = expansion.shape[2]
    rows = length // members
    shorts = rows // 3
    member_bits = [("dp", b) for b in reversed(bits_of("dp")) if b < members]
    member = lax.axis_index("dp") % members
    group = (lax.axis_index("seq") * dp_size + lax.axis_index("dp")) // members

    integers = jnp.stack(
        [tokens, next_targets, triple_targets.reshape(held, piece), loss_mask]
    ).astype(jnp.bfloat16)
    integers = integers.reshape(share, -1)
    integer_width = integers.shape[1]
    integer_room = -(-integer_width // 128) * 128
    down_low = jnp.swapaxes(lowered(contraction), 1, 2)
    attention_low, projection_low, expansion_low = map(lowered, (attention, projection, expansion))
    parcels = (
        [
            pad_columns(integers, integer_room),
            pad_columns(lowered(scales).T, 128),
            lowered(embedding).T,
            attention_low[0],
        ],
        [projection_low[0], expansion_low[0], down_low[0]],
        [attention_low[1], projection_low[1], expansion_low[1]],
        [down_low[1], lowered(readout), lowered(trigram)],
    )
    spread = []
    for turn, parcel in enumerate(parcels):
        whole = gather_blocks(jnp.concatenate(parcel, axis=1), bits, rotated(bits, turn))
        start = 0
        for part in parcel:
            spread.append(whole[:, start : start + part.shape[1]])
            start += part.shape[1]
    (
        all_integers,
        scale_columns,
        embed_columns,
        attend_zero,
        project_zero,
        expand_zero,
        down_zero,
        attend_one,
        project_one,
        expand_one,
        down_one,
        readout_rows,
        trigram_rows,
    ) = spread
    scale_rows = scale_columns[:, :6].astype(jnp.float32).T
    all_integers = all_integers[:, :integer_width].reshape(
        seq_size, dp_size, 4, held, piece
    )
    mask_total = jnp.sum(all_integers[:, :, 3].astype(jnp.float32))
    inverse_total = 1.0 / jnp.maximum(mask_total, 1.0)
    sequence = lax.dynamic_slice(
        all_integers,
        (0, group // held, 0, group % held, 0),
        (seq_size, 1, 4, 1, piece),
    )
    sequence = jnp.swapaxes(sequence.reshape(seq_size, 4, piece), 0, 1).reshape(4, length)
    own = lax.dynamic_slice_in_dim(sequence, member * rows, rows, 1).astype(jnp.int32)
    sequence_tokens = sequence[0].astype(jnp.int32)
    own_tokens, own_next, own_triple, own_mask = own
    weights = own_mask.astype(jnp.float32)

    letters = jnp.arange(vocabulary, dtype=jnp.int32)
    is_token = (own_tokens[:, None] == letters).astype(jnp.bfloat16)
    place = member * rows + jnp.arange(rows, dtype=jnp.int32)
    earlier = (jnp.arange(length, dtype=jnp.int32)[None, :] <= place[:, None]).astype(jnp.bfloat16)
    counts = contract(
        earlier, (sequence_tokens[:, None] == letters).astype(jnp.bfloat16), "rt,tv->rv"
    )
    table = embed_columns.astype(jnp.float32).T
    table_inverse = norm_scale(table)
    table_normed = lowered(table * table_inverse * scale_rows[0])
    table_qkv = lowered(contract(table_normed, attend_zero, "vd,dc->vc"))
    embedded = contract(is_token, embed_columns, "rv,dv->rd")
    queries = heads_of(
        lowered(contract(is_token, table_qkv[:, :features], "rv,vc->rc"))
    )
    keys = heads_of(table_qkv[:, features : 2 * features])
    values = heads_of(table_qkv[:, 2 * features :])
    mixed, shares = weighted_attention(queries, keys, values, counts)
    mixed_low = lowered(mixed.reshape(rows, features))
    hidden = embedded + contract(mixed_low, project_zero, "rd,de->re")
    first_stream, fed_zero = feed_forward(hidden, expand_zero, down_zero, scale_rows[1])

    along = [(i, i + 1) for i in range(dp_size - 1) if (i + 1) % members]
    back = [(i + 1, i) for i, _ in along]
    previous = lax.ppermute(first_stream[-2:], "dp", along)
    pooled = jnp.mean(
        jnp.concatenate([previous, first_stream[:-2]], axis=0).reshape(-1, 3, features), axis=1
    )

    pooled_inverse = norm_scale(pooled)
    pooled_normed = lowered(pooled * pooled_inverse * scale_rows[2])
    short_qkv = lowered(contract(pooled_normed, attend_one, "rd,dc->rc"))
    pairs = gather_blocks(short_qkv[:, features:], member_bits, member_bits)
    short_queries = heads_of(short_qkv[:, :features])
    short_keys = heads_of(pairs[:, :features])
    short_values = heads_of(pairs[:, features:])
    short_place = member * shorts + jnp.arange(shorts, dtype=jnp.int32)
    visible = (
        jnp.arange(shorts * members, dtype=jnp.int32)[None, :] <= short_place[:, None]
    ).astype(jnp.float32)
    short_mixed, short_shares = weighted_attention(
        short_queries, short_keys, short_values, visible
    )
    short_mixed_low = lowered(short_mixed.reshape(shorts, features))
    short_hidden = pooled + contract(short_mixed_low, project_one, "rd,de->re")
    short_stream, fed_one = feed_forward(short_hidden, expand_one, down_one, scale_rows[3])
    merged = first_stream + jnp.repeat(short_stream, 3, axis=0)

    main_sum, merged_grad, main_scale, readout_grad = head_back(
        merged, scale_rows[4], readout_rows, own_next[:, None], weights[:, None], inverse_total
    )
    extra_sum, short_grad, extra_scale, trigram_grad = head_back(
        short_stream,
        scale_rows[5],
        trigram_rows,
        own_triple.reshape(shorts, 3),
        weights.reshape(shorts, 3),
        trigram_share * inverse_total,
    )
    loss_local = main_sum + trigram_share * extra_sum

    short_grad = short_grad + jnp.sum(merged_grad.reshape(-1, 3, features), axis=1)
    short_hidden_grad, expand_one_grad, down_one_grad, feed_one_scale = feed_back(
        short_hidden, fed_one, short_grad, expand_one, down_one, scale_rows[3]
    )
    short_hidden_low = lowered(short_hidden_grad)
    project_one_grad = lowered(contract(short_mixed_low, short_hidden_low, "rd,re->de"))
    short_mixed_grad = heads_of(lowered(contract(short_hidden_low, project_one, "re,de->rd")))
    query_grad, key_grad, value_grad = weighted_attention_back(
        short_queries, short_keys, short_values, short_shares, short_mixed, short_mixed_grad
    )
    pair_terms = jnp.concatenate(
        [key_grad.reshape(-1, features), value_grad.reshape(-1, features)], axis=1
    )
    pair_grad = scatter_sums(lowered(pair_terms), member_bits, member_bits)
    short_qkv_grad = lowered(
        jnp.concatenate([query_grad.reshape(shorts, features), pair_grad], axis=1)
    )
    attend_one_grad = lowered(contract(pooled_normed, short_qkv_grad, "rd,rc->dc"))
    pooled_grad, attend_one_scale = norm_back(
        pooled,
        pooled_inverse,
        scale_rows[2],
        contract(short_qkv_grad, attend_one, "rc,dc->rd"),
    )
    pooled_grad = pooled_grad + short_hidden_grad

    shifted_grad = jnp.repeat(pooled_grad / 3.0, 3, axis=0)
    returned = lax.ppermute(shifted_grad[:2], "dp", back)
    first_grad = merged_grad + jnp.concatenate([shifted_grad[2:], returned], axis=0)
    hidden_grad, expand_zero_grad, down_zero_grad, feed_zero_scale = feed_back(
        hidden, fed_zero, first_grad, expand_zero, down_zero, scale_rows[1]
    )
    hidden_low = lowered(hidden_grad)
    project_zero_grad = lowered(contract(mixed_low, hidden_low, "rd,re->de"))
    mixed_grad = heads_of(lowered(contract(hidden_low, project_zero, "re,de->rd")))
    query_grad, key_grad, value_grad = weighted_attention_back(
        queries, keys, values, shares, mixed, mixed_grad
    )
    table_query_grad = contract(
        is_token, lowered(query_grad.reshape(rows, features)), "rv,rc->vc"
    )
    table_qkv_grad = lowered(
        jnp.concatenate(
            [
                table_query_grad,
                key_grad.reshape(vocabulary, features),
                value_grad.reshape(vocabulary, features),
            ],
            axis=1,
        )
    )
    attend_zero_grad = lowered(contract(table_normed, table_qkv_grad, "vd,vc->dc"))
    table_grad, attend_zero_scale = norm_back(
        table,
        table_inverse,
        scale_rows[0],
        contract(table_qkv_grad, attend_zero, "vc,dc->vd"),
    )
    table_grad = table_grad + contract(is_token, hidden_low, "rv,rd->vd")
    scale_grads = jnp.stack(
        [
            attend_zero_scale,
            feed_zero_scale,
            attend_one_scale,
            feed_one_scale,
            main_scale,
            extra_scale,
        ],
        axis=1,
    )

    returns = (
        [readout_grad, trigram_grad, down_one_grad, expand_one_grad],
        [project_one_grad, attend_one_grad],
        [down_zero_grad, expand_zero_grad],
        [
            project_zero_grad,
            attend_zero_grad,
            lowered(table_grad.T),
            lowered(pad_columns(scale_grads, 128)),
        ],
    )
    sums = []
    for turn, parcel in enumerate(returns):
        total = scatter_sums(
            jnp.concatenate(parcel, axis=1), bits, list(reversed(rotated(bits, turn)))
        )
        start = 0
        for part in parcel:
            sums.append(total[:, start : start + part.shape[1]])
            start += part.shape[1]
    (
        readout_sum,
        trigram_sum,
        down_one_sum,
        expand_one_sum,
        project_one_sum,
        attend_one_sum,
        down_zero_sum,
        expand_zero_sum,
        project_zero_sum,
        attend_zero_sum,
        embed_sum,
        scale_sum,
    ) = sums
    reduced = (
        embed_sum.T,
        jnp.stack([attend_zero_sum, attend_one_sum]),
        jnp.stack([project_zero_sum, project_one_sum]),
        jnp.stack([expand_zero_sum, expand_one_sum]),
        jnp.stack([down_zero_sum.T, down_one_sum.T]),
        readout_sum,
        trigram_sum,
        scale_sum[:, :6].T,
    )
    squares = sum((jnp.sum(part * part) for part in sums))
    totals = jnp.broadcast_to(jnp.stack([squares, loss_local])[:, None], (2, 128))
    for step in reversed(bits):
        totals = totals + swapped(totals, step)
    square_total, loss_total = totals[0, 0], totals[1, 0]
    norm_value = jnp.sqrt(square_total)
    factor = clip_limit / jnp.maximum(norm_value, clip_limit)
    results = [
        adam_step(
            masters[at],
            firsts[at],
            seconds[at],
            reduced[at],
            factor,
            learning_rates[at],
            weight_decays[at],
        )
        for at in range(8)
    ]
    return (
        loss_total,
        mask_total,
        norm_value,
        *(result[0] for result in results),
        *(result[1] for result in results),
        *(result[2] for result in results),
    )


def solution(mesh):
    weight_specs = (
        P(None, ("seq", "dp")),
        P(None, ("seq", "dp"), None),
        P(None, ("seq", "dp"), None),
        P(None, ("seq", "dp"), None),
        P(None, None, ("seq", "dp")),
        P(("seq", "dp"), None),
        P(("seq", "dp"), None),
        P(None, ("seq", "dp")),
    )
    in_specs = (
        P("dp", "seq"),
        P("dp", "seq"),
        P("dp", "seq", None),
        P("dp", "seq"),
    ) + weight_specs * 3
    out_specs = (P(), P(), P()) + weight_specs * 3
    return jax.shard_map(local, mesh=mesh, in_specs=in_specs, out_specs=out_specs, check_vma=False)
```

```python
import functools

import jax
import jax.numpy as jnp
from jax import lax
from jax.experimental import pallas as pl
from jax.experimental.pallas import tpu as pltpu
from jax.sharding import PartitionSpec as P

HEADS = 8
STEP = 10


norm_epsilon = 1e-06
trigram_share = 0.5
clip_limit = 0.1
beta_first = 0.9
beta_second = 0.95
adam_epsilon = 1e-08
learning_rates = (0.6, 0.05, 0.2, 0.05, 0.03, 0.05, 0.05, 0.6)
weight_decays = (0.0, 0.1, 0.1, 0.1, 0.1, 0.1, 0.1, 0.0)
exact_precision = lax.Precision.HIGHEST
vmem_bytes = 48 * 1024 * 1024
lanes = 128


def lowered(array):
    return array.astype(jnp.bfloat16)


def contract(left, right, form):
    return jnp.einsum(form, left, right, preferred_element_type=jnp.float32)


def exactly(left, right, form):
    return jnp.einsum(
        form, left, right, preferred_element_type=jnp.float32, precision=exact_precision
    )


def bits_of(axis):
    return [1 << k for k in range((lax.axis_size(axis) - 1).bit_length())]


def index_bits():
    return [("seq", b) for b in reversed(bits_of("seq"))] + [
        ("dp", b) for b in reversed(bits_of("dp"))
    ]


def own_bit(step):
    axis, weight = step
    return (lax.axis_index(axis) // weight) % 2


def swapped(x, step):
    axis, weight = step
    return lax.ppermute(x, axis, [(i, i ^ weight) for i in range(lax.axis_size(axis))])


def gather_blocks(block, bits, order):
    x = block.reshape((1,) * len(bits) + block.shape)
    for step in order:
        k = bits.index(step)
        other = swapped(x, step)
        mine = lax.broadcasted_iota(jnp.int32, (1,) * k + (2,) + (1,) * (x.ndim - k - 1), k)
        x = jnp.where(mine == own_bit(step), x, other)
    return x.reshape((-1,) + block.shape[1:])


def scatter_sums(terms, bits, order):
    count = 1 << len(bits)
    x = terms.reshape((2,) * len(bits) + (terms.shape[0] // count,) + terms.shape[1:])
    for place, step in enumerate(order):
        k = bits.index(step)
        bit = own_bit(step)
        kept = lax.dynamic_slice_in_dim(x, bit, 1, k)
        sent = lax.dynamic_slice_in_dim(x, 1 - bit, 1, k)
        x = kept.astype(jnp.float32) + swapped(sent, step).astype(jnp.float32)
        if place + 1 < len(order):
            x = lowered(x)
    return x.reshape(x.shape[len(bits):])


def whole_in_vmem(count):
    return [pl.BlockSpec(memory_space=pltpu.VMEM)] * count


def cost(flops, moved, exponentials=0):
    return pl.CostEstimate(
        flops=int(flops), bytes_accessed=int(moved), transcendentals=int(exponentials)
    )


def split_parts_kernel(bit_ref, *refs):
    *part_refs, sent_ref, kept_ref = refs
    bit = bit_ref[0]
    start = 0
    for part_ref in part_refs:
        width = part_ref.shape[-1]
        sent_ref[:, :, start : start + width] = part_ref[:, pl.ds(1 - bit, 1)][:, 0]
        kept_ref[:, :, start : start + width] = part_ref[:, pl.ds(bit, 1)][:, 0]
        start += width


def split_parts(parts, bit, share):
    chips = parts[0].shape[0] // (2 * share)
    step = min(chips, 4)
    width = sum(part.shape[1] for part in parts)
    shaped = [part.reshape(chips, 2, share, part.shape[1]) for part in parts]
    half = jax.ShapeDtypeStruct((chips, share, width), jnp.bfloat16)
    return pl.pallas_call(
        split_parts_kernel,
        grid_spec=pltpu.PrefetchScalarGridSpec(
            num_scalar_prefetch=1,
            grid=(chips // step,),
            in_specs=[
                pl.BlockSpec((step, 2, share, part.shape[-1]), lambda i, bit: (i, 0, 0, 0))
                for part in shaped
            ],
            out_specs=[pl.BlockSpec((step, share, width), lambda i, bit: (i, 0, 0))] * 2,
        ),
        out_shape=[half, half],
        compiler_params=pltpu.CompilerParams(vmem_limit_bytes=vmem_bytes),
        cost_estimate=cost(0, 8 * chips * share * width),
    )(bit.reshape(1), *shaped)


def add_and_split_kernel(bit_ref, kept_ref, came_ref, sent_out, kept_out):
    bit = bit_ref[0]

    def total(at):
        return lowered(
            kept_ref[:, pl.ds(at, 1)].astype(jnp.float32)
            + came_ref[:, pl.ds(at, 1)].astype(jnp.float32)
        )[:, 0]

    sent_out[...] = total(1 - bit)
    kept_out[...] = total(bit)


def add_and_split(kept, came, bit, before, after):
    share, width = kept.shape[-2:]
    shape = (before, 2, after, share, width)
    half = jax.ShapeDtypeStruct((before, after, share, width), jnp.bfloat16)
    sent, kept = pl.pallas_call(
        add_and_split_kernel,
        grid_spec=pltpu.PrefetchScalarGridSpec(
            num_scalar_prefetch=1,
            grid=(before, after),
            in_specs=[
                pl.BlockSpec((1, 2, 1, share, width), lambda i, j, bit: (i, 0, j, 0, 0))
            ]
            * 2,
            out_specs=[
                pl.BlockSpec((1, 1, share, width), lambda i, j, bit: (i, j, 0, 0))
            ]
            * 2,
        ),
        out_shape=[half, half],
        compiler_params=pltpu.CompilerParams(vmem_limit_bytes=vmem_bytes),
        cost_estimate=cost(before * after * share * width, 12 * before * after * share * width),
    )(bit.reshape(1), kept.reshape(shape), came.reshape(shape))
    flat = (before * after, share, width)
    return sent.reshape(flat), kept.reshape(flat)


def add_and_square_kernel(kept_ref, came_ref, total_ref, square_ref):
    total = kept_ref[...].astype(jnp.float32) + came_ref[...].astype(jnp.float32)
    total_ref[...] = total
    squares = jnp.zeros(square_ref.shape, jnp.float32)
    for start in range(0, total.shape[1], lanes):
        piece = total[:, start : start + lanes]
        squares = squares + piece * piece
    square_ref[...] = squares


def add_and_square(kept, came):
    share, width = kept.shape[-2:]
    return pl.pallas_call(
        add_and_square_kernel,
        in_specs=whole_in_vmem(2),
        out_specs=whole_in_vmem(2),
        out_shape=[
            jax.ShapeDtypeStruct((share, width), jnp.float32),
            jax.ShapeDtypeStruct((share, lanes), jnp.float32),
        ],
        cost_estimate=cost(3 * share * width, 8 * share * width),
    )(kept.reshape(share, width), came.reshape(share, width))


def reduce_parts(parts, bits, order, share):
    sent, kept = split_parts(parts, own_bit(order[0]), share)
    left = list(bits[:-1])
    for now, following in zip(order[:-1], order[1:]):
        at = left.index(following)
        came = swapped(sent, now)
        sent, kept = add_and_split(
            kept, came, own_bit(following), 1 << at, 1 << (len(left) - at - 1)
        )
        left.remove(following)
    return add_and_square(kept, swapped(sent, order[-1]))


def rotated(bits, turn):
    rest = bits[1:-1]
    turn = turn % max(len(rest), 1)
    return [bits[0]] + rest[turn:] + rest[:turn] + [bits[-1]]


def norm_scale(stream):
    return lax.rsqrt(jnp.mean(stream * stream, axis=-1, keepdims=True) + norm_epsilon)


def norm_back(stream, inverse, scaling, gradient):
    unit = stream * inverse
    scaled = gradient * scaling
    scaling_grad = jnp.sum(gradient * unit, axis=0)
    stream_grad = inverse * (scaled - unit * jnp.mean(scaled * unit, axis=-1, keepdims=True))
    return stream_grad, scaling_grad


def times(left, right, left_side=1, right_side=0):
    return lax.dot_general(
        left, right, (((left_side,), (right_side,)), ((), ())), preferred_element_type=jnp.float32
    )


def exact_times(left, right, left_side=1, right_side=0):
    return lax.dot_general(
        left,
        right,
        (((left_side,), (right_side,)), ((), ())),
        preferred_element_type=jnp.float32,
        precision=exact_precision,
    )


def head_groups(features):
    depth = features // HEADS
    together = max(1, lanes // depth)
    return depth, [
        (first * depth, together * depth, range(first, first + together))
        for first in range(0, HEADS, together)
    ]


def own_lanes(width, depth, at):
    lane = lax.broadcasted_iota(jnp.int32, (1, width), 1)
    return (lane >= at * depth) & (lane < (at + 1) * depth)


def attend_kernel(query_ref, key_ref, value_ref, count_ref, mixed_ref, share_ref):
    counts = count_ref[...]
    depth, groups = head_groups(query_ref.shape[1])
    for start, width, places in groups:
        span = slice(start, start + width)
        queries = query_ref[:, span] * jnp.asarray(depth ** (-0.5), query_ref.dtype)
        keys, values = key_ref[:, span], value_ref[:, span]
        mixed = None
        for at, place in enumerate(places):
            own = own_lanes(width, depth, at)
            scores = times(queries, jnp.where(own, keys, jnp.zeros_like(keys)), 1, 1)
            scores = jnp.where(counts > 0.0, scores, -1e30)
            exponent = counts * jnp.exp(scores - jnp.max(scores, axis=-1, keepdims=True))
            shares = exponent * (1.0 / jnp.sum(exponent, axis=-1, keepdims=True))
            share_ref[place] = shares
            product = times(lowered(shares), values)
            mixed = product if mixed is None else jnp.where(own, product, mixed)
        mixed_ref[:, span] = lowered(mixed)


def block_of_rows(rows):
    return rows // 3 if rows > 256 and rows % 48 == 0 else rows


def weighted_attention(queries, keys, values, counts):
    rows, features = queries.shape
    entries = keys.shape[0]
    block = block_of_rows(rows)
    return pl.pallas_call(
        attend_kernel,
        grid=(rows // block,),
        in_specs=[
            pl.BlockSpec((block, features), lambda i: (i, 0)),
            pl.BlockSpec((entries, features), lambda i: (0, 0)),
            pl.BlockSpec((entries, features), lambda i: (0, 0)),
            pl.BlockSpec((block, entries), lambda i: (i, 0)),
        ],
        out_specs=[
            pl.BlockSpec((block, features), lambda i: (i, 0)),
            pl.BlockSpec((HEADS, block, entries), lambda i: (0, i, 0)),
        ],
        out_shape=[
            jax.ShapeDtypeStruct((rows, features), jnp.bfloat16),
            jax.ShapeDtypeStruct((HEADS, rows, entries), jnp.float32),
        ],
        compiler_params=pltpu.CompilerParams(vmem_limit_bytes=vmem_bytes),
        cost_estimate=cost(
            4 * rows * entries * features,
            4 * rows * features + 4 * entries * features + 4 * (HEADS + 1) * rows * entries,
            HEADS * rows * entries,
        ),
    )(queries, keys, values, counts)


def attend_back_kernel(
    query_ref, key_ref, value_ref, share_ref, grad_ref, query_out, key_out, value_out
):
    @pl.when(pl.program_id(0) == 0)
    def _():
        key_out[...] = jnp.zeros_like(key_out)
        value_out[...] = jnp.zeros_like(value_out)

    depth, groups = head_groups(query_ref.shape[1])
    scaled = depth ** (-0.5)
    for start, width, places in groups:
        span = slice(start, start + width)
        queries, keys, values = query_ref[:, span], key_ref[:, span], value_ref[:, span]
        gradient = grad_ref[:, span]
        query_sum = key_sum = value_sum = None
        for at, place in enumerate(places):
            own = own_lanes(width, depth, at)
            shares = share_ref[place]
            share_grad = times(gradient, jnp.where(own, values, jnp.zeros_like(values)), 1, 1)
            dots = jnp.sum(shares * share_grad, axis=-1, keepdims=True)
            score_grad = lowered(shares * (share_grad - dots))
            query_part = times(score_grad, keys)
            key_part = times(score_grad, queries, 0, 0)
            value_part = times(lowered(shares), gradient, 0, 0)
            if query_sum is None:
                query_sum, key_sum, value_sum = query_part, key_part, value_part
            else:
                query_sum = jnp.where(own, query_part, query_sum)
                key_sum = jnp.where(own, key_part, key_sum)
                value_sum = jnp.where(own, value_part, value_sum)
        query_out[:, span] = lowered(query_sum * scaled)
        key_out[:, span] += key_sum * scaled
        value_out[:, span] += value_sum


def weighted_attention_back(queries, keys, values, shares, mixed_grad):
    rows, features = queries.shape
    entries = keys.shape[0]
    block = block_of_rows(rows)
    by_rows = pl.BlockSpec((block, features), lambda i: (i, 0))
    by_entries = pl.BlockSpec((entries, features), lambda i: (0, 0))
    return pl.pallas_call(
        attend_back_kernel,
        grid=(rows // block,),
        in_specs=[
            by_rows,
            by_entries,
            by_entries,
            pl.BlockSpec((HEADS, block, entries), lambda i: (0, i, 0)),
            by_rows,
        ],
        out_specs=[by_rows, by_entries, by_entries],
        out_shape=[
            jax.ShapeDtypeStruct((rows, features), jnp.bfloat16),
            jax.ShapeDtypeStruct((entries, features), jnp.float32),
            jax.ShapeDtypeStruct((entries, features), jnp.float32),
        ],
        compiler_params=pltpu.CompilerParams(vmem_limit_bytes=vmem_bytes),
        cost_estimate=cost(
            8 * rows * entries * features,
            6 * rows * features + 12 * entries * features + 4 * HEADS * rows * entries,
        ),
    )(queries, keys, values, shares, mixed_grad)


def feed_forward(hidden, in_weight, down_weight, scaling):
    inverse = norm_scale(hidden)
    normed = lowered(hidden * inverse * scaling)
    before = contract(normed, in_weight, "rd,df->rf")
    activated = lowered(jax.nn.gelu(before))
    return hidden + contract(activated, down_weight, "rf,df->rd"), (inverse, normed, before, activated)


def feed_back(hidden, kept, gradient, in_weight, down_weight, scaling):
    inverse, normed, before, activated = kept
    grad_low = lowered(gradient)
    down_grad = contract(grad_low, activated, "rd,rf->df")
    act_grad = contract(grad_low, down_weight, "rd,df->rf")
    before_grad = lowered(jax.vjp(jax.nn.gelu, before)[1](act_grad)[0])
    in_grad = contract(normed, before_grad, "rd,rf->df")
    normed_grad = contract(before_grad, in_weight, "rf,df->rd")
    hidden_grad, scaling_grad = norm_back(hidden, inverse, scaling, normed_grad)
    return hidden_grad + gradient, lowered(in_grad), lowered(down_grad), scaling_grad


def head_terms(stream, scaling, matrix, targets, weights, factor):
    inverse = norm_scale(stream)
    normed_low = lowered(stream * inverse * scaling)
    logits = times(normed_low, matrix)
    vocabulary = logits.shape[1] // targets.shape[1]
    letters = lax.broadcasted_iota(jnp.int32, (stream.shape[0], vocabulary), 1)
    gradients = []
    loss = None
    for place in range(targets.shape[1]):
        some = logits[:, place * vocabulary : (place + 1) * vocabulary]
        highest = jnp.max(some, axis=-1, keepdims=True)
        exponent = jnp.exp(some - highest)
        denominator = jnp.sum(exponent, axis=-1, keepdims=True)
        matches = letters == targets[:, place : place + 1]
        picked = jnp.sum(jnp.where(matches, some, 0.0), axis=-1, keepdims=True)
        weight = weights[:, place : place + 1]
        term = weight * (highest + jnp.log(denominator) - picked)
        loss = term if loss is None else loss + term
        chance = exponent * (1.0 / denominator)
        gradients.append(lowered((chance - jnp.where(matches, 1.0, 0.0)) * (weight * factor)))
    logit_low = gradients[0] if len(gradients) == 1 else jnp.concatenate(gradients, axis=1)
    matrix_grad = times(normed_low, logit_low, 0, 0)
    stream_grad, scaling_grad = norm_back(
        stream, inverse, scaling, times(logit_low, matrix, 1, 1)
    )
    return jnp.sum(loss, axis=0, keepdims=True), stream_grad, scaling_grad, lowered(matrix_grad)


def heads_kernel(
    total_ref,
    first_ref,
    short_ref,
    scale_ref,
    readout_ref,
    trigram_ref,
    next_ref,
    weight_ref,
    triple_ref,
    triple_weight_ref,
    loss_ref,
    first_out,
    short_out,
    readout_out,
    trigram_out,
    scale_out,
):
    inverse_total = 1.0 / jnp.maximum(total_ref[0, 0], 1.0)
    short = short_ref[...]
    rows, shorts = first_ref.shape[0], short.shape[0]
    gap = lax.broadcasted_iota(jnp.int32, (rows, shorts), 0) - 3 * lax.broadcasted_iota(
        jnp.int32, (rows, shorts), 1
    )
    thrice = jnp.where((gap >= 0) & (gap < 3), 1.0, 0.0)
    merged = first_ref[...] + exact_times(thrice, short)
    main_loss, merged_grad, main_scale, readout_grad = head_terms(
        merged, scale_ref[0:1], readout_ref[...], next_ref[...], weight_ref[...], inverse_total
    )
    first_out[...] = merged_grad
    readout_out[...] = readout_grad
    scale_out[0:1] = main_scale[None]
    extra_loss, short_grad, extra_scale, trigram_grad = head_terms(
        short,
        scale_ref[1:2],
        trigram_ref[...],
        triple_ref[...],
        triple_weight_ref[...],
        trigram_share * inverse_total,
    )
    short_out[...] = short_grad + exact_times(thrice, merged_grad, 0, 0)
    trigram_out[...] = trigram_grad
    scale_out[1:2] = extra_scale[None]
    loss_ref[...] = main_loss + trigram_share * extra_loss


def both_heads(
    mask_total, first, short, scaling, readout, trigram, next_targets, weights, triples, triple_weights
):
    rows, features = first.shape
    shorts = short.shape[0]
    vocabulary = readout.shape[1]
    return pl.pallas_call(
        heads_kernel,
        in_specs=[pl.BlockSpec(memory_space=pltpu.SMEM)] + whole_in_vmem(9),
        out_specs=whole_in_vmem(6),
        out_shape=[
            jax.ShapeDtypeStruct((1, 1), jnp.float32),
            jax.ShapeDtypeStruct((rows, features), jnp.float32),
            jax.ShapeDtypeStruct((shorts, features), jnp.float32),
            jax.ShapeDtypeStruct(readout.shape, jnp.bfloat16),
            jax.ShapeDtypeStruct(trigram.shape, jnp.bfloat16),
            jax.ShapeDtypeStruct((2, features), jnp.float32),
        ],
        compiler_params=pltpu.CompilerParams(vmem_limit_bytes=vmem_bytes),
        cost_estimate=cost(
            6 * features * vocabulary * (rows + 3 * shorts) + 24 * rows * shorts * features,
            8 * features * (rows + shorts) + 16 * features * vocabulary,
            vocabulary * (rows + 3 * shorts),
        ),
    )(
        mask_total.reshape(1, 1),
        first,
        short,
        scaling,
        readout,
        trigram,
        next_targets,
        weights,
        triples,
        triple_weights,
    )


def adam_step(master, prior_first, prior_second, gradient, factor, rate, decay):
    clipped = gradient * factor
    moment = beta_first * prior_first + (1.0 - beta_first) * clipped
    variance = beta_second * prior_second + (1.0 - beta_second) * clipped * clipped
    ratio = (
        moment
        / (1.0 - beta_first**STEP)
        / (jnp.sqrt(variance / (1.0 - beta_second**STEP)) + adam_epsilon)
    )
    return (master - rate * (ratio + decay * master), moment, variance)


def adam_kernel(layout, total_ref, *refs):
    group_count = 1 + max(at[0] for places in layout for at in places)
    weights = len(layout)
    group_refs, refs = refs[:group_count], refs[group_count:]
    masters, firsts, seconds = (refs[k * weights : (k + 1) * weights] for k in range(3))
    loss_ref, norm_ref = refs[3 * weights : 3 * weights + 2]
    outs = refs[3 * weights + 2 :]
    share = total_ref.shape[0] - 8
    loss_ref[...] = total_ref[share : share + 1, 0:1]
    square_total = jnp.sum(
        jnp.sum(total_ref[0:share], axis=1, keepdims=True), axis=0, keepdims=True
    )
    norm_value = jnp.sqrt(square_total)
    norm_ref[...] = norm_value
    factor = clip_limit / jnp.maximum(norm_value, clip_limit)
    for place, layers in enumerate(layout):
        for at, (group, start) in enumerate(layers):
            here = at if len(layers) > 1 else Ellipsis
            width = masters[place].shape[-1]
            gradient = group_refs[group][:, start : start + width]
            new = adam_step(
                masters[place][here],
                firsts[place][here],
                seconds[place][here],
                gradient,
                factor,
                learning_rates[place],
                weight_decays[place],
            )
            for kind in range(3):
                outs[kind * weights + place][here] = new[kind]


def adam_all(layout, totals, groups, masters, firsts, seconds):
    arrays = [*masters, *firsts, *seconds]
    shapes = [jax.ShapeDtypeStruct(array.shape, jnp.float32) for array in arrays]
    scalar = jax.ShapeDtypeStruct((1, 1), jnp.float32)
    moved = sum(8 * array.size for array in arrays)
    return pl.pallas_call(
        functools.partial(adam_kernel, layout),
        in_specs=whole_in_vmem(1 + len(groups) + len(arrays)),
        out_specs=whole_in_vmem(2 + len(arrays)),
        out_shape=[scalar, scalar, *shapes],
        compiler_params=pltpu.CompilerParams(vmem_limit_bytes=vmem_bytes),
        cost_estimate=cost(2 * moved, moved),
    )(totals, *groups, *arrays)


def pad_columns(array, width):
    return jnp.pad(array, ((0, 0), (0, width - array.shape[1])))


def local(
    tokens,
    next_targets,
    triple_targets,
    loss_mask,
    embedding,
    attention,
    projection,
    expansion,
    contraction,
    readout,
    trigram,
    scales,
    *moments,
):
    masters = (embedding, attention, projection, expansion, contraction, readout, trigram, scales)
    firsts = moments[:8]
    seconds = moments[8:]
    bits = index_bits()
    seq_size, dp_size = lax.axis_size("seq"), lax.axis_size("dp")
    devices = seq_size * dp_size
    held, piece = tokens.shape
    length = piece * seq_size
    sequences = held * dp_size
    members = devices // sequences
    vocabulary, share = embedding.shape
    features = share * devices
    hidden_size = expansion.shape[2]
    rows = length // members
    shorts = rows // 3
    member_bits = [("dp", b) for b in reversed(bits_of("dp")) if b < members]
    member = lax.axis_index("dp") % members
    group = (lax.axis_index("seq") * dp_size + lax.axis_index("dp")) // members

    integers = jnp.stack(
        [tokens, next_targets, triple_targets.reshape(held, piece), loss_mask]
    ).astype(jnp.bfloat16)
    integers = integers.reshape(share, -1)
    integer_width = integers.shape[1]
    integer_room = -(-integer_width // 128) * 128
    down_low = jnp.swapaxes(lowered(contraction), 1, 2)
    attention_low, projection_low, expansion_low = map(lowered, (attention, projection, expansion))
    parcels = (
        [
            pad_columns(integers, integer_room),
            pad_columns(lowered(scales).T, 128),
            lowered(embedding).T,
            attention_low[0],
        ],
        [projection_low[0], expansion_low[0], down_low[0]],
        [attention_low[1], projection_low[1], expansion_low[1]],
        [down_low[1], lowered(readout), lowered(trigram)],
    )
    spread = []
    for turn, parcel in enumerate(parcels):
        whole = gather_blocks(jnp.concatenate(parcel, axis=1), bits, rotated(bits, turn))
        start = 0
        for part in parcel:
            spread.append(whole[:, start : start + part.shape[1]])
            start += part.shape[1]
    (
        all_integers,
        scale_columns,
        embed_columns,
        attend_zero,
        project_zero,
        expand_zero,
        down_zero,
        attend_one,
        project_one,
        expand_one,
        down_one,
        readout_rows,
        trigram_rows,
    ) = spread
    scale_rows = scale_columns[:, :6].astype(jnp.float32).T
    all_integers = all_integers[:, :integer_width].reshape(
        seq_size, dp_size, 4, held, piece
    )
    mask_total = jnp.sum(all_integers[:, :, 3].astype(jnp.float32))
    inverse_total = 1.0 / jnp.maximum(mask_total, 1.0)
    sequence = lax.dynamic_slice(
        all_integers,
        (0, group // held, 0, group % held, 0),
        (seq_size, 1, 4, 1, piece),
    )
    sequence = jnp.swapaxes(sequence.reshape(seq_size, 4, piece), 0, 1).reshape(4, length)
    own = lax.dynamic_slice_in_dim(sequence, member * rows, rows, 1).astype(jnp.int32)
    sequence_tokens = sequence[0].astype(jnp.int32)
    own_tokens, own_next, own_triple, own_mask = own
    weights = own_mask.astype(jnp.float32)

    letters = jnp.arange(vocabulary, dtype=jnp.int32)
    is_token = (own_tokens[:, None] == letters).astype(jnp.bfloat16)
    place = member * rows + jnp.arange(rows, dtype=jnp.int32)
    earlier = (jnp.arange(length, dtype=jnp.int32)[None, :] <= place[:, None]).astype(jnp.bfloat16)
    counts = contract(
        earlier, (sequence_tokens[:, None] == letters).astype(jnp.bfloat16), "rt,tv->rv"
    )
    table = embed_columns.astype(jnp.float32).T
    table_inverse = norm_scale(table)
    table_normed = lowered(table * table_inverse * scale_rows[0])
    table_qkv = lowered(contract(table_normed, attend_zero, "vd,dc->vc"))
    embedded = contract(is_token, embed_columns, "rv,dv->rd")
    queries = lowered(contract(is_token, table_qkv[:, :features], "rv,vc->rc"))
    keys = table_qkv[:, features : 2 * features]
    values = table_qkv[:, 2 * features :]
    mixed_low, shares = weighted_attention(queries, keys, values, counts)
    hidden = embedded + contract(mixed_low, project_zero, "rd,de->re")
    first_stream, fed_zero = feed_forward(hidden, expand_zero, down_zero, scale_rows[1])

    along = [(i, i + 1) for i in range(dp_size - 1) if (i + 1) % members]
    back = [(i + 1, i) for i, _ in along]
    previous = lax.ppermute(first_stream[-2:], "dp", along)
    gap = jnp.arange(rows, dtype=jnp.int32)[None, :] + 2 - 3 * jnp.arange(
        shorts, dtype=jnp.int32
    )[:, None]
    pooling = ((gap >= 0) & (gap < 3)).astype(jnp.float32)
    pooled = exactly(pooling, first_stream, "jr,rd->jd")
    pooled = (
        jnp.concatenate([pooled[:1] + jnp.sum(previous, axis=0, keepdims=True), pooled[1:]]) / 3.0
    )

    pooled_inverse = norm_scale(pooled)
    pooled_normed = lowered(pooled * pooled_inverse * scale_rows[2])
    short_qkv = lowered(contract(pooled_normed, attend_one, "rd,dc->rc"))
    pairs = gather_blocks(short_qkv[:, features:], member_bits, member_bits)
    short_queries = short_qkv[:, :features]
    short_keys = pairs[:, :features]
    short_values = pairs[:, features:]
    short_place = member * shorts + jnp.arange(shorts, dtype=jnp.int32)
    visible = (
        jnp.arange(shorts * members, dtype=jnp.int32)[None, :] <= short_place[:, None]
    ).astype(jnp.float32)
    short_mixed_low, short_shares = weighted_attention(
        short_queries, short_keys, short_values, visible
    )
    short_hidden = pooled + contract(short_mixed_low, project_one, "rd,de->re")
    short_stream, fed_one = feed_forward(short_hidden, expand_one, down_one, scale_rows[3])

    (
        loss_local,
        merged_grad,
        short_grad,
        readout_grad,
        trigram_grad,
        head_scales,
    ) = both_heads(
        mask_total,
        first_stream,
        short_stream,
        scale_rows[4:6],
        readout_rows,
        trigram_rows,
        own_next[:, None],
        weights[:, None],
        own_triple.reshape(shorts, 3),
        weights.reshape(shorts, 3),
    )

    short_hidden_grad, expand_one_grad, down_one_grad, feed_one_scale = feed_back(
        short_hidden, fed_one, short_grad, expand_one, down_one, scale_rows[3]
    )
    short_hidden_low = lowered(short_hidden_grad)
    project_one_grad = lowered(contract(short_mixed_low, short_hidden_low, "rd,re->de"))
    short_mixed_grad = lowered(contract(short_hidden_low, project_one, "re,de->rd"))
    query_grad, key_grad, value_grad = weighted_attention_back(
        short_queries, short_keys, short_values, short_shares, short_mixed_grad
    )
    pair_terms = jnp.concatenate([key_grad, value_grad], axis=1)
    pair_grad = scatter_sums(lowered(pair_terms), member_bits, member_bits)
    short_qkv_grad = jnp.concatenate([query_grad, lowered(pair_grad)], axis=1)
    attend_one_grad = lowered(contract(pooled_normed, short_qkv_grad, "rd,rc->dc"))
    pooled_grad, attend_one_scale = norm_back(
        pooled,
        pooled_inverse,
        scale_rows[2],
        contract(short_qkv_grad, attend_one, "rc,dc->rd"),
    )
    pooled_grad = pooled_grad + short_hidden_grad

    pooled_grad = pooled_grad / 3.0
    returned = lax.ppermute(pooled_grad[:1], "dp", back)
    shifted_grad = exactly(pooling, pooled_grad, "jr,jd->rd")
    shifted_grad = jnp.concatenate([shifted_grad[:-2], shifted_grad[-2:] + returned])
    first_grad = merged_grad + shifted_grad
    hidden_grad, expand_zero_grad, down_zero_grad, feed_zero_scale = feed_back(
        hidden, fed_zero, first_grad, expand_zero, down_zero, scale_rows[1]
    )
    hidden_low = lowered(hidden_grad)
    project_zero_grad = lowered(contract(mixed_low, hidden_low, "rd,re->de"))
    mixed_grad = lowered(contract(hidden_low, project_zero, "re,de->rd"))
    query_grad, key_grad, value_grad = weighted_attention_back(
        queries, keys, values, shares, mixed_grad
    )
    table_query_grad = contract(is_token, query_grad, "rv,rc->vc")
    table_qkv_grad = lowered(
        jnp.concatenate([table_query_grad, key_grad, value_grad], axis=1)
    )
    attend_zero_grad = lowered(contract(table_normed, table_qkv_grad, "vd,vc->dc"))
    table_grad, attend_zero_scale = norm_back(
        table,
        table_inverse,
        scale_rows[0],
        contract(table_qkv_grad, attend_zero, "vc,dc->vd"),
    )
    table_grad = table_grad + contract(is_token, hidden_low, "rv,rd->vd")
    scale_grads = jnp.stack(
        [
            attend_zero_scale,
            feed_zero_scale,
            attend_one_scale,
            feed_one_scale,
            head_scales[0],
            head_scales[1],
        ],
        axis=1,
    )

    returns = (
        [readout_grad, trigram_grad, down_one_grad, expand_one_grad],
        [project_one_grad, attend_one_grad],
        [down_zero_grad, expand_zero_grad],
        [
            project_zero_grad,
            attend_zero_grad,
            lowered(table_grad.T),
            lowered(pad_columns(scale_grads, 128)),
        ],
    )
    sums, squares = [], []
    for turn, parcel in enumerate(returns):
        total, square = reduce_parts(parcel, bits, list(reversed(rotated(bits, turn))), share)
        sums.append(total)
        squares.append(square)
    totals = jnp.concatenate(
        [sum(squares), jnp.broadcast_to(loss_local, (8, lanes))], axis=0
    )
    for step in reversed(bits):
        totals = totals + swapped(totals, step)
    starts = []
    for group, parcel in enumerate(returns):
        at = 0
        for part in parcel:
            starts.append((group, at))
            at += part.shape[1]
    (
        readout_at,
        trigram_at,
        down_one_at,
        expand_one_at,
        project_one_at,
        attend_one_at,
        down_zero_at,
        expand_zero_at,
        project_zero_at,
        attend_zero_at,
        embed_at,
        scale_at,
    ) = starts
    scale_sum = sums[scale_at[0]][:, scale_at[1] : scale_at[1] + 6].T
    layout = (
        (embed_at,),
        (attend_zero_at, attend_one_at),
        (project_zero_at, project_one_at),
        (expand_zero_at, expand_one_at),
        (down_zero_at, down_one_at),
        (readout_at,),
        (trigram_at,),
        ((len(sums), 0),),
    )

    def turned(arrays):
        embed, attend, project, expand, down, *rest = arrays
        return (embed.T, attend, project, expand, jnp.swapaxes(down, 1, 2), *rest)

    loss_total, norm_value, *results = adam_all(
        layout,
        totals,
        [*sums, scale_sum],
        turned(masters),
        turned(firsts),
        turned(seconds),
    )
    return (
        loss_total.reshape(()),
        mask_total,
        norm_value.reshape(()),
        *turned(results[:8]),
        *turned(results[8:16]),
        *turned(results[16:]),
    )


def solution(mesh):
    weight_specs = (
        P(None, ("seq", "dp")),
        P(None, ("seq", "dp"), None),
        P(None, ("seq", "dp"), None),
        P(None, ("seq", "dp"), None),
        P(None, None, ("seq", "dp")),
        P(("seq", "dp"), None),
        P(("seq", "dp"), None),
        P(None, ("seq", "dp")),
    )
    in_specs = (
        P("dp", "seq"),
        P("dp", "seq"),
        P("dp", "seq", None),
        P("dp", "seq"),
    ) + weight_specs * 3
    out_specs = (P(), P(), P()) + weight_specs * 3
    return jax.shard_map(local, mesh=mesh, in_specs=in_specs, out_specs=out_specs, check_vma=False)
```

```python
import functools

import jax
import jax.numpy as jnp
from jax import lax
from jax.experimental import pallas as pl
from jax.experimental.pallas import tpu as pltpu
from jax.sharding import PartitionSpec as P

HEADS = 8
STEP = 10


norm_epsilon = 1e-06
trigram_share = 0.5
clip_limit = 0.1
beta_first = 0.9
beta_second = 0.95
adam_epsilon = 1e-08
learning_rates = (0.6, 0.05, 0.2, 0.05, 0.03, 0.05, 0.05, 0.6)
weight_decays = (0.0, 0.1, 0.1, 0.1, 0.1, 0.1, 0.1, 0.0)
exact_precision = lax.Precision.HIGHEST
megabyte = 1024 * 1024
lanes = 128


def lowered(array):
    return array.astype(jnp.bfloat16)


def contract(left, right, form):
    return jnp.einsum(form, left, right, preferred_element_type=jnp.float32)


def exactly(left, right, form):
    return jnp.einsum(
        form, left, right, preferred_element_type=jnp.float32, precision=exact_precision
    )


def bits_of(axis):
    return [1 << k for k in range((lax.axis_size(axis) - 1).bit_length())]


def index_bits():
    return [("seq", b) for b in reversed(bits_of("seq"))] + [
        ("dp", b) for b in reversed(bits_of("dp"))
    ]


def own_bit(step):
    axis, weight = step
    return (lax.axis_index(axis) // weight) % 2


def swapped(x, step):
    axis, weight = step
    return lax.ppermute(x, axis, [(i, i ^ weight) for i in range(lax.axis_size(axis))])


def stages_of(bits):
    rest = bits[:-1]
    return [rest[max(0, end - 2) : end] for end in range(len(rest), 0, -2)]


def exchanged(x, steps):
    masks = {"seq": 0, "dp": 0}
    for axis, weight in steps:
        masks[axis] |= weight
    if not masks["seq"]:
        pairs = [(i, i ^ masks["dp"]) for i in range(lax.axis_size("dp"))]
        return lax.ppermute(x, "dp", pairs)
    if not masks["dp"]:
        pairs = [(i, i ^ masks["seq"]) for i in range(lax.axis_size("seq"))]
        return lax.ppermute(x, "seq", pairs)
    width = lax.axis_size("dp")
    pairs = [
        (i * width + j, (i ^ masks["seq"]) * width + (j ^ masks["dp"]))
        for i in range(lax.axis_size("seq"))
        for j in range(width)
    ]
    return lax.ppermute(x, ("seq", "dp"), pairs)


def chosen_steps(stage, number):
    return [step for at, step in enumerate(stage) if number >> (len(stage) - 1 - at) & 1]


def own_number(stage):
    number = jnp.int32(0)
    for step in stage:
        number = 2 * number + own_bit(step)
    return number


def stage_blocks(x, stage):
    return [x] + [exchanged(x, chosen_steps(stage, m)) for m in range(1, 1 << len(stage))]


def stage_gather(x, stage):
    return jnp.concatenate(stage_blocks(x, stage))


def merge_kernel(widths, pieces, number_ref, *refs):
    mine, others, outs = refs[:pieces], refs[pieces : 2 * pieces], refs[2 * pieces :]
    bit, number = number_ref[0], number_ref[1]
    for piece in range(pieces):
        start = 0
        at = pl.ds(number ^ piece, 1)
        for width, out in zip(widths, outs):
            span = slice(start, start + width)
            out[at, pl.ds(bit, 1)] = mine[piece][:, :, span][None]
            out[at, pl.ds(1 - bit, 1)] = others[piece][:, :, span][None]
            start += width


def merge_blocks(mine, others, widths, bits):
    blocks, share, width = mine[0].shape
    pieces = len(mine)
    stages = stages_of(bits)
    block = jnp.arange(blocks, dtype=jnp.int32)
    place = jnp.zeros((blocks,), jnp.int32)
    low = 0
    for stage in stages[1:]:
        high = len(bits) - 1 - len(stages[0]) - low - len(stage)
        number = (block >> high) % (1 << len(stage)) ^ own_number(stage)
        place = place + (number << low)
        low += len(stage)
    numbers = jnp.concatenate(
        [jnp.stack([own_bit(bits[-1]), own_number(stages[0])]), place]
    )
    taken = pl.BlockSpec((1, share, width), lambda i, numbers: (i, 0, 0))
    outs = pl.pallas_call(
        functools.partial(merge_kernel, widths, pieces),
        grid_spec=pltpu.PrefetchScalarGridSpec(
            num_scalar_prefetch=1,
            grid=(blocks,),
            in_specs=[taken] * (2 * pieces),
            out_specs=[
                pl.BlockSpec(
                    (pieces, 2, share, w), lambda i, numbers: (numbers[2 + i], 0, 0, 0)
                )
                for w in widths
            ],
        ),
        out_shape=[
            pltpu.HBM((pieces * blocks, 2, share, w), mine[0].dtype) for w in widths
        ],
        compiler_params=pltpu.CompilerParams(vmem_limit_bytes=12 * megabyte),
        cost_estimate=cost(0, 8 * pieces * blocks * share * width),
    )(numbers, *[in_hbm(x) for x in (*mine, *others)])
    return [out.reshape(2 * pieces * blocks * share, out.shape[-1]) for out in outs]


def together(*arrays):
    return lax.optimization_barrier(arrays)


def whole_in_vmem(count):
    return [pl.BlockSpec(memory_space=pltpu.VMEM)] * count


def in_hbm(array):
    return pltpu.with_memory_space_constraint(array, pltpu.HBM)


def cost(flops, moved, exponentials=0):
    return pl.CostEstimate(
        flops=int(flops), bytes_accessed=int(moved), transcendentals=int(exponentials)
    )


def halves(product, bit):
    low, high = product[:, 0], product[:, 1]
    return jnp.where(bit == 0, high, low), jnp.where(bit == 0, low, high)


def by_core(product, share):
    return lowered(product).reshape(-1, 2, share, product.shape[-1])


def split_kernel(widths, summands, pieces, number_ref, *refs):
    sources, outs = refs[: len(widths) * summands], refs[len(widths) * summands :]
    number = number_ref[0]
    start = 0
    for at, width in enumerate(widths):
        terms = sources[at * summands : (at + 1) * summands]
        for m in range(pieces):
            place = pl.ds(number ^ m, 1)
            total = terms[0][:, place].astype(jnp.float32)
            for term in terms[1:]:
                total = total + term[:, place].astype(jnp.float32)
            outs[m][:, :, start : start + width] = lowered(total)[:, 0]
        start += width


def add_and_split(sources, stage):
    blocks, share, _ = sources[0][0].shape
    pieces = 1 << len(stage)
    widths = [terms[0].shape[-1] for terms in sources]
    total = sum(widths)
    arrays = [
        in_hbm(term.reshape(blocks // pieces, pieces, share, term.shape[-1]))
        for terms in sources
        for term in terms
    ]
    return pl.pallas_call(
        functools.partial(split_kernel, widths, len(sources[0]), pieces),
        grid_spec=pltpu.PrefetchScalarGridSpec(
            num_scalar_prefetch=1,
            grid=(blocks // pieces,),
            in_specs=[
                pl.BlockSpec((1, *x.shape[1:]), lambda i, number: (i, 0, 0, 0)) for x in arrays
            ],
            out_specs=[pl.BlockSpec((1, share, total), lambda i, number: (i, 0, 0))] * pieces,
        ),
        out_shape=[pltpu.HBM((blocks // pieces, share, total), jnp.bfloat16)] * pieces,
        compiler_params=pltpu.CompilerParams(vmem_limit_bytes=16 * megabyte),
        cost_estimate=cost(1, 1),
    )(own_number(stage).reshape(1), *arrays)


def add_and_square_kernel(*refs):
    *terms, total_ref, square_ref = refs
    total = terms[0][...].astype(jnp.float32)
    for term in terms[1:]:
        total = total + term[...].astype(jnp.float32)
    total_ref[...] = total
    squares = jnp.zeros(square_ref.shape, jnp.float32)
    for start in range(0, total.shape[1], lanes):
        piece = total[:, start : start + lanes]
        squares = squares + piece * piece
    square_ref[...] = squares


def add_and_square(terms):
    share, width = terms[0].shape[-2:]
    return pl.pallas_call(
        add_and_square_kernel,
        in_specs=whole_in_vmem(len(terms)),
        out_specs=whole_in_vmem(2),
        out_shape=[
            jax.ShapeDtypeStruct((share, width), jnp.float32),
            jax.ShapeDtypeStruct((share, lanes), jnp.float32),
        ],
        compiler_params=pltpu.CompilerParams(vmem_limit_bytes=8 * megabyte),
        cost_estimate=cost(3 * share * width, 12 * share * width),
    )(*[term.reshape(share, width) for term in terms])


def stage_sums(pieces, stage):
    return [pieces[0]] + [
        exchanged(pieces[m], chosen_steps(stage, m)) for m in range(1, 1 << len(stage))
    ]


def norm_scale(stream):
    return lax.rsqrt(jnp.mean(stream * stream, axis=-1, keepdims=True) + norm_epsilon)


def norm_back(stream, inverse, scaling, gradient):
    unit = stream * inverse
    scaled = gradient * scaling
    scaling_grad = jnp.sum(gradient * unit, axis=0)
    stream_grad = inverse * (scaled - unit * jnp.mean(scaled * unit, axis=-1, keepdims=True))
    return stream_grad, scaling_grad


def times(left, right, left_side=1, right_side=0):
    return lax.dot_general(
        left, right, (((left_side,), (right_side,)), ((), ())), preferred_element_type=jnp.float32
    )


def exact_times(left, right, left_side=1, right_side=0):
    return lax.dot_general(
        left,
        right,
        (((left_side,), (right_side,)), ((), ())),
        preferred_element_type=jnp.float32,
        precision=exact_precision,
    )


def head_groups(features):
    depth = features // HEADS
    together = max(1, lanes // depth)
    return depth, [
        (first * depth, together * depth, range(first, first + together))
        for first in range(0, HEADS, together)
    ]


def own_lanes(width, depth, at):
    lane = lax.broadcasted_iota(jnp.int32, (1, width), 1)
    return (lane >= at * depth) & (lane < (at + 1) * depth)


def attend(queries, key_ref, value_ref, counts, share_ref):
    features = queries.shape[1]
    depth, groups = head_groups(features)
    queries = queries * jnp.asarray(depth ** (-0.5), queries.dtype)
    turned_values = value_ref[...].T
    mixed = []
    for start, width, places in groups:
        span = slice(start, start + width)
        keys = key_ref[:, span]
        for at, place in enumerate(places):
            own = own_lanes(width, depth, at)
            scores = times(jnp.where(own, keys, jnp.zeros_like(keys)), queries[:, span], 1, 1)
            scores = jnp.where(counts > 0.0, scores, -1e30)
            exponent = counts * jnp.exp(scores - jnp.max(scores, axis=0, keepdims=True))
            shares = lowered(exponent * (1.0 / jnp.sum(exponent, axis=0, keepdims=True)))
            share_ref[place] = shares
            here = slice(start + at * depth, start + (at + 1) * depth)
            mixed.append(lowered(times(turned_values[here], shares)))
    return jnp.concatenate(mixed, axis=0)


def attend_back(queries, key_ref, value_ref, share_ref, gradient, key_out, value_out):
    features = queries.shape[1]
    depth, groups = head_groups(features)
    scaled = depth ** (-0.5)
    turned_keys = key_ref[...].T
    query_grads = []
    for start, width, places in groups:
        span = slice(start, start + width)
        values = value_ref[:, span]
        key_sum = value_sum = None
        for at, place in enumerate(places):
            own = own_lanes(width, depth, at)
            low = share_ref[place]
            shares = low.astype(jnp.float32)
            share_grad = times(
                jnp.where(own, values, jnp.zeros_like(values)), gradient[:, span], 1, 1
            )
            dots = jnp.sum(shares * share_grad, axis=0, keepdims=True)
            score_grad = lowered(shares * (share_grad - dots))
            here = slice(start + at * depth, start + (at + 1) * depth)
            query_grads.append(lowered(times(turned_keys[here], score_grad) * scaled))
            key_part = times(score_grad, queries[:, span])
            value_part = times(low, gradient[:, span])
            if key_sum is None:
                key_sum, value_sum = key_part, value_part
            else:
                key_sum = jnp.where(own, key_part, key_sum)
                value_sum = jnp.where(own, value_part, value_sum)
        key_out[:, span] = lowered(key_sum * scaled)
        value_out[:, span] = lowered(value_sum)
    return jnp.concatenate(query_grads, axis=0)


def attend_kernel(query_ref, key_ref, value_ref, count_ref, mixed_ref, share_ref):
    mixed_ref[...] = attend(
        query_ref[...], key_ref, value_ref, count_ref[...], share_ref
    ).T


def weighted_attention(queries, table_qkv, counts):
    rows, features = queries.shape
    entries = table_qkv.shape[0]
    return pl.pallas_call(
        attend_kernel,
        grid=(1,),
        in_specs=[
            pl.BlockSpec((rows, features), lambda i: (0, 0)),
            pl.BlockSpec((entries, features), lambda i: (0, 1)),
            pl.BlockSpec((entries, features), lambda i: (0, 2)),
            pl.BlockSpec((entries, rows), lambda i: (0, 0)),
        ],
        out_specs=[
            pl.BlockSpec((rows, features), lambda i: (0, 0)),
            pl.BlockSpec((HEADS, entries, rows), lambda i: (0, 0, 0)),
        ],
        out_shape=[
            jax.ShapeDtypeStruct((rows, features), jnp.bfloat16),
            pltpu.HBM((HEADS, entries, rows), jnp.bfloat16),
        ],
        compiler_params=pltpu.CompilerParams(vmem_limit_bytes=24 * megabyte),
        cost_estimate=cost(
            4 * rows * entries * features,
            4 * rows * features + 4 * entries * features + (2 * HEADS + 4) * rows * entries,
            HEADS * rows * entries,
        ),
    )(queries, table_qkv, table_qkv, counts)


gelu_rate = 0.7978845608
gelu_cube = 0.044715


feed_steps = 4
feed_parts = 2
upper_steps = 2


def gelu_terms(before):
    square = before * before
    bent = jnp.tanh(before * (gelu_rate + gelu_rate * gelu_cube * square))
    half = 0.5 + 0.5 * bent
    return square, bent, half


def feed_forward_part(normed, in_ref, down_ref):
    width = in_ref.shape[1] // feed_parts
    total = None
    for part in range(feed_parts):
        span = slice(part * width, (part + 1) * width)
        before = times(normed, in_ref[:, span])
        _, _, half = gelu_terms(before)
        product = times(lowered(before * half), down_ref[:, span], 1, 1)
        total = product if total is None else total + product
    return total


def feed_forward_kernel(
    token_ref,
    embed_ref,
    mixed_ref,
    project_ref,
    in_ref,
    down_ref,
    scale_ref,
    result_ref,
    normed_ref,
    hidden_ref,
):
    @pl.when(pl.program_id(0) == 0)
    def _():
        hidden = times(token_ref[...], embed_ref[...], 1, 1) + times(
            mixed_ref[...], project_ref[...]
        )
        hidden_ref[...] = hidden
        normed_ref[...] = lowered(hidden * norm_scale(hidden) * scale_ref[...])
        result_ref[...] = hidden

    result_ref[...] += feed_forward_part(normed_ref[...], in_ref, down_ref)


def first_layer_end(is_token, embed_columns, mixed_low, project, in_weight, down_weight, scaling):
    rows, features = mixed_low.shape
    hidden_size = in_weight.shape[1]
    width = hidden_size // feed_steps

    def whole(shape):
        return pl.BlockSpec(shape, lambda j: (0, 0))

    chunk = pl.BlockSpec((features, width), lambda j: (0, j))
    return pl.pallas_call(
        feed_forward_kernel,
        grid=(feed_steps,),
        in_specs=[
            whole(is_token.shape),
            whole(embed_columns.shape),
            whole(mixed_low.shape),
            whole(project.shape),
            chunk,
            chunk,
            whole(scaling.shape),
        ],
        out_specs=[whole((rows, features))] * 3,
        out_shape=[
            pltpu.HBM((rows, features), jnp.float32),
            pltpu.HBM((rows, features), jnp.bfloat16),
            pltpu.HBM((rows, features), jnp.float32),
        ],
        compiler_params=pltpu.CompilerParams(vmem_limit_bytes=20 * megabyte),
        cost_estimate=cost(
            4 * rows * features * hidden_size,
            4 * features * hidden_size + 14 * rows * features,
            rows * hidden_size,
        ),
    )(
        in_hbm(is_token),
        in_hbm(embed_columns),
        mixed_low,
        in_hbm(project),
        in_hbm(in_weight),
        in_hbm(down_weight),
        scaling,
    )


def pool_kernel(
    first_ref, last_ref, attend_ref, scale_ref, pooled_ref, normed_ref, query_ref, pair_ref
):
    rows, shorts = first_ref.shape[0], pooled_ref.shape[0]
    gap = (
        lax.broadcasted_iota(jnp.int32, (shorts, rows), 1)
        + 2
        - 3 * lax.broadcasted_iota(jnp.int32, (shorts, rows), 0)
    )
    pooling = jnp.where((gap >= 0) & (gap < 3), 1.0, 0.0)
    pooled = exact_times(pooling, first_ref[...])
    row = lax.broadcasted_iota(jnp.int32, (shorts, 1), 0)
    pooled = (
        pooled + jnp.where(row == 0, jnp.sum(last_ref[...], axis=0, keepdims=True), 0.0)
    ) * (1.0 / 3.0)
    pooled_ref[...] = pooled
    normed = lowered(pooled * norm_scale(pooled) * scale_ref[...])
    normed_ref[...] = normed
    features = first_ref.shape[1]
    query_ref[...] = lowered(times(normed, attend_ref[:, :features]))
    pair_ref[...] = lowered(times(normed, attend_ref[:, features:]))


def pooled_rows(first, previous, weights, scaling, shorts):
    rows, features = first.shape

    def whole(shape):
        return pl.BlockSpec(shape, lambda j: (0, 0))

    return pl.pallas_call(
        pool_kernel,
        grid=(1,),
        in_specs=[
            whole(first.shape),
            whole(previous.shape),
            whole((features, 3 * features)),
            whole(scaling.shape),
        ],
        out_specs=[
            whole((shorts, features)),
            whole((shorts, features)),
            whole((shorts, features)),
            whole((shorts, 2 * features)),
        ],
        out_shape=[
            pltpu.HBM((shorts, features), jnp.float32),
            pltpu.HBM((shorts, features), jnp.bfloat16),
            pltpu.HBM((shorts, features), jnp.bfloat16),
            jax.ShapeDtypeStruct((shorts, 2 * features), jnp.bfloat16),
        ],
        compiler_params=pltpu.CompilerParams(vmem_limit_bytes=12 * megabyte),
        cost_estimate=cost(
            6 * shorts * features * features + 12 * rows * shorts * features,
            6 * features * features + 4 * rows * features,
        ),
    )(in_hbm(first), previous, in_hbm(weights), scaling)


def feed_back_part(normed, gradient, in_weight, down_weight, turned_gradient, turned_normed, store):
    before = times(normed, in_weight)
    square, bent, half = gelu_terms(before)
    slope = half + half * (1.0 - bent) * before * (
        gelu_rate + 3.0 * gelu_rate * gelu_cube * square
    )
    before_grad = lowered(times(gradient, down_weight) * slope)
    store(0, times(turned_gradient, lowered(before * half)))
    store(1, times(turned_normed, before_grad))
    return times(before_grad, in_weight, 1, 1)


def feed_back_kernel(share, pieces, number_ref, *refs):
    (
        above_ref,
        back_ref,
        other_gradient_ref,
        other_back_ref,
        normed_ref,
        other_normed_ref,
        in_ref,
        down_ref,
        *outs,
        grad_out,
        other_grad_out,
        gradient_out,
        gradient_ref,
        all_normed,
        turned_gradient,
        turned_normed,
        normed_grad,
        product_ref,
    ) = refs
    step = pl.program_id(0)
    number = number_ref[1]
    rows = above_ref.shape[0]

    @pl.when(step == 0)
    def _():
        row = lax.broadcasted_iota(jnp.int32, (rows, 1), 0)
        gradient = above_ref[...] + jnp.where(row >= rows - 2, back_ref[0:1], 0.0)
        gradient_out[...] = gradient
        gradient_ref[:rows] = lowered(gradient)
        gradient_ref[rows:] = lowered(
            other_gradient_ref[...].astype(jnp.float32)
            + jnp.where(row >= rows - 2, other_back_ref[0:1], 0.0)
        )
        all_normed[:rows] = normed_ref[...]
        all_normed[rows:] = other_normed_ref[...]
        turned_gradient[...] = gradient_ref[...].T
        turned_normed[...] = all_normed[...].T
        normed_grad[...] = jnp.zeros_like(normed_grad)

    width = in_ref.shape[1]

    def store(place, product):
        product_ref[...] = lowered(product).reshape(product_ref.shape)
        span = slice(place * width, (place + 1) * width)
        for m in range(pieces):
            outs[m][:, :, span] = product_ref[:, pl.ds(number ^ m, 1)][:, 0]

    normed_grad[...] += feed_back_part(
        all_normed[...],
        gradient_ref[...],
        in_ref[...],
        down_ref[...],
        turned_gradient[...],
        turned_normed[...],
        store,
    )

    @pl.when(step == pl.num_programs(0) - 1)
    def _():
        grad_out[...] = normed_grad[:rows]
        other_grad_out[...] = lowered(normed_grad[rows:])


def feed_back(
    above,
    back,
    other_gradient,
    other_back,
    normed,
    other_normed,
    in_weight,
    down_weight,
    stage,
    bit,
    share,
):
    rows, features = above.shape
    hidden_size = in_weight.shape[1]
    steps = feed_steps
    width = hidden_size // (2 * steps)
    blocks = features // (2 * share)
    pieces = 1 << len(stage)
    far = blocks // pieces

    def whole(shape):
        return pl.BlockSpec(shape, lambda j, numbers: (0, 0))

    chunk = pl.BlockSpec((features, width), lambda j, numbers: (0, numbers[0] * steps + j))
    piece = pl.BlockSpec((far, 2 * share, 2 * width), lambda j, numbers: (0, 0, j))
    *results, grad, other_grad, gradient = pl.pallas_call(
        functools.partial(feed_back_kernel, share, pieces),
        grid_spec=pltpu.PrefetchScalarGridSpec(
            num_scalar_prefetch=1,
            grid=(steps,),
            in_specs=[
                whole(above.shape),
                whole(back.shape),
                whole(above.shape),
                whole(back.shape),
                whole(normed.shape),
                whole(normed.shape),
                chunk,
                chunk,
            ],
            out_specs=[piece] * pieces + [whole(above.shape)] * 3,
            scratch_shapes=[
                pltpu.VMEM((2 * rows, features), jnp.bfloat16),
                pltpu.VMEM((2 * rows, features), jnp.bfloat16),
                pltpu.VMEM((features, 2 * rows), jnp.bfloat16),
                pltpu.VMEM((features, 2 * rows), jnp.bfloat16),
                pltpu.VMEM((2 * rows, features), jnp.float32),
                pltpu.VMEM((far, pieces, 2 * share, width), jnp.bfloat16),
            ],
        ),
        out_shape=[pltpu.HBM((far, 2 * share, hidden_size), jnp.bfloat16)] * pieces
        + [
            jax.ShapeDtypeStruct(above.shape, jnp.float32),
            jax.ShapeDtypeStruct(above.shape, jnp.bfloat16),
            pltpu.HBM(above.shape, jnp.float32),
        ],
        compiler_params=pltpu.CompilerParams(vmem_limit_bytes=36 * megabyte),
        cost_estimate=cost(1, 1),
    )(
        jnp.stack([bit, own_number(stage)]),
        in_hbm(above),
        back,
        other_gradient,
        other_back,
        in_hbm(normed),
        in_hbm(other_normed),
        in_hbm(in_weight),
        in_hbm(down_weight),
    )
    return results, grad, other_grad, gradient


def middle_kernel(
    share,
    members,
    bit_ref,
    query_ref,
    *refs,
):
    pair_refs, refs = refs[:members], refs[members:]
    (
        normed_ref,
        mixed_ref,
        low_ref,
        pooled_ref,
        hidden_grad_ref,
        above_ref,
        attend_ref,
        scale_ref,
        sent_ref,
        kept_ref,
        rows_out,
        rows_low_out,
        back_out,
        scale_out,
    ) = refs
    bit = bit_ref[0]
    features = query_ref.shape[1]
    pairs = pair_refs[0][...].astype(jnp.float32)
    for pair_ref in pair_refs[1:]:
        pairs = pairs + pair_ref[...].astype(jnp.float32)
    pairs = lowered(pairs)
    queries = query_ref[...]
    normed_grad = times(queries, attend_ref[:, :features], 1, 1) + times(
        pairs, attend_ref[:, features:], 1, 1
    )
    pooled = pooled_ref[...]
    pooled_grad, scaling_grad = norm_back(
        pooled, norm_scale(pooled), scale_ref[...], normed_grad
    )
    scale_out[...] = scaling_grad[None]
    pooled_grad = (pooled_grad + hidden_grad_ref[...]) * (1.0 / 3.0)
    back_out[...] = pooled_grad[0 : back_out.shape[0]]
    rows, shorts = rows_out.shape[0], pooled.shape[0]
    gap = (
        lax.broadcasted_iota(jnp.int32, (rows, shorts), 0)
        + 2
        - 3 * lax.broadcasted_iota(jnp.int32, (rows, shorts), 1)
    )
    spreading = jnp.where((gap >= 0) & (gap < 3), 1.0, 0.0)
    rows_grad = above_ref[...] + exact_times(spreading, pooled_grad)
    rows_out[...] = rows_grad
    rows_low_out[...] = lowered(rows_grad)
    turned_normed = normed_ref[...].T
    start = 0
    for product in (
        lambda: times(turned_normed, queries),
        lambda: times(turned_normed, pairs),
        lambda: times(mixed_ref[...], low_ref[...], 0, 0),
    ):
        product = product()
        span = slice(start, start + product.shape[1])
        sent_ref[:, :, span], kept_ref[:, :, span] = halves(by_core(product, share), bit)
        start += product.shape[1]


def middle_gradients(
    bits,
    query_grad,
    pair_grads,
    normed,
    mixed_low,
    hidden_low,
    pooled,
    hidden_grad,
    above,
    weights,
    scaling,
    share,
):
    shorts, features = pooled.shape
    rows = above.shape[0]
    chips = features // (2 * share)
    width = 4 * features

    def whole(shape):
        return pl.BlockSpec(shape, lambda j, bit: (0, 0))

    operands = [
        query_grad,
        *pair_grads,
        normed,
        mixed_low,
        hidden_low,
        pooled,
        hidden_grad,
        above,
        weights,
        scaling,
    ]
    specs = [whole(x.shape) for x in operands]
    specs[-2] = whole((features, 3 * features))
    buffer = pltpu.HBM((chips, share, width), jnp.bfloat16)
    piece = pl.BlockSpec((chips, share, width), lambda j, bit: (0, 0, 0))
    return pl.pallas_call(
        functools.partial(middle_kernel, share, len(pair_grads)),
        grid_spec=pltpu.PrefetchScalarGridSpec(
            num_scalar_prefetch=1,
            grid=(1,),
            in_specs=specs,
            out_specs=[
                piece,
                piece,
                whole(above.shape),
                whole(above.shape),
                whole((8, features)),
                whole((1, features)),
            ],
        ),
        out_shape=[
            buffer,
            buffer,
            pltpu.HBM(above.shape, jnp.float32),
            jax.ShapeDtypeStruct(above.shape, jnp.bfloat16),
            jax.ShapeDtypeStruct((8, features), jnp.float32),
            pltpu.HBM((1, features), jnp.float32),
        ],
        compiler_params=pltpu.CompilerParams(vmem_limit_bytes=24 * megabyte),
        cost_estimate=cost(1, 1),
    )(own_bit(bits[-1]).reshape(1), *[in_hbm(x) for x in operands])


def head_terms(stream, scaling, matrix, columns, factor):
    count = columns.shape[1] // 2
    inverse = norm_scale(stream)
    normed_low = lowered(stream * inverse * scaling)
    logits = times(normed_low, matrix)
    vocabulary = logits.shape[1] // count
    letters = lax.broadcasted_iota(jnp.int32, (stream.shape[0], vocabulary), 1)
    gradients = []
    loss = None
    for place in range(count):
        some = logits[:, place * vocabulary : (place + 1) * vocabulary]
        highest = jnp.max(some, axis=-1, keepdims=True)
        exponent = jnp.exp(some - highest)
        denominator = jnp.sum(exponent, axis=-1, keepdims=True)
        matches = letters == columns[:, place : place + 1]
        picked = jnp.sum(jnp.where(matches, some, 0.0), axis=-1, keepdims=True)
        weight = columns[:, count + place : count + place + 1].astype(jnp.float32)
        term = weight * (highest + jnp.log(denominator) - picked)
        loss = term if loss is None else loss + term
        chance = exponent * (1.0 / denominator)
        gradients.append(lowered((chance - jnp.where(matches, 1.0, 0.0)) * (weight * factor)))
    logit_low = gradients[0] if len(gradients) == 1 else jnp.concatenate(gradients, axis=1)
    matrix_grad = times(normed_low, logit_low, 0, 0)
    stream_grad, scaling_grad = norm_back(
        stream, inverse, scaling, times(logit_low, matrix, 1, 1)
    )
    return jnp.sum(loss, axis=0, keepdims=True), stream_grad, scaling_grad, lowered(matrix_grad)


def heads_part(
    share,
    bit,
    total,
    first,
    short,
    scaling,
    readout,
    trigram,
    main_columns,
    triple_columns,
    sent_ref,
    kept_ref,
):
    inverse_total = 1.0 / jnp.maximum(total, 1.0)
    vocabulary = readout.shape[1]
    rows, shorts = first.shape[0], short.shape[0]
    gap = lax.broadcasted_iota(jnp.int32, (rows, shorts), 0) - 3 * lax.broadcasted_iota(
        jnp.int32, (rows, shorts), 1
    )
    thrice = jnp.where((gap >= 0) & (gap < 3), 1.0, 0.0)
    merged = first + exact_times(thrice, short)
    main_loss, merged_grad, main_scale, readout_grad = head_terms(
        merged, scaling[0:1], readout, main_columns, inverse_total
    )
    sent_ref[:, :, :vocabulary], kept_ref[:, :, :vocabulary] = halves(
        by_core(readout_grad, share), bit
    )
    extra_loss, short_grad, extra_scale, trigram_grad = head_terms(
        short, scaling[1:2], trigram, triple_columns, trigram_share * inverse_total
    )
    sent_ref[:, :, vocabulary:], kept_ref[:, :, vocabulary:] = halves(
        by_core(trigram_grad, share), bit
    )
    short_grad = short_grad + exact_times(thrice, merged_grad, 0, 0)
    loss = main_loss + trigram_share * extra_loss
    return loss, merged_grad, short_grad, main_scale[None], extra_scale[None]


def upper_kernel(share, members, number_ref, total_ref, query_ref, *refs):
    pair_refs, refs = refs[:members], refs[members:]
    (
        pooled_ref,
        first_ref,
        scale_ref,
        project_ref,
        in_ref,
        down_ref,
        readout_ref,
        trigram_ref,
        main_ref,
        triple_ref,
        loss_ref,
        first_out,
        sent_ref,
        kept_ref,
        table_sent,
        table_kept,
        mixed_out,
        low_out,
        hidden_out,
        query_out,
        *refs,
    ) = refs
    pair_outs, refs = refs[:members], refs[members:]
    (
        scale_out,
        key_ref,
        value_ref,
        key_out,
        value_out,
        share_ref,
        hidden_ref,
        normed_ref,
        short_ref,
        gradient_ref,
        turned_gradient,
        turned_normed,
        normed_grad,
        in_scratch,
        down_scratch,
    ) = refs
    step = pl.program_id(0)
    bit, member = number_ref[0], number_ref[1]

    @pl.when(step == 0)
    def _():
        rows, features = query_ref.shape
        row = lax.broadcasted_iota(jnp.int32, (rows, rows), 1)
        entry = lax.broadcasted_iota(jnp.int32, (rows, rows), 0)
        counts = []
        for at, pair_ref in enumerate(pair_refs):
            here = slice(at * rows, (at + 1) * rows)
            key_ref[here], value_ref[here] = pair_ref[:, :features], pair_ref[:, features:]
            ahead = (member - (member ^ at)) * rows
            counts.append(jnp.where(entry <= row + ahead, 1.0, 0.0))
        mixed = attend(
            query_ref[...], key_ref, value_ref, jnp.concatenate(counts, axis=0), share_ref
        ).T
        mixed_out[...] = mixed
        hidden = pooled_ref[...] + times(mixed, project_ref[...])
        hidden_ref[...] = hidden
        normed_ref[...] = lowered(hidden * norm_scale(hidden) * scale_ref[0:1])
        short_ref[...] = hidden

    width = in_ref.shape[1]
    steps = in_scratch.shape[0]

    @pl.when(step < steps)
    def _():
        short_ref[...] += feed_forward_part(normed_ref[...], in_ref, down_ref)
        in_scratch[step] = in_ref[...]
        down_scratch[step] = down_ref[...]

    @pl.when(step == steps - 1)
    def _():
        loss, merged_grad, short_grad, main_scale, extra_scale = heads_part(
            share,
            bit,
            total_ref[0, 0],
            first_ref[...],
            short_ref[...],
            scale_ref[1:3],
            readout_ref[...],
            trigram_ref[...],
            main_ref[...],
            triple_ref[...],
            table_sent,
            table_kept,
        )
        loss_ref[...] = loss
        first_out[...] = merged_grad
        gradient_ref[...] = short_grad
        scale_out[1:2] = main_scale
        scale_out[2:3] = extra_scale
        turned_gradient[...] = lowered(short_grad).T
        turned_normed[...] = normed_ref[...].T
        normed_grad[...] = jnp.zeros_like(normed_grad)

    def store(place, product):
        span = slice(place * width, (place + 1) * width)
        sent_ref[:, :, span], kept_ref[:, :, span] = halves(by_core(product, share), bit)

    @pl.when(step >= steps)
    def _():
        normed_grad[...] += feed_back_part(
            normed_ref[...],
            lowered(gradient_ref[...]),
            in_scratch[step - steps],
            down_scratch[step - steps],
            turned_gradient[...],
            turned_normed[...],
            store,
        )

    @pl.when(step == 2 * steps - 1)
    def _():
        hidden = hidden_ref[...]
        hidden_grad, scaling_grad = norm_back(
            hidden, norm_scale(hidden), scale_ref[0:1], normed_grad[...]
        )
        hidden_grad = hidden_grad + gradient_ref[...]
        hidden_low = lowered(hidden_grad)
        hidden_out[...] = hidden_grad
        low_out[...] = hidden_low
        scale_out[0:1] = scaling_grad[None]
        mixed_grad = lowered(times(hidden_low, project_ref[...], 1, 1))
        query_out[...] = attend_back(
            query_ref[...], key_ref, value_ref, share_ref, mixed_grad, key_out, value_out
        ).T
        rows, features = query_ref.shape
        for at, pair_out in enumerate(pair_outs):
            here = slice(at * rows, (at + 1) * rows)
            pair_out[:, :features], pair_out[:, features:] = key_out[here], value_out[here]


def upper_layer(
    numbers,
    mask_total,
    queries,
    pairs,
    pooled,
    first,
    scaling,
    weights,
    places,
    hidden_size,
    vocabulary,
    main_columns,
    triple_columns,
    share,
):
    shorts, features = pooled.shape
    rows = first.shape[0]
    members = len(pairs)
    entries = members * shorts
    steps = upper_steps
    width = hidden_size // steps
    chips = features // (2 * share)
    project_at, in_at, down_at, tables_at = places

    def whole(shape, at=(0, 0)):
        return pl.BlockSpec(shape, lambda j, numbers: at)

    def chunk(start):
        return pl.BlockSpec(
            (features, width),
            lambda j, numbers: (0, start // width + jnp.minimum(j, steps - 1)),
        )

    piece = pl.BlockSpec(
        (chips, share, 2 * width),
        lambda j, numbers: (0, 0, jnp.maximum(j - steps, 0)),
    )
    table_piece = pl.BlockSpec((chips, share, 4 * vocabulary), lambda j, numbers: (0, 0, 0))
    buffer = pltpu.HBM((chips, share, 2 * hidden_size), jnp.bfloat16)
    table_buffer = pltpu.HBM((chips, share, 4 * vocabulary), jnp.bfloat16)
    half = (entries, features)
    weights = in_hbm(weights)
    results = pl.pallas_call(
        functools.partial(upper_kernel, share, members),
        grid_spec=pltpu.PrefetchScalarGridSpec(
            num_scalar_prefetch=1,
            grid=(2 * steps,),
            in_specs=[
                pl.BlockSpec(memory_space=pltpu.SMEM),
                whole(queries.shape),
                *[whole(pair.shape) for pair in pairs],
                whole(pooled.shape),
                whole(first.shape),
                whole(scaling.shape),
                whole((features, features), (0, project_at // features)),
                chunk(in_at),
                chunk(down_at),
                whole((features, vocabulary), (0, tables_at // vocabulary + 3)),
                whole((features, 3 * vocabulary), (0, tables_at // (3 * vocabulary))),
                whole(main_columns.shape),
                whole(triple_columns.shape),
            ],
            out_specs=[
                whole((1, 1)),
                whole(first.shape),
                piece,
                piece,
                table_piece,
                table_piece,
                whole(pooled.shape),
                whole(pooled.shape),
                whole(pooled.shape),
                whole(pooled.shape),
                *[whole(pair.shape) for pair in pairs],
                whole(scaling.shape),
            ],
            scratch_shapes=[
                pltpu.VMEM(half, jnp.bfloat16),
                pltpu.VMEM(half, jnp.bfloat16),
                pltpu.VMEM(half, jnp.bfloat16),
                pltpu.VMEM(half, jnp.bfloat16),
                pltpu.VMEM((HEADS, entries, shorts), jnp.bfloat16),
                pltpu.VMEM((shorts, features), jnp.float32),
                pltpu.VMEM((shorts, features), jnp.bfloat16),
                pltpu.VMEM((shorts, features), jnp.float32),
                pltpu.VMEM((shorts, features), jnp.float32),
                pltpu.VMEM((features, shorts), jnp.bfloat16),
                pltpu.VMEM((features, shorts), jnp.bfloat16),
                pltpu.VMEM((shorts, features), jnp.float32),
                pltpu.VMEM((steps, features, width), jnp.bfloat16),
                pltpu.VMEM((steps, features, width), jnp.bfloat16),
            ],
        ),
        out_shape=[
            pltpu.HBM((1, 1), jnp.float32),
            pltpu.HBM((rows, features), jnp.float32),
            buffer,
            buffer,
            table_buffer,
            table_buffer,
            pltpu.HBM((shorts, features), jnp.bfloat16),
            pltpu.HBM((shorts, features), jnp.bfloat16),
            pltpu.HBM((shorts, features), jnp.float32),
            pltpu.HBM((shorts, features), jnp.bfloat16),
            *[pltpu.HBM(pair.shape, jnp.bfloat16) for pair in pairs],
            pltpu.HBM(scaling.shape, jnp.float32),
        ],
        compiler_params=pltpu.CompilerParams(vmem_limit_bytes=(40 if entries <= 512 else 60) * megabyte),
        cost_estimate=cost(
            14 * shorts * features * hidden_size + 6 * features * vocabulary * (rows + 3 * shorts),
            16 * features * hidden_size + 8 * rows * features,
            shorts * hidden_size,
        ),
    )(
        numbers,
        mask_total.reshape(1, 1),
        in_hbm(queries),
        *[in_hbm(pair) for pair in pairs],
        in_hbm(pooled),
        in_hbm(first),
        scaling,
        weights,
        weights,
        weights,
        weights,
        weights,
        main_columns,
        triple_columns,
    )
    return *results[:10], results[10:-1], results[-1]


def lower_kernel(
    share,
    bit_ref,
    grad_ref,
    came_ref,
    hidden_ref,
    gradient_ref,
    feed_scale_ref,
    project_ref,
    query_ref,
    key_ref,
    value_ref,
    share_ref,
    token_ref,
    mixed_ref,
    table_ref,
    attend_ref,
    scale_ref,
    attend_one_ref,
    upper_ref,
    sent_ref,
    kept_ref,
    key_out,
    value_out,
):
    bit = bit_ref[0]
    features = grad_ref.shape[1]
    is_token = token_ref[...]
    hidden = hidden_ref[...]
    hidden_grad, feed_scale = norm_back(
        hidden,
        norm_scale(hidden),
        feed_scale_ref[...],
        grad_ref[...] + came_ref[...].astype(jnp.float32),
    )
    hidden_low = lowered(hidden_grad + gradient_ref[...])
    mixed_grad = lowered(times(hidden_low, project_ref[...], 1, 1))
    query_grad = attend_back(
        query_ref[...], key_ref, value_ref, share_ref, mixed_grad, key_out, value_out
    )
    query_grad = lowered(times(query_grad, is_token).T)
    table = table_ref[...].astype(jnp.float32).T
    inverse = norm_scale(table)
    turned_normed = lowered((table * inverse * scale_ref[...]).T)
    parts = (query_grad, key_out[...], value_out[...])
    normed_grad = None
    for place, part in enumerate(parts):
        span = slice(place * features, (place + 1) * features)
        product = times(part, attend_ref[:, span], 1, 1)
        normed_grad = product if normed_grad is None else normed_grad + product
    table_grad, scaling_grad = norm_back(table, inverse, scale_ref[...], normed_grad)
    table_grad = table_grad + times(is_token, hidden_low, 0, 0)
    known = (scaling_grad[None], feed_scale[None], attend_one_ref[...], upper_ref[...])
    scale_rows = jnp.concatenate(
        [*known, jnp.zeros((lanes - 6, features), jnp.float32)], axis=0
    )
    products = (
        lambda: times(mixed_ref[...], hidden_low, 0, 0),
        *(lambda part=part: times(turned_normed, part) for part in parts),
        lambda: table_grad.T,
        lambda: scale_rows.T,
    )
    start = 0
    for product in products:
        product = product()
        span = slice(start, start + product.shape[1])
        sent_ref[:, :, span], kept_ref[:, :, span] = halves(by_core(product, share), bit)
        start += product.shape[1]


def lower_gradients(
    bit,
    grad,
    came,
    hidden,
    gradient,
    feed_scaling,
    project,
    queries,
    table_qkv,
    shares,
    is_token,
    mixed_low,
    embed_columns,
    attend,
    scaling,
    attend_one_scale,
    upper_scales,
    share,
):
    rows, features = hidden.shape
    entries = table_qkv.shape[0]
    chips = features // (2 * share)
    width = 4 * features + entries + lanes

    def whole(x, at=(0, 0)):
        return pl.BlockSpec(x.shape, lambda j, bit: (0,) * x.ndim)

    def third(at):
        return pl.BlockSpec((entries, features), lambda j, bit: (0, at))

    operands = [
        grad,
        came,
        hidden,
        gradient,
        feed_scaling,
        project,
        queries,
        table_qkv,
        table_qkv,
        shares,
        is_token,
        mixed_low,
        embed_columns,
        attend,
        scaling,
        attend_one_scale,
        upper_scales,
    ]
    specs = [whole(x) for x in operands]
    specs[7:9] = [third(1), third(2)]
    buffer = pltpu.HBM((chips, share, width), jnp.bfloat16)
    return pl.pallas_call(
        functools.partial(lower_kernel, share),
        grid_spec=pltpu.PrefetchScalarGridSpec(
            num_scalar_prefetch=1,
            grid=(1,),
            in_specs=specs,
            out_specs=[pl.BlockSpec((chips, share, width), lambda j, bit: (0, 0, 0))] * 2,
            scratch_shapes=[pltpu.VMEM((entries, features), jnp.bfloat16)] * 2,
        ),
        out_shape=[buffer, buffer],
        compiler_params=pltpu.CompilerParams(vmem_limit_bytes=36 * megabyte),
        cost_estimate=cost(1, 1),
    )(bit, *operands)


def adam_step(master, prior_first, prior_second, gradient, factor, rate, decay):
    clipped = gradient * factor
    moment = beta_first * prior_first + (1.0 - beta_first) * clipped
    variance = beta_second * prior_second + (1.0 - beta_second) * clipped * clipped
    ratio = (
        moment
        / (1.0 - beta_first**STEP)
        / (jnp.sqrt(variance / (1.0 - beta_second**STEP)) + adam_epsilon)
    )
    return (master - rate * (ratio + decay * master), moment, variance)


def adam_kernel(layout, group_count, total_ref, *refs):
    weights = len(layout)
    group_refs, refs = refs[:group_count], refs[group_count:]
    masters, firsts, seconds = (refs[k * weights : (k + 1) * weights] for k in range(3))
    loss_ref, norm_ref = refs[3 * weights : 3 * weights + 2]
    outs = refs[3 * weights + 2 :]
    share = total_ref.shape[0] - 8
    loss_ref[...] = total_ref[share : share + 1, 0:1]
    square_total = jnp.sum(
        jnp.sum(total_ref[0:share], axis=1, keepdims=True), axis=0, keepdims=True
    )
    norm_value = jnp.sqrt(square_total)
    norm_ref[...] = norm_value
    factor = clip_limit / jnp.maximum(norm_value, clip_limit)
    for place, layers in enumerate(layout):
        for at, pieces in enumerate(layers):
            for group, start, here, width in pieces:
                span = (slice(None), slice(here, here + width))
                span = (at, *span) if len(layers) > 1 else span
                new = adam_step(
                    masters[place][span],
                    firsts[place][span],
                    seconds[place][span],
                    group_refs[group][:, start : start + width],
                    factor,
                    learning_rates[place],
                    weight_decays[place],
                )
                for kind in range(3):
                    outs[kind * weights + place][span] = new[kind]


def adam_all(layout, totals, groups, masters, firsts, seconds):
    arrays = [*masters, *firsts, *seconds]
    shapes = [jax.ShapeDtypeStruct(array.shape, jnp.float32) for array in arrays]
    scalar = jax.ShapeDtypeStruct((1, 1), jnp.float32)
    moved = sum(8 * array.size for array in arrays)
    return pl.pallas_call(
        functools.partial(adam_kernel, layout, len(groups)),
        in_specs=whole_in_vmem(1 + len(groups) + len(arrays)),
        out_specs=whole_in_vmem(2 + len(arrays)),
        out_shape=[scalar, scalar, *shapes],
        compiler_params=pltpu.CompilerParams(vmem_limit_bytes=16 * megabyte),
        cost_estimate=cost(2 * moved, moved),
    )(totals, *groups, *arrays)


def pad_columns(array, width):
    return jnp.pad(array, ((0, 0), (0, width - array.shape[1])))


def local(
    tokens,
    next_targets,
    triple_targets,
    loss_mask,
    embedding,
    attention,
    projection,
    expansion,
    contraction,
    readout,
    trigram,
    scales,
    *moments,
):
    masters = (embedding, attention, projection, expansion, contraction, readout, trigram, scales)
    firsts = moments[:8]
    seconds = moments[8:]
    bits = index_bits()
    seq_size, dp_size = lax.axis_size("seq"), lax.axis_size("dp")
    devices = seq_size * dp_size
    held, piece = tokens.shape
    length = piece * seq_size
    sequences = held * dp_size
    members = devices // sequences
    vocabulary, share = embedding.shape
    features = share * devices
    hidden_size = expansion.shape[2]
    rows = length // members
    shorts = rows // 3
    member_bits = [("dp", b) for b in reversed(bits_of("dp")) if b < members]
    member = lax.axis_index("dp") % members
    group = (lax.axis_index("seq") * dp_size + lax.axis_index("dp")) // members

    integers = jnp.stack(
        [tokens, next_targets, triple_targets.reshape(held, piece), loss_mask]
    ).astype(jnp.bfloat16)
    integers = integers.reshape(share, -1)
    integer_width = integers.shape[1]
    integer_room = -(-integer_width // 128) * 128
    down_low = jnp.swapaxes(lowered(contraction), 1, 2)
    attention_low, projection_low, expansion_low = map(lowered, (attention, projection, expansion))
    stages = stages_of(bits)

    def packed(parts):
        return jnp.concatenate(parts, axis=1)[None]

    first_parts = [
        pad_columns(integers, integer_room),
        pad_columns(lowered(scales).T, 128),
        lowered(embedding).T,
        attention_low[0],
    ]
    second_parts = [projection_low[0], expansion_low[0], down_low[0]]
    third_parts = [
        attention_low[1],
        projection_low[1],
        expansion_low[1],
        down_low[1],
        lowered(trigram),
        lowered(readout),
    ]
    third = lax.all_gather(jnp.concatenate(third_parts, axis=1), ("seq", "dp"), axis=0, tiled=True)
    first, second = packed(first_parts), packed(second_parts)
    behind = None
    for stage in reversed(stages):
        first = stage_blocks(first, stage)
        if behind is not None:
            second = stage_blocks(second, behind)
            terms = together(*first, *second)
            first, second = terms[: len(first)], jnp.concatenate(terms[len(first) :])
        behind = stage
        if stage is not stages[0]:
            first, second = together(jnp.concatenate(first), second)
    first_other = [swapped(piece, bits[-1]) for piece in first]
    second = stage_blocks(second, behind)
    all_integers, scale_columns, embed_columns, attend_zero = merge_blocks(
        first, first_other, [part.shape[1] for part in first_parts], bits
    )
    project_one_at = 3 * features
    expand_one_at = 4 * features
    down_one_at = expand_one_at + hidden_size
    tables_at = down_one_at + hidden_size
    scale_rows = scale_columns[:, :6].astype(jnp.float32).T
    all_integers = all_integers[:, :integer_width].reshape(
        seq_size, dp_size, 4, held, piece
    )
    mask_total = jnp.sum(all_integers[:, :, 3].astype(jnp.float32))
    inverse_total = 1.0 / jnp.maximum(mask_total, 1.0)
    sequence = lax.dynamic_slice(
        all_integers,
        (0, group // held, 0, group % held, 0),
        (seq_size, 1, 4, 1, piece),
    )
    sequence = jnp.swapaxes(sequence.reshape(seq_size, 4, piece), 0, 1).reshape(4, length)
    own = lax.dynamic_slice_in_dim(sequence, member * rows, rows, 1).astype(jnp.int32)
    sequence_tokens = sequence[0].astype(jnp.int32)
    own_tokens = own[0]
    main_columns = own[1:4:2].T
    triple_columns = jnp.concatenate([own[2].reshape(shorts, 3), own[3].reshape(shorts, 3)], 1)

    letters = jnp.arange(vocabulary, dtype=jnp.int32)
    is_token = (own_tokens[:, None] == letters).astype(jnp.bfloat16)
    place = member * rows + jnp.arange(rows, dtype=jnp.int32)
    earlier = (jnp.arange(length, dtype=jnp.int32)[None, :] <= place[:, None]).astype(jnp.bfloat16)
    counts = contract(
        (sequence_tokens[:, None] == letters).astype(jnp.bfloat16), earlier, "tv,rt->vr"
    )
    table = embed_columns.astype(jnp.float32).T
    table_inverse = norm_scale(table)
    table_normed = lowered(table * table_inverse * scale_rows[0])
    table_qkv = lowered(contract(table_normed, attend_zero, "vd,dc->vc"))
    queries = lowered(contract(is_token, table_qkv[:, :features], "rv,vc->rc"))
    counts, main_columns, triple_columns, mask_total, scale_rows = together(
        counts, main_columns, triple_columns, mask_total, scale_rows
    )
    mixed_low, shares = weighted_attention(queries, table_qkv, counts)
    mixed_low, *second = together(mixed_low, *second)
    second_other = [swapped(piece, bits[-1]) for piece in second]
    project_zero, expand_zero, down_zero = merge_blocks(
        second, second_other, [part.shape[1] for part in second_parts], bits
    )
    first_stream, normed_zero, hidden = first_layer_end(
        is_token,
        embed_columns,
        mixed_low,
        project_zero,
        expand_zero,
        down_zero,
        scale_rows[1:2],
    )

    normed_other = swapped(normed_zero, bits[-1])

    along = [(i, i + 1) for i in range(dp_size - 1) if (i + 1) % members]
    back = [(i + 1, i) for i, _ in along]
    previous = lax.ppermute(first_stream[-2:], "dp", along)
    pooled, pooled_normed, short_queries, pairs = pooled_rows(
        first_stream, previous, third, scale_rows[2:3], shorts
    )
    pairs = stage_blocks(pairs, member_bits)
    (
        loss_local,
        merged_grad,
        *upper,
        table_sent,
        table_kept,
        short_mixed_low,
        short_hidden_low,
        short_hidden_grad,
        query_grad,
        pair_grads,
        upper_scales,
    ) = upper_layer(
        jnp.stack([own_bit(bits[-1]), member]),
        mask_total,
        short_queries,
        pairs,
        pooled,
        first_stream,
        scale_rows[3:6],
        third,
        (project_one_at, expand_one_at, down_one_at, tables_at),
        hidden_size,
        vocabulary,
        main_columns,
        triple_columns,
        share,
    )

    upper = [upper[1], swapped(upper[0], bits[-1])]
    tables = [table_kept, swapped(table_sent, bits[-1])]
    pair_grads = stage_sums(pair_grads, member_bits)
    terms = together(*pair_grads, *add_and_split([upper, tables], stages[0]))
    pair_grads, upper = terms[:members], stage_sums(terms[members:], stages[0])
    count = len(upper)
    *middle, rows_grad, rows_low, returned, attend_one_scale = middle_gradients(
        bits,
        query_grad,
        pair_grads,
        pooled_normed,
        short_mixed_low,
        short_hidden_low,
        pooled,
        short_hidden_grad,
        merged_grad,
        third,
        scale_rows[2:3],
        share,
    )

    rows_other = swapped(rows_low, bits[-1])
    after_next = [(i + 2, i) for i in range(dp_size - 2) if i % members < members - 2]
    if after_next:
        later = lax.ppermute(returned, "dp", after_next)
    else:
        later = jnp.zeros_like(returned)
    other_back = jnp.where(member % 2 == 1, returned, later)
    returned = lax.ppermute(returned, "dp", back)
    fed, grad, other_grad, gradient = feed_back(
        rows_grad,
        returned,
        rows_other,
        other_back,
        normed_zero,
        normed_other,
        expand_zero,
        down_zero,
        stages[0],
        own_bit(bits[-1]),
        share,
    )
    grad, other_grad, gradient, sent, kept, *terms = together(
        grad, other_grad, gradient, *middle, *fed, *upper
    )
    fed, upper = stage_sums(terms[:count], stages[0]), terms[count:]
    middle = [kept, swapped(sent, bits[-1])]
    came = swapped(other_grad, bits[-1])
    came, *upper = together(came, *add_and_split([upper], stages[1]))
    upper = stage_sums(upper, stages[1])
    lower = lower_gradients(
        own_bit(bits[-1]).reshape(1),
        grad,
        came,
        hidden,
        gradient,
        scale_rows[1:2],
        project_zero,
        queries,
        table_qkv,
        shares,
        is_token,
        mixed_low,
        embed_columns,
        attend_zero,
        scale_rows[0:1],
        attend_one_scale,
        upper_scales,
        share,
    )

    sent, kept, *terms = together(*lower, *fed, *upper)
    fed, upper = terms[:count], terms[count:]
    lower = [kept, swapped(sent, bits[-1])]
    fed = add_and_split([fed], stages[1])
    terms = together(*lower, *middle, *fed)
    lower, middle, fed = terms[:2], terms[2:4], terms[4:]
    lower = add_and_split([lower, middle], stages[0])
    fed, lower = stage_sums(fed, stages[1]), stage_sums(lower, stages[0])
    terms = together(*fed, *lower)
    fed, lower = terms[: len(fed)], add_and_split([terms[len(fed) :]], stages[1])
    lower = stage_sums(lower, stages[1])
    for stage in stages[2:]:
        upper, fed, lower = (
            stage_sums(add_and_split([terms], stage), stage) for terms in (upper, fed, lower)
        )
    sums, squares = [], []
    for terms in (upper, fed, lower):
        total, square = add_and_square(terms)
        sums.append(total)
        squares.append(square)
    bit = own_bit(bits[-1])
    mine = lax.dynamic_slice_in_dim(sums[1], bit * share, share, 0)
    others = lax.dynamic_slice_in_dim(sums[1], (1 - bit) * share, share, 0)
    came = swapped(others, bits[-1])
    sums[1] = jnp.where(
        bit == 0,
        jnp.concatenate([mine, came], axis=1),
        jnp.concatenate([came, mine], axis=1),
    )
    squares[1] = squares[1][:share] + squares[1][share:]
    totals = jnp.concatenate(
        [sum(squares), jnp.broadcast_to(loss_local, (8, lanes))], axis=0
    )
    for stage in [[bits[-1]], *stages]:
        totals = sum(stage_sums([totals] * (1 << len(stage)), stage))
    def fed_at(group, kind, steps):
        width = hidden_size // steps
        return [(group, (2 * j + kind) * width, j * width, width) for j in range(steps)]

    tables_at = 2 * hidden_size
    beyond = 4 * features + vocabulary + lanes
    scale_at = (2, 4 * features + vocabulary)
    scale_sum = sums[scale_at[0]][:, scale_at[1] : scale_at[1] + 6].T
    layout = (
        ([(2, 4 * features, 0, vocabulary)],),
        (
            [(2, features, 0, 3 * features)],
            [(2, beyond, 0, 3 * features)],
        ),
        ([(2, 0, 0, features)], [(2, beyond + 3 * features, 0, features)]),
        (fed_at(1, 1, 2 * feed_steps), fed_at(0, 1, upper_steps)),
        (fed_at(1, 0, 2 * feed_steps), fed_at(0, 0, upper_steps)),
        ([(0, tables_at, 0, vocabulary)],),
        ([(0, tables_at + vocabulary, 0, 3 * vocabulary)],),
        ([(3, 0, 0, share)],),
    )

    def turned(arrays):
        embed, attend, project, expand, down, *rest = arrays
        return (embed.T, attend, project, expand, jnp.swapaxes(down, 1, 2), *rest)

    late = lax.optimization_barrier(
        (turned(masters), turned(firsts), turned(seconds), lower[0])
    )
    loss_total, norm_value, *results = adam_all(
        layout, totals, [*sums, scale_sum], *late[:3]
    )
    return (
        loss_total.reshape(()),
        mask_total,
        norm_value.reshape(()),
        *turned(results[:8]),
        *turned(results[8:16]),
        *turned(results[16:]),
    )


def solution(mesh):
    weight_specs = (
        P(None, ("seq", "dp")),
        P(None, ("seq", "dp"), None),
        P(None, ("seq", "dp"), None),
        P(None, ("seq", "dp"), None),
        P(None, None, ("seq", "dp")),
        P(("seq", "dp"), None),
        P(("seq", "dp"), None),
        P(None, ("seq", "dp")),
    )
    in_specs = (
        P("dp", "seq"),
        P("dp", "seq"),
        P("dp", "seq", None),
        P("dp", "seq"),
    ) + weight_specs * 3
    out_specs = (P(), P(), P()) + weight_specs * 3
    return jax.shard_map(local, mesh=mesh, in_specs=in_specs, out_specs=out_specs, check_vma=False)
```

```python
import functools

import jax
import jax.numpy as jnp
from jax import lax
from jax.experimental import pallas as pl
from jax.experimental.pallas import tpu as pltpu
from jax.sharding import PartitionSpec as P

HEADS = 8
STEP = 10


norm_epsilon = 1e-06
trigram_share = 0.5
clip_limit = 0.1
beta_first = 0.9
beta_second = 0.95
adam_epsilon = 1e-08
learning_rates = (0.6, 0.05, 0.2, 0.05, 0.03, 0.05, 0.05, 0.6)
weight_decays = (0.0, 0.1, 0.1, 0.1, 0.1, 0.1, 0.1, 0.0)
exact_precision = lax.Precision.HIGHEST
megabyte = 1024 * 1024
lanes = 128


def lowered(array):
    return array.astype(jnp.bfloat16)


def contract(left, right, form):
    return jnp.einsum(form, left, right, preferred_element_type=jnp.float32)


def exactly(left, right, form):
    return jnp.einsum(
        form, left, right, preferred_element_type=jnp.float32, precision=exact_precision
    )


def bits_of(axis):
    return [1 << k for k in range((lax.axis_size(axis) - 1).bit_length())]


def index_bits():
    return [("seq", b) for b in reversed(bits_of("seq"))] + [
        ("dp", b) for b in reversed(bits_of("dp"))
    ]


def own_bit(step):
    axis, weight = step
    return (lax.axis_index(axis) // weight) % 2


def swapped(x, step):
    axis, weight = step
    return lax.ppermute(x, axis, [(i, i ^ weight) for i in range(lax.axis_size(axis))])


def stages_of(bits):
    rest = bits[:-1]
    return [rest[max(0, end - 2) : end] for end in range(len(rest), 0, -2)]


def exchanged(x, steps):
    masks = {"seq": 0, "dp": 0}
    for axis, weight in steps:
        masks[axis] |= weight
    if not masks["seq"]:
        pairs = [(i, i ^ masks["dp"]) for i in range(lax.axis_size("dp"))]
        return lax.ppermute(x, "dp", pairs)
    if not masks["dp"]:
        pairs = [(i, i ^ masks["seq"]) for i in range(lax.axis_size("seq"))]
        return lax.ppermute(x, "seq", pairs)
    width = lax.axis_size("dp")
    pairs = [
        (i * width + j, (i ^ masks["seq"]) * width + (j ^ masks["dp"]))
        for i in range(lax.axis_size("seq"))
        for j in range(width)
    ]
    return lax.ppermute(x, ("seq", "dp"), pairs)


def chosen_steps(stage, number):
    return [step for at, step in enumerate(stage) if number >> (len(stage) - 1 - at) & 1]


def own_number(stage):
    number = jnp.int32(0)
    for step in stage:
        number = 2 * number + own_bit(step)
    return number


def stage_blocks(x, stage):
    return [x] + [exchanged(x, chosen_steps(stage, m)) for m in range(1, 1 << len(stage))]


def stage_gather(x, stage):
    return jnp.concatenate(stage_blocks(x, stage))


def merge_kernel(widths, pieces, number_ref, *refs):
    mine, others, outs = refs[:pieces], refs[pieces : 2 * pieces], refs[2 * pieces :]
    bit, number = number_ref[0], number_ref[1]
    for piece in range(pieces):
        start = 0
        at = pl.ds(number ^ piece, 1)
        for width, out in zip(widths, outs):
            span = slice(start, start + width)
            out[at, pl.ds(bit, 1)] = mine[piece][:, :, span][None]
            out[at, pl.ds(1 - bit, 1)] = others[piece][:, :, span][None]
            start += width


def merge_blocks(mine, others, widths, bits):
    blocks, share, width = mine[0].shape
    pieces = len(mine)
    stages = stages_of(bits)
    block = jnp.arange(blocks, dtype=jnp.int32)
    place = jnp.zeros((blocks,), jnp.int32)
    low = 0
    for stage in stages[1:]:
        high = len(bits) - 1 - len(stages[0]) - low - len(stage)
        number = (block >> high) % (1 << len(stage)) ^ own_number(stage)
        place = place + (number << low)
        low += len(stage)
    numbers = jnp.concatenate(
        [jnp.stack([own_bit(bits[-1]), own_number(stages[0])]), place]
    )
    taken = pl.BlockSpec((1, share, width), lambda i, numbers: (i, 0, 0))
    outs = pl.pallas_call(
        functools.partial(merge_kernel, widths, pieces),
        grid_spec=pltpu.PrefetchScalarGridSpec(
            num_scalar_prefetch=1,
            grid=(blocks,),
            in_specs=[taken] * (2 * pieces),
            out_specs=[
                pl.BlockSpec(
                    (pieces, 2, share, w), lambda i, numbers: (numbers[2 + i], 0, 0, 0)
                )
                for w in widths
            ],
        ),
        out_shape=[
            pltpu.HBM((pieces * blocks, 2, share, w), mine[0].dtype) for w in widths
        ],
        compiler_params=pltpu.CompilerParams(vmem_limit_bytes=12 * megabyte),
        cost_estimate=cost(0, 8 * pieces * blocks * share * width),
    )(numbers, *[in_hbm(x) for x in mine], *others)
    return [out.reshape(2 * pieces * blocks * share, out.shape[-1]) for out in outs]


def together(*arrays):
    return lax.optimization_barrier(arrays)


def whole_in_vmem(count):
    return [pl.BlockSpec(memory_space=pltpu.VMEM)] * count


def in_hbm(array):
    return pltpu.with_memory_space_constraint(array, pltpu.HBM)


def cost(flops, moved, exponentials=0):
    return pl.CostEstimate(
        flops=int(flops), bytes_accessed=int(moved), transcendentals=int(exponentials)
    )


def halves(product, bit):
    low, high = product[:, 0], product[:, 1]
    return jnp.where(bit == 0, high, low), jnp.where(bit == 0, low, high)


def by_core(product, share):
    return lowered(product).reshape(-1, 2, share, product.shape[-1])


def split_kernel(widths, summands, pieces, number_ref, *refs):
    sources, outs = refs[: len(widths) * summands], refs[len(widths) * summands :]
    number = number_ref[0]
    start = 0
    for at, width in enumerate(widths):
        terms = sources[at * summands : (at + 1) * summands]
        for m in range(pieces):
            place = pl.ds(number ^ m, 1)
            total = terms[0][:, place].astype(jnp.float32)
            for term in terms[1:]:
                total = total + term[:, place].astype(jnp.float32)
            outs[m][:, :, start : start + width] = lowered(total)[:, 0]
        start += width


def add_and_split(sources, stage):
    blocks, share, _ = sources[0][0].shape
    pieces = 1 << len(stage)
    widths = [terms[0].shape[-1] for terms in sources]
    total = sum(widths)
    arrays = [
        place(term.reshape(blocks // pieces, pieces, share, term.shape[-1]))
        for terms in sources
        for place, term in zip(
            [in_hbm] + [in_hbm if len(sources) > 2 else lambda x: x] * len(terms), terms
        )
    ]
    return pl.pallas_call(
        functools.partial(split_kernel, widths, len(sources[0]), pieces),
        grid_spec=pltpu.PrefetchScalarGridSpec(
            num_scalar_prefetch=1,
            grid=(blocks // pieces,),
            in_specs=[
                pl.BlockSpec((1, *x.shape[1:]), lambda i, number: (i, 0, 0, 0)) for x in arrays
            ],
            out_specs=[pl.BlockSpec((1, share, total), lambda i, number: (i, 0, 0))] * pieces,
        ),
        out_shape=[pltpu.HBM((blocks // pieces, share, total), jnp.bfloat16)] * pieces,
        compiler_params=pltpu.CompilerParams(vmem_limit_bytes=16 * megabyte),
        cost_estimate=cost(1, 1),
    )(own_number(stage).reshape(1), *arrays)


def add_and_square_kernel(earlier, terms_count, steps, both, bit_ref, loss_ref, *refs):
    befores, refs = refs[:earlier], refs[earlier:]
    terms, outs = refs[:terms_count], list(refs[terms_count:])
    total = terms[0][...].astype(jnp.float32)
    for term in terms[1:]:
        total = total + term[...].astype(jnp.float32)
    if total.shape[1] > both:
        outs.pop(0)[...] = total[:, both:]
    if both:
        mine_ref, other_ref = outs[:2]
        width = both // (2 * steps)
        for step in range(steps):
            here = slice(step * width, (step + 1) * width)
            first = total[:, 2 * step * width : (2 * step + 1) * width]
            second = total[:, (2 * step + 1) * width : (2 * step + 2) * width]
            mine_ref[:, here] = jnp.where(bit_ref[0, 0] == 0, first, second)
            other_ref[:, here] = jnp.where(bit_ref[0, 0] == 0, second, first)
    square_ref = outs[-1]
    share = total.shape[0]
    squares = jnp.zeros((share, lanes), jnp.float32)
    for before in befores:
        squares = squares + before[0:share]
    for start in range(0, total.shape[1], lanes):
        piece = total[:, start : start + lanes]
        squares = squares + piece * piece
    square_ref[0:share] = squares
    square_ref[share:] = jnp.broadcast_to(loss_ref[...], (8, lanes))


def add_and_square(bit, loss, befores, terms, steps, both):
    share, width = terms[0].shape[-2:]
    shapes = [(share, width - both)] if width > both else []
    shapes += [(share, both // 2)] * 2 if both else []
    shapes += [(share + 8, lanes)]
    return pl.pallas_call(
        functools.partial(
            add_and_square_kernel, len(befores), len(terms), steps, both
        ),
        in_specs=[pl.BlockSpec(memory_space=pltpu.SMEM)]
        + whole_in_vmem(1 + len(befores) + len(terms)),
        out_specs=whole_in_vmem(len(shapes)),
        out_shape=[jax.ShapeDtypeStruct(shape, jnp.float32) for shape in shapes],
        compiler_params=pltpu.CompilerParams(vmem_limit_bytes=8 * megabyte),
        cost_estimate=cost(3 * share * width, 12 * share * width),
    )(bit.reshape(1, 1), loss, *befores, *[term.reshape(share, width) for term in terms])


def stage_sums(pieces, stage):
    return [pieces[0]] + [
        exchanged(pieces[m], chosen_steps(stage, m)) for m in range(1, 1 << len(stage))
    ]


def norm_scale(stream):
    return lax.rsqrt(jnp.mean(stream * stream, axis=-1, keepdims=True) + norm_epsilon)


def norm_back(stream, inverse, scaling, gradient):
    unit = stream * inverse
    scaled = gradient * scaling
    scaling_grad = jnp.sum(gradient * unit, axis=0)
    stream_grad = inverse * (scaled - unit * jnp.mean(scaled * unit, axis=-1, keepdims=True))
    return stream_grad, scaling_grad


def times(left, right, left_side=1, right_side=0):
    return lax.dot_general(
        left, right, (((left_side,), (right_side,)), ((), ())), preferred_element_type=jnp.float32
    )


def exact_times(left, right, left_side=1, right_side=0):
    return lax.dot_general(
        left,
        right,
        (((left_side,), (right_side,)), ((), ())),
        preferred_element_type=jnp.float32,
        precision=exact_precision,
    )


def head_groups(features):
    depth = features // HEADS
    together = max(1, lanes // depth)
    return depth, [
        (first * depth, together * depth, range(first, first + together))
        for first in range(0, HEADS, together)
    ]


def own_lanes(width, depth, at):
    lane = lax.broadcasted_iota(jnp.int32, (1, width), 1)
    return (lane >= at * depth) & (lane < (at + 1) * depth)


def attend(queries, key_ref, value_ref, counts, share_ref):
    features = queries.shape[1]
    depth, groups = head_groups(features)
    queries = queries * jnp.asarray(depth ** (-0.5), queries.dtype)
    turned_values = value_ref[...].T
    mixed = []
    for start, width, places in groups:
        span = slice(start, start + width)
        keys = key_ref[:, span]
        for at, place in enumerate(places):
            own = own_lanes(width, depth, at)
            scores = times(jnp.where(own, keys, jnp.zeros_like(keys)), queries[:, span], 1, 1)
            scores = jnp.where(counts > 0.0, scores, -1e30)
            exponent = counts * jnp.exp(scores - jnp.max(scores, axis=0, keepdims=True))
            shares = lowered(exponent * (1.0 / jnp.sum(exponent, axis=0, keepdims=True)))
            share_ref[place] = shares
            here = slice(start + at * depth, start + (at + 1) * depth)
            mixed.append(lowered(times(turned_values[here], shares)))
    return jnp.concatenate(mixed, axis=0)


def attend_back(queries, key_ref, value_ref, share_ref, gradient, key_out, value_out):
    features = queries.shape[1]
    depth, groups = head_groups(features)
    scaled = depth ** (-0.5)
    turned_keys = key_ref[...].T
    query_grads = []
    for start, width, places in groups:
        span = slice(start, start + width)
        values = value_ref[:, span]
        key_sum = value_sum = None
        for at, place in enumerate(places):
            own = own_lanes(width, depth, at)
            low = share_ref[place]
            shares = low.astype(jnp.float32)
            share_grad = times(
                jnp.where(own, values, jnp.zeros_like(values)), gradient[:, span], 1, 1
            )
            dots = jnp.sum(shares * share_grad, axis=0, keepdims=True)
            score_grad = lowered(shares * (share_grad - dots))
            here = slice(start + at * depth, start + (at + 1) * depth)
            query_grads.append(lowered(times(turned_keys[here], score_grad) * scaled))
            key_part = times(score_grad, queries[:, span])
            value_part = times(low, gradient[:, span])
            if key_sum is None:
                key_sum, value_sum = key_part, value_part
            else:
                key_sum = jnp.where(own, key_part, key_sum)
                value_sum = jnp.where(own, value_part, value_sum)
        key_out[:, span] = lowered(key_sum * scaled)
        value_out[:, span] = lowered(value_sum)
    return jnp.concatenate(query_grads, axis=0)


def attend_kernel(query_ref, key_ref, value_ref, count_ref, mixed_ref, share_ref):
    mixed_ref[...] = attend(
        query_ref[...], key_ref, value_ref, count_ref[...], share_ref
    ).T


def weighted_attention(queries, table_qkv, counts):
    rows, features = queries.shape
    entries = table_qkv.shape[0]
    return pl.pallas_call(
        attend_kernel,
        grid=(1,),
        in_specs=[
            pl.BlockSpec((rows, features), lambda i: (0, 0)),
            pl.BlockSpec((entries, features), lambda i: (0, 1)),
            pl.BlockSpec((entries, features), lambda i: (0, 2)),
            pl.BlockSpec((entries, rows), lambda i: (0, 0)),
        ],
        out_specs=[
            pl.BlockSpec((rows, features), lambda i: (0, 0)),
            pl.BlockSpec((HEADS, entries, rows), lambda i: (0, 0, 0)),
        ],
        out_shape=[
            jax.ShapeDtypeStruct((rows, features), jnp.bfloat16),
            pltpu.HBM((HEADS, entries, rows), jnp.bfloat16),
        ],
        compiler_params=pltpu.CompilerParams(vmem_limit_bytes=24 * megabyte),
        cost_estimate=cost(
            4 * rows * entries * features,
            4 * rows * features + 4 * entries * features + (2 * HEADS + 4) * rows * entries,
            HEADS * rows * entries,
        ),
    )(queries, table_qkv, table_qkv, counts)


gelu_rate = 0.7978845608
gelu_cube = 0.044715


feed_steps = 2
feed_parts = 2
upper_steps = 2


def gelu_terms(before):
    square = before * before
    bent = jnp.tanh(before * (gelu_rate + gelu_rate * gelu_cube * square))
    half = 0.5 + 0.5 * bent
    return square, bent, half


def feed_forward_part(normed, in_ref, down_ref):
    width = in_ref.shape[1] // feed_parts
    total = None
    for part in range(feed_parts):
        span = slice(part * width, (part + 1) * width)
        before = times(normed, in_ref[:, span])
        _, _, half = gelu_terms(before)
        product = times(lowered(before * half), down_ref[:, span], 1, 1)
        total = product if total is None else total + product
    return total


def feed_forward_kernel(
    token_ref,
    embed_ref,
    mixed_ref,
    project_ref,
    in_ref,
    down_ref,
    scale_ref,
    result_ref,
    normed_ref,
    hidden_ref,
    last_ref,
):
    @pl.when(pl.program_id(0) == 0)
    def _():
        hidden = times(token_ref[...], embed_ref[...], 1, 1) + times(
            mixed_ref[...], project_ref[...]
        )
        hidden_ref[...] = hidden
        normed_ref[...] = lowered(hidden * norm_scale(hidden) * scale_ref[...])
        result_ref[...] = hidden

    result_ref[...] += feed_forward_part(normed_ref[...], in_ref, down_ref)
    last_ref[...] = result_ref[result_ref.shape[0] - last_ref.shape[0] :]


def first_layer_end(is_token, embed_columns, mixed_low, project, in_weight, down_weight, scaling):
    rows, features = mixed_low.shape
    hidden_size = in_weight.shape[1]
    width = hidden_size // feed_steps

    def whole(shape):
        return pl.BlockSpec(shape, lambda j: (0, 0))

    chunk = pl.BlockSpec((features, width), lambda j: (0, j))
    return pl.pallas_call(
        feed_forward_kernel,
        grid=(feed_steps,),
        in_specs=[
            whole(is_token.shape),
            whole(embed_columns.shape),
            whole(mixed_low.shape),
            whole(project.shape),
            chunk,
            chunk,
            whole(scaling.shape),
        ],
        out_specs=[whole((rows, features))] * 3 + [whole((8, features))],
        out_shape=[
            pltpu.HBM((rows, features), jnp.float32),
            pltpu.HBM((rows, features), jnp.bfloat16),
            pltpu.HBM((rows, features), jnp.float32),
            jax.ShapeDtypeStruct((8, features), jnp.float32),
        ],
        compiler_params=pltpu.CompilerParams(vmem_limit_bytes=20 * megabyte),
        cost_estimate=cost(
            4 * rows * features * hidden_size,
            4 * features * hidden_size + 14 * rows * features,
            rows * hidden_size,
        ),
    )(
        in_hbm(is_token),
        in_hbm(embed_columns),
        mixed_low,
        in_hbm(project),
        in_hbm(in_weight),
        in_hbm(down_weight),
        scaling,
    )


def pool_kernel(
    first_ref, last_ref, attend_ref, scale_ref, pooled_ref, normed_ref, query_ref, pair_ref
):
    rows, shorts = first_ref.shape[0], pooled_ref.shape[0]
    gap = (
        lax.broadcasted_iota(jnp.int32, (shorts, rows), 1)
        + 2
        - 3 * lax.broadcasted_iota(jnp.int32, (shorts, rows), 0)
    )
    pooling = jnp.where((gap >= 0) & (gap < 3), 1.0, 0.0)
    pooled = exact_times(pooling, first_ref[...])
    row = lax.broadcasted_iota(jnp.int32, (shorts, 1), 0)
    pooled = (
        pooled + jnp.where(row == 0, jnp.sum(last_ref[6:8], axis=0, keepdims=True), 0.0)
    ) * (1.0 / 3.0)
    pooled_ref[...] = pooled
    normed = lowered(pooled * norm_scale(pooled) * scale_ref[...])
    normed_ref[...] = normed
    features = first_ref.shape[1]
    query_ref[...] = lowered(times(normed, attend_ref[:, :features]))
    pair_ref[...] = lowered(times(normed, attend_ref[:, features:]))


def pooled_rows(first, previous, weights, scaling, shorts):
    rows, features = first.shape

    def whole(shape):
        return pl.BlockSpec(shape, lambda j: (0, 0))

    return pl.pallas_call(
        pool_kernel,
        grid=(1,),
        in_specs=[
            whole(first.shape),
            whole(previous.shape),
            whole((features, 3 * features)),
            whole(scaling.shape),
        ],
        out_specs=[
            whole((shorts, features)),
            whole((shorts, features)),
            whole((shorts, features)),
            whole((shorts, 2 * features)),
        ],
        out_shape=[
            pltpu.HBM((shorts, features), jnp.float32),
            pltpu.HBM((shorts, features), jnp.bfloat16),
            pltpu.HBM((shorts, features), jnp.bfloat16),
            jax.ShapeDtypeStruct((shorts, 2 * features), jnp.bfloat16),
        ],
        compiler_params=pltpu.CompilerParams(vmem_limit_bytes=12 * megabyte),
        cost_estimate=cost(
            6 * shorts * features * features + 12 * rows * shorts * features,
            6 * features * features + 4 * rows * features,
        ),
    )(in_hbm(first), previous, in_hbm(weights), scaling)


def feed_back_part(normed, gradient, in_weight, down_weight, turned_gradient, turned_normed, store):
    before = times(normed, in_weight)
    square, bent, half = gelu_terms(before)
    slope = half + half * (1.0 - bent) * before * (
        gelu_rate + 3.0 * gelu_rate * gelu_cube * square
    )
    before_grad = lowered(times(gradient, down_weight) * slope)
    store(0, times(turned_gradient, lowered(before * half)))
    store(1, times(turned_normed, before_grad))
    return times(before_grad, in_weight, 1, 1)


def feed_back_kernel(share, pieces, number_ref, *refs):
    (
        above_ref,
        back_ref,
        other_back_ref,
        normed_ref,
        other_normed_ref,
        in_ref,
        down_ref,
        *outs,
        grad_out,
        other_grad_out,
        gradient_out,
        gradient_ref,
        all_normed,
        turned_gradient,
        turned_normed,
        normed_grad,
        product_ref,
    ) = refs
    other_gradients, outs = outs[:-pieces], outs[-pieces:]
    step = pl.program_id(0)
    number = number_ref[1]
    rows = above_ref.shape[0]

    @pl.when(step == 0)
    def _():
        row = lax.broadcasted_iota(jnp.int32, (rows, 1), 0)
        gradient = above_ref[...] + jnp.where(row >= rows - 2, back_ref[0:1], 0.0)
        gradient_out[...] = gradient
        gradient_ref[:rows] = lowered(gradient)
        start = 0
        for other in other_gradients:
            span = slice(start, start + other.shape[1])
            gradient_ref[rows:, span] = lowered(
                other[...].astype(jnp.float32)
                + jnp.where(row >= rows - 2, other_back_ref[0:1, span], 0.0)
            )
            start += other.shape[1]
        all_normed[:rows] = normed_ref[...]
        all_normed[rows:] = other_normed_ref[...]
        turned_gradient[...] = gradient_ref[...].T
        turned_normed[...] = all_normed[...].T
        normed_grad[...] = jnp.zeros_like(normed_grad)

    width = in_ref.shape[1]

    def store(place, product):
        product_ref[...] = lowered(product).reshape(product_ref.shape)
        for core in range(2):
            span = slice((2 * core + place) * width, (2 * core + place + 1) * width)
            for m in range(pieces):
                outs[m][:, :, span] = product_ref[:, pl.ds(number ^ m, 1), core][:, 0]

    normed_grad[...] += feed_back_part(
        all_normed[...],
        gradient_ref[...],
        in_ref[...],
        down_ref[...],
        turned_gradient[...],
        turned_normed[...],
        store,
    )

    @pl.when(step == pl.num_programs(0) - 1)
    def _():
        grad_out[...] = normed_grad[:rows]
        other_grad_out[...] = lowered(normed_grad[rows:])


def feed_back(
    above,
    back,
    other_gradients,
    other_back,
    normed,
    other_normed,
    in_weight,
    down_weight,
    hidden_size,
    steps,
    stage,
    bit,
    share,
):
    rows, features = above.shape
    width = hidden_size // (2 * steps)
    blocks = features // (2 * share)
    pieces = 1 << len(stage)
    far = blocks // pieces

    def whole(shape):
        return pl.BlockSpec(shape, lambda j, numbers: (0, 0))

    def chunk(start):
        return pl.BlockSpec(
            (features, width), lambda j, numbers: (0, start // width + numbers[0] * steps + j)
        )

    piece = pl.BlockSpec((far, share, 4 * width), lambda j, numbers: (0, 0, j))
    *results, grad, other_grad, gradient = pl.pallas_call(
        functools.partial(feed_back_kernel, share, pieces),
        grid_spec=pltpu.PrefetchScalarGridSpec(
            num_scalar_prefetch=1,
            grid=(steps,),
            in_specs=[
                whole(above.shape),
                whole(back.shape),
                whole(back.shape),
                whole(normed.shape),
                whole(normed.shape),
                chunk(in_weight[1]),
                chunk(down_weight[1]),
                *[whole(x.shape) for x in other_gradients],
            ],
            out_specs=[piece] * pieces + [whole(above.shape)] * 3,
            scratch_shapes=[
                pltpu.VMEM((2 * rows, features), jnp.bfloat16),
                pltpu.VMEM((2 * rows, features), jnp.bfloat16),
                pltpu.VMEM((features, 2 * rows), jnp.bfloat16),
                pltpu.VMEM((features, 2 * rows), jnp.bfloat16),
                pltpu.VMEM((2 * rows, features), jnp.float32),
                pltpu.VMEM((far, pieces, 2, share, width), jnp.bfloat16),
            ],
        ),
        out_shape=[pltpu.HBM((far, share, 2 * hidden_size), jnp.bfloat16)] * pieces
        + [
            jax.ShapeDtypeStruct(above.shape, jnp.float32),
            jax.ShapeDtypeStruct(above.shape, jnp.bfloat16),
            pltpu.HBM(above.shape, jnp.float32),
        ],
        compiler_params=pltpu.CompilerParams(vmem_limit_bytes=36 * megabyte),
        cost_estimate=cost(1, 1),
    )(
        jnp.stack([bit, own_number(stage)]),
        in_hbm(above),
        back,
        other_back,
        in_hbm(normed),
        other_normed,
        in_hbm(in_weight[0]),
        in_hbm(down_weight[0]),
        *other_gradients,
    )
    return results, grad, other_grad, gradient


def middle_kernel(
    share,
    members,
    bit_ref,
    query_ref,
    *refs,
):
    pair_refs, refs = refs[:members], refs[members:]
    (
        normed_ref,
        mixed_ref,
        low_ref,
        pooled_ref,
        hidden_grad_ref,
        above_ref,
        attend_ref,
        scale_ref,
        *outs,
        rows_out,
        left_out,
        right_out,
        back_out,
        scale_out,
    ) = refs
    sent_refs, kept_refs = outs[: len(outs) // 2], outs[len(outs) // 2 :]
    bit = bit_ref[0]
    features = query_ref.shape[1]
    pairs = pair_refs[0][...].astype(jnp.float32)
    for pair_ref in pair_refs[1:]:
        pairs = pairs + pair_ref[...].astype(jnp.float32)
    pairs = lowered(pairs)
    queries = query_ref[...]
    normed_grad = times(queries, attend_ref[:, :features], 1, 1) + times(
        pairs, attend_ref[:, features:], 1, 1
    )
    pooled = pooled_ref[...]
    pooled_grad, scaling_grad = norm_back(
        pooled, norm_scale(pooled), scale_ref[...], normed_grad
    )
    scale_out[...] = scaling_grad[None]
    pooled_grad = (pooled_grad + hidden_grad_ref[...]) * (1.0 / 3.0)
    back_out[...] = pooled_grad[0 : back_out.shape[0]]
    rows, shorts = rows_out.shape[0], pooled.shape[0]
    gap = (
        lax.broadcasted_iota(jnp.int32, (rows, shorts), 0)
        + 2
        - 3 * lax.broadcasted_iota(jnp.int32, (rows, shorts), 1)
    )
    spreading = jnp.where((gap >= 0) & (gap < 3), 1.0, 0.0)
    rows_grad = above_ref[...] + exact_times(spreading, pooled_grad)
    rows_out[...] = rows_grad
    left_out[...] = lowered(rows_grad[:, : features // 2])
    right_out[...] = lowered(rows_grad[:, features // 2 :])
    turned_normed = normed_ref[...].T
    products = (
        lambda: times(turned_normed, queries),
        lambda: times(turned_normed, pairs[:, :features]),
        lambda: times(turned_normed, pairs[:, features:]),
        lambda: times(mixed_ref[...], low_ref[...], 0, 0),
    )
    for product, sent_ref, kept_ref in zip(products, sent_refs, kept_refs):
        sent_ref[...], kept_ref[...] = halves(by_core(product(), share), bit)


def middle_gradients(
    bits,
    query_grad,
    pair_grads,
    normed,
    mixed_low,
    hidden_low,
    pooled,
    hidden_grad,
    above,
    weights,
    scaling,
    share,
):
    shorts, features = pooled.shape
    rows = above.shape[0]
    chips = features // (2 * share)

    def whole(shape):
        return pl.BlockSpec(shape, lambda j, bit: (0, 0))

    operands = [
        in_hbm(query_grad),
        in_hbm(pair_grads[0]),
        *pair_grads[1:],
        *[
            in_hbm(x)
            for x in (
                normed,
                mixed_low,
                hidden_low,
                pooled,
                hidden_grad,
                above,
                weights,
                scaling,
            )
        ],
    ]
    specs = [whole(x.shape) for x in operands]
    specs[-2] = whole((features, 3 * features))
    buffer = pltpu.HBM((chips, share, features), jnp.bfloat16)
    piece = pl.BlockSpec((chips, share, features), lambda j, bit: (0, 0, 0))
    half = (rows, features // 2)
    return pl.pallas_call(
        functools.partial(middle_kernel, share, len(pair_grads)),
        grid_spec=pltpu.PrefetchScalarGridSpec(
            num_scalar_prefetch=1,
            grid=(1,),
            in_specs=specs,
            out_specs=[
                *[piece] * 8,
                whole(above.shape),
                whole(half),
                whole(half),
                whole((8, features)),
                whole((1, features)),
            ],
        ),
        out_shape=[
            *[buffer] * 8,
            pltpu.HBM(above.shape, jnp.float32),
            jax.ShapeDtypeStruct(half, jnp.bfloat16),
            jax.ShapeDtypeStruct(half, jnp.bfloat16),
            jax.ShapeDtypeStruct((8, features), jnp.float32),
            pltpu.HBM((1, features), jnp.float32),
        ],
        compiler_params=pltpu.CompilerParams(vmem_limit_bytes=24 * megabyte),
        cost_estimate=cost(1, 1),
    )(own_bit(bits[-1]).reshape(1), *operands)


def head_terms(stream, scaling, matrix, columns, factor):
    count = columns.shape[0] // 2
    columns = columns.T
    inverse = norm_scale(stream)
    normed_low = lowered(stream * inverse * scaling)
    logits = times(normed_low, matrix)
    vocabulary = logits.shape[1] // count
    letters = lax.broadcasted_iota(jnp.int32, (stream.shape[0], vocabulary), 1)
    gradients = []
    loss = None
    for place in range(count):
        some = logits[:, place * vocabulary : (place + 1) * vocabulary]
        highest = jnp.max(some, axis=-1, keepdims=True)
        exponent = jnp.exp(some - highest)
        denominator = jnp.sum(exponent, axis=-1, keepdims=True)
        matches = letters == columns[:, place : place + 1].astype(jnp.int32)
        picked = jnp.sum(jnp.where(matches, some, 0.0), axis=-1, keepdims=True)
        weight = columns[:, count + place : count + place + 1]
        term = weight * (highest + jnp.log(denominator) - picked)
        loss = term if loss is None else loss + term
        chance = exponent * (1.0 / denominator)
        gradients.append(lowered((chance - jnp.where(matches, 1.0, 0.0)) * (weight * factor)))
    logit_low = gradients[0] if len(gradients) == 1 else jnp.concatenate(gradients, axis=1)
    matrix_grad = times(normed_low, logit_low, 0, 0)
    stream_grad, scaling_grad = norm_back(
        stream, inverse, scaling, times(logit_low, matrix, 1, 1)
    )
    return jnp.sum(loss, axis=0, keepdims=True), stream_grad, scaling_grad, lowered(matrix_grad)


def heads_part(
    share,
    bit,
    total,
    first,
    short,
    scaling,
    readout,
    trigram,
    main_columns,
    triple_columns,
    sent_ref,
    kept_ref,
):
    inverse_total = 1.0 / jnp.maximum(total, 1.0)
    vocabulary = readout.shape[1]
    rows, shorts = first.shape[0], short.shape[0]
    gap = lax.broadcasted_iota(jnp.int32, (rows, shorts), 0) - 3 * lax.broadcasted_iota(
        jnp.int32, (rows, shorts), 1
    )
    thrice = jnp.where((gap >= 0) & (gap < 3), 1.0, 0.0)
    merged = first + exact_times(thrice, short)
    main_loss, merged_grad, main_scale, readout_grad = head_terms(
        merged, scaling[0:1], readout, main_columns, inverse_total
    )
    sent_ref[:, :, :vocabulary], kept_ref[:, :, :vocabulary] = halves(
        by_core(readout_grad, share), bit
    )
    extra_loss, short_grad, extra_scale, trigram_grad = head_terms(
        short, scaling[1:2], trigram, triple_columns, trigram_share * inverse_total
    )
    sent_ref[:, :, vocabulary:], kept_ref[:, :, vocabulary:] = halves(
        by_core(trigram_grad, share), bit
    )
    short_grad = short_grad + exact_times(thrice, merged_grad, 0, 0)
    loss = main_loss + trigram_share * extra_loss
    return loss, merged_grad, short_grad, main_scale[None], extra_scale[None]


def pair_rows(pair_refs, key_ref, value_ref):
    rows, both = pair_refs[0].shape
    for at, pair_ref in enumerate(pair_refs):
        here = slice(at * rows, (at + 1) * rows)
        key_ref[here], value_ref[here] = pair_ref[:, : both // 2], pair_ref[:, both // 2 :]


def upper_kernel(share, members, number_ref, total_ref, query_ref, *refs):
    pair_refs, refs = refs[:members], refs[members:]
    (
        pooled_ref,
        first_ref,
        scale_ref,
        project_ref,
        in_ref,
        down_ref,
        readout_ref,
        trigram_ref,
        main_ref,
        triple_ref,
        loss_ref,
        first_out,
        table_sent,
        table_kept,
        mixed_out,
        hidden_out,
        normed_out,
        gradient_out,
        low_out,
        share_out,
        scale_out,
        key_ref,
        value_ref,
        short_ref,
    ) = refs
    step = pl.program_id(0)
    bit, member = number_ref[0], number_ref[1]

    @pl.when(step == 0)
    def _():
        rows = query_ref.shape[0]
        row = lax.broadcasted_iota(jnp.int32, (rows, rows), 1)
        entry = lax.broadcasted_iota(jnp.int32, (rows, rows), 0)
        pair_rows(pair_refs, key_ref, value_ref)
        counts = [
            jnp.where(entry <= row + (member - (member ^ at)) * rows, 1.0, 0.0)
            for at in range(members)
        ]
        mixed = attend(
            query_ref[...], key_ref, value_ref, jnp.concatenate(counts, axis=0), share_out
        ).T
        mixed_out[...] = mixed
        hidden = pooled_ref[...] + times(mixed, project_ref[...])
        hidden_out[...] = hidden
        normed_out[...] = lowered(hidden * norm_scale(hidden) * scale_ref[0:1])
        short_ref[...] = hidden

    short_ref[...] += feed_forward_part(normed_out[...], in_ref, down_ref)

    @pl.when(step == pl.num_programs(0) - 1)
    def _():
        loss, merged_grad, short_grad, main_scale, extra_scale = heads_part(
            share,
            bit,
            total_ref[0, 0],
            first_ref[...],
            short_ref[...],
            scale_ref[1:3],
            readout_ref[...],
            trigram_ref[...],
            main_ref[...],
            triple_ref[...],
            table_sent,
            table_kept,
        )
        loss_ref[...] = loss
        first_out[...] = merged_grad
        gradient_out[...] = short_grad
        low_out[...] = lowered(short_grad)
        scale_out[0:1] = main_scale
        scale_out[1:2] = extra_scale


def upper_layer(
    numbers,
    mask_total,
    queries,
    pairs,
    pooled,
    first,
    scaling,
    weights,
    places,
    hidden_size,
    vocabulary,
    main_columns,
    triple_columns,
    share,
):
    shorts, features = pooled.shape
    rows = first.shape[0]
    members = len(pairs)
    entries = members * shorts
    steps = 1
    width = hidden_size // steps
    chips = features // (2 * share)
    project_at, in_at, down_at, tables_at = places

    def whole(shape, at=(0, 0)):
        return pl.BlockSpec(shape, lambda j, numbers: at)

    def chunk(start):
        return pl.BlockSpec((features, width), lambda j, numbers: (0, start // width + j))

    table_piece = pl.BlockSpec((chips, share, 4 * vocabulary), lambda j, numbers: (0, 0, 0))
    table_buffer = pltpu.HBM((chips, share, 4 * vocabulary), jnp.bfloat16)
    half = (entries, features)
    weights = in_hbm(weights)
    return pl.pallas_call(
        functools.partial(upper_kernel, share, members),
        grid_spec=pltpu.PrefetchScalarGridSpec(
            num_scalar_prefetch=1,
            grid=(steps,),
            in_specs=[
                pl.BlockSpec(memory_space=pltpu.SMEM),
                whole(queries.shape),
                *[whole(pair.shape) for pair in pairs],
                whole(pooled.shape),
                whole(first.shape),
                whole(scaling.shape),
                whole((features, features), (0, project_at // features)),
                chunk(in_at),
                chunk(down_at),
                whole((features, vocabulary), (0, tables_at // vocabulary + 3)),
                whole((features, 3 * vocabulary), (0, tables_at // (3 * vocabulary))),
                whole(main_columns.shape),
                whole(triple_columns.shape),
            ],
            out_specs=[
                whole((1, 1)),
                whole(first.shape),
                table_piece,
                table_piece,
                *[whole(pooled.shape)] * 5,
                pl.BlockSpec((HEADS, entries, shorts), lambda j, numbers: (0, 0, 0)),
                whole((2, features)),
            ],
            scratch_shapes=[
                pltpu.VMEM(half, jnp.bfloat16),
                pltpu.VMEM(half, jnp.bfloat16),
                pltpu.VMEM((shorts, features), jnp.float32),
            ],
        ),
        out_shape=[
            pltpu.HBM((1, 1), jnp.float32),
            pltpu.HBM((rows, features), jnp.float32),
            table_buffer,
            table_buffer,
            pltpu.HBM((shorts, features), jnp.bfloat16),
            pltpu.HBM((shorts, features), jnp.float32),
            jax.ShapeDtypeStruct((shorts, features), jnp.bfloat16),
            pltpu.HBM((shorts, features), jnp.float32),
            jax.ShapeDtypeStruct((shorts, features), jnp.bfloat16),
            pltpu.HBM((HEADS, entries, shorts), jnp.bfloat16),
            pltpu.HBM((2, features), jnp.float32),
        ],
        compiler_params=pltpu.CompilerParams(
            vmem_limit_bytes=(36 if entries <= 512 else 60) * megabyte
        ),
        cost_estimate=cost(
            6 * shorts * features * hidden_size + 6 * features * vocabulary * (rows + 3 * shorts),
            8 * features * hidden_size + 8 * rows * features,
            shorts * hidden_size,
        ),
    )(
        numbers,
        mask_total.reshape(1, 1),
        in_hbm(queries),
        in_hbm(pairs[0]),
        *pairs[1:],
        in_hbm(pooled),
        in_hbm(first),
        scaling,
        weights,
        weights,
        weights,
        weights,
        weights,
        main_columns,
        triple_columns,
    )


def upper_back_kernel(members, grad_ref, came_ref, hidden_ref, gradient_ref, *refs):
    scale_ref, project_ref, query_ref, share_ref, *refs = refs
    pair_refs, refs = refs[:members], refs[members:]
    low_out, hidden_out, query_out, *refs = refs
    pair_outs, refs = refs[:members], refs[members:]
    scale_out, key_ref, value_ref, key_out, value_out = refs
    pair_rows(pair_refs, key_ref, value_ref)
    hidden = hidden_ref[...]
    hidden_grad, scaling_grad = norm_back(
        hidden,
        norm_scale(hidden),
        scale_ref[...],
        grad_ref[...] + came_ref[...].astype(jnp.float32),
    )
    hidden_grad = hidden_grad + gradient_ref[...]
    hidden_low = lowered(hidden_grad)
    hidden_out[...] = hidden_grad
    low_out[...] = hidden_low
    scale_out[...] = scaling_grad[None]
    mixed_grad = lowered(times(hidden_low, project_ref[...], 1, 1))
    query_out[...] = attend_back(
        query_ref[...], key_ref, value_ref, share_ref, mixed_grad, key_out, value_out
    ).T
    rows, features = query_ref.shape
    for at, pair_out in enumerate(pair_outs):
        here = slice(at * rows, (at + 1) * rows)
        pair_out[:, :features], pair_out[:, features:] = key_out[here], value_out[here]


def upper_back(
    grad, came, hidden, gradient, scaling, weights, project_at, queries, shares, pairs
):
    shorts, features = hidden.shape
    members = len(pairs)
    half = (members * shorts, features)

    def whole(x):
        return pl.BlockSpec(x.shape, lambda j: (0,) * x.ndim)

    operands = [grad, came, hidden, gradient, scaling, weights, queries, shares, *pairs]
    specs = [whole(x) for x in operands]
    specs[5] = pl.BlockSpec((features, features), lambda j: (0, project_at // features))
    operands[2:4] = [in_hbm(hidden), in_hbm(gradient)]
    operands[5:] = [in_hbm(x) for x in operands[5:]]
    low, hidden_grad, query_grad, *pair_grads, scale_grad = pl.pallas_call(
        functools.partial(upper_back_kernel, members),
        grid=(1,),
        in_specs=specs,
        out_specs=[whole(hidden)] * 3 + [whole(pair) for pair in pairs] + [whole(scaling)],
        out_shape=[
            pltpu.HBM(hidden.shape, jnp.bfloat16),
            pltpu.HBM(hidden.shape, jnp.float32),
            pltpu.HBM(hidden.shape, jnp.bfloat16),
            *[pltpu.HBM(pair.shape, jnp.bfloat16) for pair in pairs],
            pltpu.HBM(scaling.shape, jnp.float32),
        ],
        scratch_shapes=[pltpu.VMEM(half, jnp.bfloat16)] * 4,
        compiler_params=pltpu.CompilerParams(
            vmem_limit_bytes=(20 if half[0] <= 512 else 60) * megabyte
        ),
        cost_estimate=cost(1, 1),
    )(*operands)
    return low, hidden_grad, query_grad, pair_grads, scale_grad


def lower_kernel(
    share,
    bit_ref,
    grad_ref,
    came_ref,
    hidden_ref,
    gradient_ref,
    feed_scale_ref,
    project_ref,
    query_ref,
    key_ref,
    value_ref,
    share_ref,
    token_ref,
    mixed_ref,
    table_ref,
    attend_ref,
    scale_ref,
    attend_one_ref,
    feed_one_ref,
    heads_ref,
    sent_ref,
    kept_ref,
    key_out,
    value_out,
):
    bit = bit_ref[0]
    features = grad_ref.shape[1]
    is_token = token_ref[...]
    hidden = hidden_ref[...]
    hidden_grad, feed_scale = norm_back(
        hidden,
        norm_scale(hidden),
        feed_scale_ref[...],
        grad_ref[...] + came_ref[...].astype(jnp.float32),
    )
    hidden_low = lowered(hidden_grad + gradient_ref[...])
    mixed_grad = lowered(times(hidden_low, project_ref[...], 1, 1))
    query_grad = attend_back(
        query_ref[...], key_ref, value_ref, share_ref, mixed_grad, key_out, value_out
    )
    query_grad = lowered(times(query_grad, is_token).T)
    table = table_ref[...].astype(jnp.float32).T
    inverse = norm_scale(table)
    turned_normed = lowered((table * inverse * scale_ref[...]).T)
    parts = (query_grad, key_out[...], value_out[...])
    normed_grad = None
    for place, part in enumerate(parts):
        span = slice(place * features, (place + 1) * features)
        product = times(part, attend_ref[:, span], 1, 1)
        normed_grad = product if normed_grad is None else normed_grad + product
    table_grad, scaling_grad = norm_back(table, inverse, scale_ref[...], normed_grad)
    table_grad = table_grad + times(is_token, hidden_low, 0, 0)
    known = (
        scaling_grad[None],
        feed_scale[None],
        attend_one_ref[...],
        feed_one_ref[...],
        heads_ref[...],
    )
    scale_rows = jnp.concatenate(
        [*known, jnp.zeros((lanes - 6, features), jnp.float32)], axis=0
    )
    products = (
        lambda: times(mixed_ref[...], hidden_low, 0, 0),
        *(lambda part=part: times(turned_normed, part) for part in parts),
        lambda: table_grad.T,
        lambda: scale_rows.T,
    )
    start = 0
    for product in products:
        product = product()
        span = slice(start, start + product.shape[1])
        sent_ref[:, :, span], kept_ref[:, :, span] = halves(by_core(product, share), bit)
        start += product.shape[1]


def lower_gradients(
    bit,
    grad,
    came,
    hidden,
    gradient,
    feed_scaling,
    project,
    queries,
    table_qkv,
    shares,
    is_token,
    mixed_low,
    embed_columns,
    attend,
    scaling,
    attend_one_scale,
    feed_one_scale,
    head_scales,
    share,
):
    rows, features = hidden.shape
    entries = table_qkv.shape[0]
    chips = features // (2 * share)
    width = 4 * features + entries + lanes

    def whole(x, at=(0, 0)):
        return pl.BlockSpec(x.shape, lambda j, bit: (0,) * x.ndim)

    def third(at):
        return pl.BlockSpec((entries, features), lambda j, bit: (0, at))

    operands = [
        grad,
        came,
        in_hbm(hidden),
        in_hbm(gradient),
        feed_scaling,
        project,
        queries,
        table_qkv,
        table_qkv,
        shares,
        is_token,
        mixed_low,
        embed_columns,
        attend,
        scaling,
        attend_one_scale,
        feed_one_scale,
        head_scales,
    ]
    specs = [whole(x) for x in operands]
    specs[7:9] = [third(1), third(2)]
    buffer = pltpu.HBM((chips, share, width), jnp.bfloat16)
    return pl.pallas_call(
        functools.partial(lower_kernel, share),
        grid_spec=pltpu.PrefetchScalarGridSpec(
            num_scalar_prefetch=1,
            grid=(1,),
            in_specs=specs,
            out_specs=[pl.BlockSpec((chips, share, width), lambda j, bit: (0, 0, 0))] * 2,
            scratch_shapes=[pltpu.VMEM((entries, features), jnp.bfloat16)] * 2,
        ),
        out_shape=[buffer, buffer],
        compiler_params=pltpu.CompilerParams(vmem_limit_bytes=36 * megabyte),
        cost_estimate=cost(1, 1),
    )(bit, *operands)


def adam_step(master, prior_first, prior_second, gradient, factor, rate, decay):
    clipped = gradient * factor
    moment = beta_first * prior_first + (1.0 - beta_first) * clipped
    variance = beta_second * prior_second + (1.0 - beta_second) * clipped * clipped
    ratio = (
        moment
        / (1.0 - beta_first**STEP)
        / (jnp.sqrt(variance / (1.0 - beta_second**STEP)) + adam_epsilon)
    )
    return (master - rate * (ratio + decay * master), moment, variance)


def adam_kernel(layout, group_count, bit_ref, total_ref, *refs):
    bit = bit_ref[0, 0]
    weights = len(layout)
    group_refs, refs = refs[:group_count], refs[group_count:]
    masters, firsts, seconds = (refs[k * weights : (k + 1) * weights] for k in range(3))
    loss_ref, norm_ref = refs[3 * weights : 3 * weights + 2]
    outs = refs[3 * weights + 2 :]
    share = total_ref.shape[0] - 8
    loss_ref[...] = total_ref[share : share + 1, 0:1]
    square_total = jnp.sum(
        jnp.sum(total_ref[0:share], axis=1, keepdims=True), axis=0, keepdims=True
    )
    norm_value = jnp.sqrt(square_total)
    norm_ref[...] = norm_value
    factor = clip_limit / jnp.maximum(norm_value, clip_limit)
    for place, layers in enumerate(layout):
        for at, pieces in enumerate(layers):
            for group, start, here, width in pieces:
                span = (slice(None), slice(here, here + width))
                span = (at, *span) if len(layers) > 1 else span
                there = (slice(None), slice(start, start + width))
                if isinstance(group, tuple):
                    first, half = group
                    gradient = jnp.where(
                        bit == half, group_refs[first][there], group_refs[first + 1][there]
                    )
                else:
                    gradient = group_refs[group][there]
                new = adam_step(
                    masters[place][span],
                    firsts[place][span],
                    seconds[place][span],
                    gradient,
                    factor,
                    learning_rates[place],
                    weight_decays[place],
                )
                for kind in range(3):
                    outs[kind * weights + place][span] = new[kind]


def adam_all(layout, bit, totals, groups, masters, firsts, seconds):
    arrays = [*masters, *firsts, *seconds]
    shapes = [jax.ShapeDtypeStruct(array.shape, jnp.float32) for array in arrays]
    scalar = jax.ShapeDtypeStruct((1, 1), jnp.float32)
    moved = sum(8 * array.size for array in arrays)
    return pl.pallas_call(
        functools.partial(adam_kernel, layout, len(groups)),
        in_specs=[pl.BlockSpec(memory_space=pltpu.SMEM)]
        + whole_in_vmem(1 + len(groups) + len(arrays)),
        out_specs=whole_in_vmem(2 + len(arrays)),
        out_shape=[scalar, scalar, *shapes],
        compiler_params=pltpu.CompilerParams(vmem_limit_bytes=16 * megabyte),
        cost_estimate=cost(2 * moved, moved),
    )(bit.reshape(1, 1), totals, *groups, *arrays)


def pad_columns(array, width):
    return jnp.pad(array, ((0, 0), (0, width - array.shape[1])))


def local(
    tokens,
    next_targets,
    triple_targets,
    loss_mask,
    embedding,
    attention,
    projection,
    expansion,
    contraction,
    readout,
    trigram,
    scales,
    *moments,
):
    masters = (embedding, attention, projection, expansion, contraction, readout, trigram, scales)
    firsts = moments[:8]
    seconds = moments[8:]
    bits = index_bits()
    seq_size, dp_size = lax.axis_size("seq"), lax.axis_size("dp")
    devices = seq_size * dp_size
    held, piece = tokens.shape
    length = piece * seq_size
    sequences = held * dp_size
    members = devices // sequences
    vocabulary, share = embedding.shape
    features = share * devices
    hidden_size = expansion.shape[2]
    rows = length // members
    shorts = rows // 3
    member_bits = [("dp", b) for b in reversed(bits_of("dp")) if b < members]
    member = lax.axis_index("dp") % members
    group = (lax.axis_index("seq") * dp_size + lax.axis_index("dp")) // members

    integers = jnp.stack(
        [tokens, next_targets, triple_targets.reshape(held, piece), loss_mask]
    ).astype(jnp.bfloat16)
    integers = integers.reshape(share, -1)
    integer_width = integers.shape[1]
    integer_room = -(-integer_width // 128) * 128
    down_low = jnp.swapaxes(lowered(contraction), 1, 2)
    attention_low, projection_low, expansion_low = map(lowered, (attention, projection, expansion))
    stages = stages_of(bits)

    def packed(parts):
        return jnp.concatenate(parts, axis=1)[None]

    first_parts = [
        pad_columns(integers, integer_room),
        pad_columns(lowered(scales).T, 128),
        lowered(embedding).T,
        attention_low[0],
    ]
    second_parts = [projection_low[0], expansion_low[0], down_low[0]]
    third_parts = [
        attention_low[1],
        projection_low[1],
        expansion_low[1],
        down_low[1],
        lowered(trigram),
        lowered(readout),
    ]
    third = lax.all_gather(jnp.concatenate(third_parts, axis=1), ("seq", "dp"), axis=0, tiled=True)
    first, second = packed(first_parts), packed(second_parts)
    behind = None
    for stage in reversed(stages):
        first = stage_blocks(first, stage)
        if behind is not None:
            second = stage_blocks(second, behind)
            terms = together(*first, *second)
            first, second = terms[: len(first)], jnp.concatenate(terms[len(first) :])
        behind = stage
        if stage is not stages[0]:
            first, second = together(jnp.concatenate(first), second)
    first_other = [swapped(piece, bits[-1]) for piece in first]
    second = stage_blocks(second, behind)
    all_integers, scale_columns, embed_columns, attend_zero = merge_blocks(
        first, first_other, [part.shape[1] for part in first_parts], bits
    )
    project_one_at = 3 * features
    expand_one_at = 4 * features
    down_one_at = expand_one_at + hidden_size
    tables_at = down_one_at + hidden_size
    scale_rows = scale_columns[:, :6].astype(jnp.float32).T
    all_integers = all_integers[:, :integer_width].reshape(
        seq_size, dp_size, 4, held, piece
    )
    mask_total = jnp.sum(all_integers[:, :, 3].astype(jnp.float32))
    inverse_total = 1.0 / jnp.maximum(mask_total, 1.0)
    sequence = lax.dynamic_slice(
        all_integers,
        (0, group // held, 0, group % held, 0),
        (seq_size, 1, 4, 1, piece),
    )
    sequence = jnp.swapaxes(sequence.reshape(seq_size, 4, piece), 0, 1).reshape(4, length)
    own = lax.dynamic_slice_in_dim(sequence, member * rows, rows, 1).astype(jnp.int32)
    sequence_tokens = sequence[0].astype(jnp.int32)
    own_tokens = own[0]
    main_columns = own[1:4:2].astype(jnp.float32)
    triple_columns = jnp.concatenate(
        [own[2].reshape(shorts, 3), own[3].reshape(shorts, 3)], 1
    ).T.astype(jnp.float32)

    letters = jnp.arange(vocabulary, dtype=jnp.int32)
    is_token = (own_tokens[:, None] == letters).astype(jnp.bfloat16)
    place = member * rows + jnp.arange(rows, dtype=jnp.int32)
    earlier = (jnp.arange(length, dtype=jnp.int32)[None, :] <= place[:, None]).astype(jnp.bfloat16)
    counts = contract(
        (sequence_tokens[:, None] == letters).astype(jnp.bfloat16), earlier, "tv,rt->vr"
    )
    table = embed_columns.astype(jnp.float32).T
    table_inverse = norm_scale(table)
    table_normed = lowered(table * table_inverse * scale_rows[0])
    table_qkv = lowered(contract(table_normed, attend_zero, "vd,dc->vc"))
    queries = lowered(contract(is_token, table_qkv[:, :features], "rv,vc->rc"))
    counts, main_columns, triple_columns, mask_total, scale_rows = together(
        counts, main_columns, triple_columns, mask_total, scale_rows
    )
    mixed_low, shares = weighted_attention(queries, table_qkv, counts)
    mixed_low, *second = together(mixed_low, *second)
    second_other = [swapped(piece, bits[-1]) for piece in second]
    project_zero, expand_zero, down_zero = merge_blocks(
        second, second_other, [part.shape[1] for part in second_parts], bits
    )
    first_stream, normed_zero, hidden, last = first_layer_end(
        is_token,
        embed_columns,
        mixed_low,
        project_zero,
        expand_zero,
        down_zero,
        scale_rows[1:2],
    )

    normed_other = swapped(normed_zero, bits[-1])

    along = [(i, i + 1) for i in range(dp_size - 1) if (i + 1) % members]
    back = [(i + 1, i) for i, _ in along]
    previous = lax.ppermute(last, "dp", along)
    pooled, pooled_normed, short_queries, pairs = pooled_rows(
        first_stream, previous, third, scale_rows[2:3], shorts
    )
    pairs = stage_blocks(pairs, member_bits)
    (
        loss_local,
        merged_grad,
        table_sent,
        table_kept,
        short_mixed_low,
        short_hidden,
        short_normed,
        short_grad,
        short_low,
        short_shares,
        head_scales,
    ) = upper_layer(
        jnp.stack([own_bit(bits[-1]), member]),
        mask_total,
        short_queries,
        pairs,
        pooled,
        first_stream,
        scale_rows[3:6],
        third,
        (project_one_at, expand_one_at, down_one_at, tables_at),
        hidden_size,
        vocabulary,
        main_columns,
        triple_columns,
        share,
    )

    bit = own_bit(bits[-1])
    none = jnp.zeros((8, features), jnp.float32)
    upper, grad, other_grad, gradient = feed_back(
        short_grad,
        none,
        [swapped(short_low, bits[-1])],
        none,
        short_normed,
        swapped(short_normed, bits[-1]),
        (third, expand_one_at),
        (third, down_one_at),
        hidden_size,
        upper_steps,
        stages[0],
        bit,
        share,
    )
    grad, other_grad, gradient, *upper = together(grad, other_grad, gradient, *upper)
    upper = stage_sums(upper, stages[0])
    count = len(upper)
    short_hidden_low, short_hidden_grad, query_grad, pair_grads, feed_one_scale = upper_back(
        grad,
        swapped(other_grad, bits[-1]),
        short_hidden,
        gradient,
        scale_rows[3:4],
        third,
        project_one_at,
        short_queries,
        short_shares,
        pairs,
    )
    pair_grads = stage_sums(pair_grads, member_bits)
    *middle, rows_grad, rows_left, rows_right, returned, attend_one_scale = middle_gradients(
        bits,
        query_grad,
        pair_grads,
        pooled_normed,
        short_mixed_low,
        short_hidden_low,
        pooled,
        short_hidden_grad,
        merged_grad,
        third,
        scale_rows[2:3],
        share,
    )

    rows_left, rows_right = swapped(rows_left, bits[-1]), swapped(rows_right, bits[-1])
    middle = [[middle[4 + k], swapped(middle[k], bits[-1])] for k in range(4)]
    tables = [table_kept, swapped(table_sent, bits[-1])]
    middle = add_and_split([tables, *middle], stages[0])
    after_next = [(i + 2, i) for i in range(dp_size - 2) if i % members < members - 2]
    if after_next:
        later = lax.ppermute(returned, "dp", after_next)
    else:
        later = jnp.zeros_like(returned)
    other_back = jnp.where(member % 2 == 1, returned, later)
    returned = lax.ppermute(returned, "dp", back)
    rows_grad, rows_left, rows_right, returned, other_back, *terms = together(
        rows_grad, rows_left, rows_right, returned, other_back, *middle, *upper
    )
    middle, upper = stage_sums(terms[:count], stages[0]), terms[count:]
    fed, grad, other_grad, gradient = feed_back(
        rows_grad,
        returned,
        [rows_left, rows_right],
        other_back,
        normed_zero,
        normed_other,
        (expand_zero, 0),
        (down_zero, 0),
        hidden_size,
        feed_steps,
        stages[0],
        bit,
        share,
    )
    grad, other_grad, gradient, *terms = together(grad, other_grad, gradient, *fed, *middle)
    fed, middle = stage_sums(terms[:count], stages[0]), terms[count:]
    came = swapped(other_grad, bits[-1])
    came, *upper = together(came, *add_and_split([upper, middle], stages[1]))
    upper = stage_sums(upper, stages[1])
    lower = lower_gradients(
        own_bit(bits[-1]).reshape(1),
        grad,
        came,
        hidden,
        gradient,
        scale_rows[1:2],
        project_zero,
        queries,
        table_qkv,
        shares,
        is_token,
        mixed_low,
        embed_columns,
        attend_zero,
        scale_rows[0:1],
        attend_one_scale,
        feed_one_scale,
        head_scales,
        share,
    )

    *upper, later = upper
    sent, kept, *terms = together(*lower, *fed, *upper)
    fed, upper = terms[:count], terms[count:]
    lower = [kept, swapped(sent, bits[-1])]
    lower, *fed = together(tuple(add_and_split([lower], stages[0])), *fed)
    lower = stage_sums(lower, stages[0])
    fed = stage_sums(add_and_split([fed], stages[1]), stages[1])
    terms = together(*fed, *lower, later)
    upper, fed = [*upper, terms[-1]], terms[: len(fed)]
    lower = stage_sums(add_and_split([terms[len(fed) : -1]], stages[1]), stages[1])
    groups = (upper, fed, lower)
    for stage in stages[2:]:
        groups = [stage_sums(add_and_split([terms], stage), stage) for terms in groups]
    both = 2 * hidden_size
    upper, fed, lower = groups
    upper_rest, upper_mine, upper_other, square = add_and_square(
        bit, loss_local, [], upper, upper_steps, both
    )
    fed_mine, fed_other, square = add_and_square(
        bit, loss_local, [square], fed, feed_steps, both
    )
    upper_came, fed_came = swapped(upper_other, bits[-1]), swapped(fed_other, bits[-1])
    lower_sum, totals = add_and_square(bit, loss_local, [square], lower, 0, 0)
    for stage in [[bits[-1]], stages[0]]:
        totals = sum(stage_sums([totals] * (1 << len(stage)), stage))
    for stage in stages[1:]:
        totals = sum(stage_sums([totals] * (1 << len(stage)), stage))
    def fed_at(group, kind, steps):
        width = hidden_size // (2 * steps)
        return [
            ((group, half), (2 * j + kind) * width, (half * steps + j) * width, width)
            for half in range(2)
            for j in range(steps)
        ]

    groups = [upper_rest, lower_sum, upper_mine, upper_came, fed_mine, fed_came]
    scale_at = 4 * features + vocabulary
    groups.append(lower_sum[:, scale_at : scale_at + 6].T)
    attend_at = 4 * vocabulary
    layout = (
        ([(1, 4 * features, 0, vocabulary)],),
        ([(1, features, 0, 3 * features)], [(0, attend_at, 0, 3 * features)]),
        ([(1, 0, 0, features)], [(0, attend_at + 3 * features, 0, features)]),
        (fed_at(4, 1, feed_steps), fed_at(2, 1, upper_steps)),
        (fed_at(4, 0, feed_steps), fed_at(2, 0, upper_steps)),
        ([(0, 0, 0, vocabulary)],),
        ([(0, vocabulary, 0, 3 * vocabulary)],),
        ([(6, 0, 0, share)],),
    )

    def turned(arrays):
        embed, attend, project, expand, down, *rest = arrays
        return (embed.T, attend, project, expand, jnp.swapaxes(down, 1, 2), *rest)

    late = lax.optimization_barrier(
        (turned(masters), turned(firsts), turned(seconds), lower[0])
    )
    loss_total, norm_value, *results = adam_all(
        layout, bit, totals, groups, *late[:3]
    )
    return (
        loss_total.reshape(()),
        mask_total,
        norm_value.reshape(()),
        *turned(results[:8]),
        *turned(results[8:16]),
        *turned(results[16:]),
    )


def solution(mesh):
    weight_specs = (
        P(None, ("seq", "dp")),
        P(None, ("seq", "dp"), None),
        P(None, ("seq", "dp"), None),
        P(None, ("seq", "dp"), None),
        P(None, None, ("seq", "dp")),
        P(("seq", "dp"), None),
        P(("seq", "dp"), None),
        P(None, ("seq", "dp")),
    )
    in_specs = (
        P("dp", "seq"),
        P("dp", "seq"),
        P("dp", "seq", None),
        P("dp", "seq"),
    ) + weight_specs * 3
    out_specs = (P(), P(), P()) + weight_specs * 3
    return jax.shard_map(local, mesh=mesh, in_specs=in_specs, out_specs=out_specs, check_vma=False)
```

```python
import functools

import jax
import jax.numpy as jnp
from jax import lax
from jax.experimental import pallas as pl
from jax.experimental.pallas import tpu as pltpu
from jax.sharding import PartitionSpec as P

HEADS = 8
STEP = 10


norm_epsilon = 1e-06
trigram_share = 0.5
clip_limit = 0.1
beta_first = 0.9
beta_second = 0.95
adam_epsilon = 1e-08
learning_rates = (0.6, 0.05, 0.2, 0.05, 0.03, 0.05, 0.05, 0.6)
weight_decays = (0.0, 0.1, 0.1, 0.1, 0.1, 0.1, 0.1, 0.0)
exact_precision = lax.Precision.HIGHEST
megabyte = 1024 * 1024
lanes = 128


def lowered(array):
    return array.astype(jnp.bfloat16)


def contract(left, right, form):
    return jnp.einsum(form, left, right, preferred_element_type=jnp.float32)


def bits_of(axis):
    return [1 << k for k in range((lax.axis_size(axis) - 1).bit_length())]


def index_bits():
    return [("seq", b) for b in reversed(bits_of("seq"))] + [
        ("dp", b) for b in reversed(bits_of("dp"))
    ]


def own_bit(step):
    axis, weight = step
    return (lax.axis_index(axis) // weight) % 2


def swapped(x, step):
    axis, weight = step
    return lax.ppermute(x, axis, [(i, i ^ weight) for i in range(lax.axis_size(axis))])


def stages_of(bits):
    rest = bits[:-1]
    return [rest[max(0, end - 2) : end] for end in range(len(rest), 0, -2)]


def exchanged(x, steps):
    masks = {"seq": 0, "dp": 0}
    for axis, weight in steps:
        masks[axis] |= weight
    if not masks["seq"]:
        pairs = [(i, i ^ masks["dp"]) for i in range(lax.axis_size("dp"))]
        return lax.ppermute(x, "dp", pairs)
    if not masks["dp"]:
        pairs = [(i, i ^ masks["seq"]) for i in range(lax.axis_size("seq"))]
        return lax.ppermute(x, "seq", pairs)
    width = lax.axis_size("dp")
    pairs = [
        (i * width + j, (i ^ masks["seq"]) * width + (j ^ masks["dp"]))
        for i in range(lax.axis_size("seq"))
        for j in range(width)
    ]
    return lax.ppermute(x, ("seq", "dp"), pairs)


def chosen_steps(stage, number):
    return [step for at, step in enumerate(stage) if number >> (len(stage) - 1 - at) & 1]


def own_number(stage):
    number = jnp.int32(0)
    for step in stage:
        number = 2 * number + own_bit(step)
    return number


def stage_blocks(x, stage):
    return [x] + [exchanged(x, chosen_steps(stage, m)) for m in range(1, 1 << len(stage))]


def merge_kernel(widths, pieces, number_ref, *refs):
    mine, others, outs = refs[:pieces], refs[pieces : 2 * pieces], refs[2 * pieces :]
    bit, number = number_ref[0], number_ref[1]
    for piece in range(pieces):
        start = 0
        at = pl.ds(number ^ piece, 1)
        for width, out in zip(widths, outs):
            span = slice(start, start + width)
            out[at, pl.ds(bit, 1)] = mine[piece][:, :, span][None]
            out[at, pl.ds(1 - bit, 1)] = others[piece][:, :, span][None]
            start += width


def merge_blocks(mine, others, widths, bits):
    blocks, share, width = mine[0].shape
    pieces = len(mine)
    stages = stages_of(bits)
    block = jnp.arange(blocks, dtype=jnp.int32)
    place = jnp.zeros((blocks,), jnp.int32)
    low = 0
    for stage in stages[1:]:
        high = len(bits) - 1 - len(stages[0]) - low - len(stage)
        number = (block >> high) % (1 << len(stage)) ^ own_number(stage)
        place = place + (number << low)
        low += len(stage)
    numbers = jnp.concatenate(
        [jnp.stack([own_bit(bits[-1]), own_number(stages[0])]), place]
    )
    taken = pl.BlockSpec((1, share, width), lambda i, numbers: (i, 0, 0))
    outs = pl.pallas_call(
        functools.partial(merge_kernel, widths, pieces),
        grid_spec=pltpu.PrefetchScalarGridSpec(
            num_scalar_prefetch=1,
            grid=(blocks,),
            in_specs=[taken] * (2 * pieces),
            out_specs=[
                pl.BlockSpec(
                    (pieces, 2, share, w), lambda i, numbers: (numbers[2 + i], 0, 0, 0)
                )
                for w in widths
            ],
        ),
        out_shape=[
            pltpu.HBM((pieces * blocks, 2, share, w), mine[0].dtype) for w in widths
        ],
        compiler_params=pltpu.CompilerParams(vmem_limit_bytes=12 * megabyte),
        cost_estimate=cost(0, 8 * pieces * blocks * share * width),
    )(numbers, *[in_hbm(x) for x in mine], *others)
    return [out.reshape(2 * pieces * blocks * share, out.shape[-1]) for out in outs]


def together(*arrays):
    return lax.optimization_barrier(arrays)


def whole_in_vmem(count):
    return [pl.BlockSpec(memory_space=pltpu.VMEM)] * count


def in_hbm(array):
    return pltpu.with_memory_space_constraint(array, pltpu.HBM)


def cost(flops, moved, exponentials=0):
    return pl.CostEstimate(
        flops=int(flops), bytes_accessed=int(moved), transcendentals=int(exponentials)
    )


def halves(product, bit):
    low, high = product[:, 0], product[:, 1]
    return jnp.where(bit == 0, high, low), jnp.where(bit == 0, low, high)


def by_core(product, share):
    return lowered(product).reshape(-1, 2, share, product.shape[-1])


def split_kernel(widths, summands, pieces, number_ref, *refs):
    sources, outs = refs[: len(widths) * summands], refs[len(widths) * summands :]
    number = number_ref[0]
    start = 0
    for at, width in enumerate(widths):
        terms = sources[at * summands : (at + 1) * summands]
        for m in range(pieces):
            place = pl.ds(number ^ m, 1)
            total = terms[0][:, place].astype(jnp.float32)
            for term in terms[1:]:
                total = total + term[:, place].astype(jnp.float32)
            outs[m][:, :, start : start + width] = lowered(total)[:, 0]
        start += width


def add_and_split(sources, stage, settled=True):
    blocks, share, _ = sources[0][0].shape
    pieces = 1 << len(stage)
    widths = [terms[0].shape[-1] for terms in sources]
    total = sum(widths)
    arrays = []
    for terms in sources:
        for at, term in enumerate(terms):
            term = term.reshape(blocks // pieces, pieces, share, term.shape[-1])
            stays = settled and (at == 0 or len(sources) > 2)
            arrays.append(in_hbm(term) if stays else term)
    return pl.pallas_call(
        functools.partial(split_kernel, widths, len(sources[0]), pieces),
        grid_spec=pltpu.PrefetchScalarGridSpec(
            num_scalar_prefetch=1,
            grid=(blocks // pieces,),
            in_specs=[
                pl.BlockSpec((1, *x.shape[1:]), lambda i, number: (i, 0, 0, 0)) for x in arrays
            ],
            out_specs=[pl.BlockSpec((1, share, total), lambda i, number: (i, 0, 0))] * pieces,
        ),
        out_shape=[jax.ShapeDtypeStruct((blocks // pieces, share, total), jnp.bfloat16)] * pieces,
        compiler_params=pltpu.CompilerParams(vmem_limit_bytes=16 * megabyte),
        cost_estimate=cost(1, 1),
    )(own_number(stage).reshape(1), *arrays)


def add_and_square_kernel(earlier, terms_count, steps, both, bit_ref, loss_ref, *refs):
    befores, refs = refs[:earlier], refs[earlier:]
    terms, outs = refs[:terms_count], list(refs[terms_count:])
    total = terms[0][...].astype(jnp.float32)
    for term in terms[1:]:
        total = total + term[...].astype(jnp.float32)
    if total.shape[1] > both:
        outs.pop(0)[...] = total[:, both:]
    if both:
        mine_ref, other_ref = outs[:2]
        width = both // (2 * steps)
        for step in range(steps):
            here = slice(step * width, (step + 1) * width)
            first = total[:, 2 * step * width : (2 * step + 1) * width]
            second = total[:, (2 * step + 1) * width : (2 * step + 2) * width]
            mine_ref[:, here] = jnp.where(bit_ref[0, 0] == 0, first, second)
            other_ref[:, here] = jnp.where(bit_ref[0, 0] == 0, second, first)
    square_ref = outs[-1]
    share = total.shape[0]
    squares = jnp.zeros((share, lanes), jnp.float32)
    for before in befores:
        squares = squares + before[0:share]
    for start in range(0, total.shape[1], lanes):
        piece = total[:, start : start + lanes]
        squares = squares + piece * piece
    square_ref[0:share] = squares
    square_ref[share:] = jnp.broadcast_to(loss_ref[...], (8, lanes))


def add_and_square(bit, loss, befores, terms, steps, both):
    share, width = terms[0].shape[-2:]
    shapes = [(share, width - both)] if width > both else []
    shapes += [(share, both // 2)] * 2 if both else []
    shapes += [(share + 8, lanes)]
    return pl.pallas_call(
        functools.partial(
            add_and_square_kernel, len(befores), len(terms), steps, both
        ),
        in_specs=[pl.BlockSpec(memory_space=pltpu.SMEM)]
        + whole_in_vmem(1 + len(befores) + len(terms)),
        out_specs=whole_in_vmem(len(shapes)),
        out_shape=[jax.ShapeDtypeStruct(shape, jnp.float32) for shape in shapes],
        compiler_params=pltpu.CompilerParams(vmem_limit_bytes=8 * megabyte),
        cost_estimate=cost(3 * share * width, 12 * share * width),
    )(bit.reshape(1, 1), loss, *befores, *[term.reshape(share, width) for term in terms])


def stage_sums(pieces, stage):
    return [pieces[0]] + [
        exchanged(pieces[m], chosen_steps(stage, m)) for m in range(1, 1 << len(stage))
    ]


def norm_scale(stream):
    return lax.rsqrt(jnp.mean(stream * stream, axis=-1, keepdims=True) + norm_epsilon)


def norm_back(stream, inverse, scaling, gradient):
    unit = stream * inverse
    scaled = gradient * scaling
    scaling_grad = jnp.sum(gradient * unit, axis=0)
    stream_grad = inverse * (scaled - unit * jnp.mean(scaled * unit, axis=-1, keepdims=True))
    return stream_grad, scaling_grad


def times(left, right, left_side=1, right_side=0):
    return lax.dot_general(
        left, right, (((left_side,), (right_side,)), ((), ())), preferred_element_type=jnp.float32
    )


def exact_times(left, right, left_side=1, right_side=0):
    return lax.dot_general(
        left,
        right,
        (((left_side,), (right_side,)), ((), ())),
        preferred_element_type=jnp.float32,
        precision=exact_precision,
    )


def head_groups(features):
    depth = features // HEADS
    together = max(1, lanes // depth)
    return depth, [
        (first * depth, together * depth, range(first, first + together))
        for first in range(0, HEADS, together)
    ]


def own_lanes(width, depth, at):
    lane = lax.broadcasted_iota(jnp.int32, (1, width), 1)
    return (lane >= at * depth) & (lane < (at + 1) * depth)


def attend(queries, key_ref, value_ref, counts, share_ref):
    features = queries.shape[1]
    depth, groups = head_groups(features)
    queries = queries * jnp.asarray(depth ** (-0.5), queries.dtype)
    turned_values = value_ref[...].T
    mixed = []
    for start, width, places in groups:
        span = slice(start, start + width)
        keys = key_ref[:, span]
        for at, place in enumerate(places):
            own = own_lanes(width, depth, at)
            scores = times(jnp.where(own, keys, jnp.zeros_like(keys)), queries[:, span], 1, 1)
            scores = jnp.where(counts > 0.0, scores, -1e30)
            exponent = counts * jnp.exp(scores - jnp.max(scores, axis=0, keepdims=True))
            shares = lowered(exponent * (1.0 / jnp.sum(exponent, axis=0, keepdims=True)))
            share_ref[place] = shares
            here = slice(start + at * depth, start + (at + 1) * depth)
            mixed.append(lowered(times(turned_values[here], shares)))
    return jnp.concatenate(mixed, axis=0)


def attend_back(queries, key_ref, value_ref, share_ref, gradient, key_out, value_out):
    features = queries.shape[1]
    depth, groups = head_groups(features)
    scaled = depth ** (-0.5)
    turned_keys = key_ref[...].T
    query_grads = []
    for start, width, places in groups:
        span = slice(start, start + width)
        values = value_ref[:, span]
        key_sum = value_sum = None
        for at, place in enumerate(places):
            own = own_lanes(width, depth, at)
            low = share_ref[place]
            shares = low.astype(jnp.float32)
            share_grad = times(
                jnp.where(own, values, jnp.zeros_like(values)), gradient[:, span], 1, 1
            )
            dots = jnp.sum(shares * share_grad, axis=0, keepdims=True)
            score_grad = lowered(shares * (share_grad - dots))
            here = slice(start + at * depth, start + (at + 1) * depth)
            query_grads.append(lowered(times(turned_keys[here], score_grad) * scaled))
            key_part = times(score_grad, queries[:, span])
            value_part = times(low, gradient[:, span])
            if key_sum is None:
                key_sum, value_sum = key_part, value_part
            else:
                key_sum = jnp.where(own, key_part, key_sum)
                value_sum = jnp.where(own, value_part, value_sum)
        key_out[:, span] = lowered(key_sum * scaled)
        value_out[:, span] = lowered(value_sum)
    return jnp.concatenate(query_grads, axis=0)


def attend_kernel(query_ref, key_ref, value_ref, count_ref, mixed_ref, share_ref):
    mixed_ref[...] = attend(
        query_ref[...], key_ref, value_ref, count_ref[...], share_ref
    ).T


def weighted_attention(queries, table_qkv, counts):
    rows, features = queries.shape
    entries = table_qkv.shape[0]
    return pl.pallas_call(
        attend_kernel,
        grid=(1,),
        in_specs=[
            pl.BlockSpec((rows, features), lambda i: (0, 0)),
            pl.BlockSpec((entries, features), lambda i: (0, 1)),
            pl.BlockSpec((entries, features), lambda i: (0, 2)),
            pl.BlockSpec((entries, rows), lambda i: (0, 0)),
        ],
        out_specs=[
            pl.BlockSpec((rows, features), lambda i: (0, 0)),
            pl.BlockSpec((HEADS, entries, rows), lambda i: (0, 0, 0)),
        ],
        out_shape=[
            jax.ShapeDtypeStruct((rows, features), jnp.bfloat16),
            pltpu.HBM((HEADS, entries, rows), jnp.bfloat16),
        ],
        compiler_params=pltpu.CompilerParams(vmem_limit_bytes=24 * megabyte),
        cost_estimate=cost(
            4 * rows * entries * features,
            4 * rows * features + 4 * entries * features + (2 * HEADS + 4) * rows * entries,
            HEADS * rows * entries,
        ),
    )(queries, table_qkv, table_qkv, counts)


gelu_rate = 0.7978845608
gelu_cube = 0.044715


feed_steps = 2
feed_parts = 2
upper_steps = 2


def gelu_terms(before):
    square = before * before
    bent = jnp.tanh(before * (gelu_rate + gelu_rate * gelu_cube * square))
    half = 0.5 + 0.5 * bent
    return square, bent, half


def feed_forward_part(normed, in_ref, down_ref):
    width = in_ref.shape[1] // feed_parts
    total = None
    for part in range(feed_parts):
        span = slice(part * width, (part + 1) * width)
        before = times(normed, in_ref[:, span])
        _, _, half = gelu_terms(before)
        product = times(lowered(before * half), down_ref[:, span], 1, 1)
        total = product if total is None else total + product
    return total


def feed_forward_kernel(
    token_ref,
    embed_ref,
    mixed_ref,
    project_ref,
    in_ref,
    down_ref,
    scale_ref,
    result_ref,
    normed_ref,
    hidden_ref,
    last_ref,
):
    @pl.when(pl.program_id(0) == 0)
    def _():
        hidden = times(token_ref[...], embed_ref[...], 1, 1) + times(
            mixed_ref[...], project_ref[...]
        )
        hidden_ref[...] = hidden
        normed_ref[...] = lowered(hidden * norm_scale(hidden) * scale_ref[...])
        result_ref[...] = hidden

    result_ref[...] += feed_forward_part(normed_ref[...], in_ref, down_ref)
    last_ref[...] = result_ref[result_ref.shape[0] - last_ref.shape[0] :]


def first_layer_end(is_token, embed_columns, mixed_low, project, in_weight, down_weight, scaling):
    rows, features = mixed_low.shape
    hidden_size = in_weight.shape[1]
    width = hidden_size // feed_steps

    def whole(shape):
        return pl.BlockSpec(shape, lambda j: (0, 0))

    chunk = pl.BlockSpec((features, width), lambda j: (0, j))
    return pl.pallas_call(
        feed_forward_kernel,
        grid=(feed_steps,),
        in_specs=[
            whole(is_token.shape),
            whole(embed_columns.shape),
            whole(mixed_low.shape),
            whole(project.shape),
            chunk,
            chunk,
            whole(scaling.shape),
        ],
        out_specs=[whole((rows, features))] * 3 + [whole((8, features))],
        out_shape=[
            pltpu.HBM((rows, features), jnp.float32),
            pltpu.HBM((rows, features), jnp.bfloat16),
            pltpu.HBM((rows, features), jnp.float32),
            jax.ShapeDtypeStruct((8, features), jnp.float32),
        ],
        compiler_params=pltpu.CompilerParams(vmem_limit_bytes=20 * megabyte),
        cost_estimate=cost(
            4 * rows * features * hidden_size,
            4 * features * hidden_size + 14 * rows * features,
            rows * hidden_size,
        ),
    )(
        in_hbm(is_token),
        in_hbm(embed_columns),
        mixed_low,
        in_hbm(project),
        in_hbm(in_weight),
        in_hbm(down_weight),
        scaling,
    )


def pool_kernel(
    first_ref, last_ref, attend_ref, scale_ref, pooled_ref, normed_ref, query_ref, pair_ref
):
    rows, shorts = first_ref.shape[0], pooled_ref.shape[0]
    gap = (
        lax.broadcasted_iota(jnp.int32, (shorts, rows), 1)
        + 2
        - 3 * lax.broadcasted_iota(jnp.int32, (shorts, rows), 0)
    )
    pooling = jnp.where((gap >= 0) & (gap < 3), 1.0, 0.0)
    pooled = exact_times(pooling, first_ref[...])
    row = lax.broadcasted_iota(jnp.int32, (shorts, 1), 0)
    pooled = (
        pooled + jnp.where(row == 0, jnp.sum(last_ref[6:8], axis=0, keepdims=True), 0.0)
    ) * (1.0 / 3.0)
    pooled_ref[...] = pooled
    normed = lowered(pooled * norm_scale(pooled) * scale_ref[...])
    normed_ref[...] = normed
    features = first_ref.shape[1]
    query_ref[...] = lowered(times(normed, attend_ref[:, :features]))
    pair_ref[...] = lowered(times(normed, attend_ref[:, features:]))


def pooled_rows(first, previous, weights, scaling, shorts):
    rows, features = first.shape

    def whole(shape):
        return pl.BlockSpec(shape, lambda j: (0, 0))

    return pl.pallas_call(
        pool_kernel,
        grid=(1,),
        in_specs=[
            whole(first.shape),
            whole(previous.shape),
            whole((features, 3 * features)),
            whole(scaling.shape),
        ],
        out_specs=[
            whole((shorts, features)),
            whole((shorts, features)),
            whole((shorts, features)),
            whole((shorts, 2 * features)),
        ],
        out_shape=[
            pltpu.HBM((shorts, features), jnp.float32),
            pltpu.HBM((shorts, features), jnp.bfloat16),
            pltpu.HBM((shorts, features), jnp.bfloat16),
            jax.ShapeDtypeStruct((shorts, 2 * features), jnp.bfloat16),
        ],
        compiler_params=pltpu.CompilerParams(vmem_limit_bytes=12 * megabyte),
        cost_estimate=cost(
            6 * shorts * features * features + 12 * rows * shorts * features,
            6 * features * features + 4 * rows * features,
        ),
    )(in_hbm(first), previous, in_hbm(weights), scaling)


def feed_back_part(normed, gradient, in_weight, down_weight, turned_gradient, turned_normed, store):
    before = times(normed, in_weight)
    square, bent, half = gelu_terms(before)
    slope = half + half * (1.0 - bent) * before * (
        gelu_rate + 3.0 * gelu_rate * gelu_cube * square
    )
    before_grad = lowered(times(gradient, down_weight) * slope)
    store(0, times(turned_gradient, lowered(before * half)))
    store(1, times(turned_normed, before_grad))
    return times(before_grad, in_weight, 1, 1)


def feed_back_kernel(share, pieces, number_ref, *refs):
    (
        above_ref,
        back_ref,
        other_back_ref,
        normed_ref,
        other_normed_ref,
        in_ref,
        down_ref,
        *outs,
        grad_out,
        other_grad_out,
        gradient_out,
        gradient_ref,
        all_normed,
        turned_gradient,
        turned_normed,
        normed_grad,
        product_ref,
    ) = refs
    other_gradients, outs = outs[:-pieces], outs[-pieces:]
    step = pl.program_id(0)
    number = number_ref[1]
    rows = above_ref.shape[0]

    @pl.when(step == 0)
    def _():
        row = lax.broadcasted_iota(jnp.int32, (rows, 1), 0)
        gradient = above_ref[...] + jnp.where(row >= rows - 2, back_ref[0:1], 0.0)
        gradient_out[...] = gradient
        gradient_ref[:rows] = lowered(gradient)
        start = 0
        for other in other_gradients:
            span = slice(start, start + other.shape[1])
            gradient_ref[rows:, span] = lowered(
                other[...].astype(jnp.float32)
                + jnp.where(row >= rows - 2, other_back_ref[0:1, span], 0.0)
            )
            start += other.shape[1]
        all_normed[:rows] = normed_ref[...]
        all_normed[rows:] = other_normed_ref[...]
        turned_gradient[...] = gradient_ref[...].T
        turned_normed[...] = all_normed[...].T
        normed_grad[...] = jnp.zeros_like(normed_grad)

    width = in_ref.shape[1]

    def store(place, product):
        product_ref[...] = lowered(product).reshape(product_ref.shape)
        for core in range(2):
            span = slice((2 * core + place) * width, (2 * core + place + 1) * width)
            for m in range(pieces):
                outs[m][:, :, span] = product_ref[:, pl.ds(number ^ m, 1), core][:, 0]

    normed_grad[...] += feed_back_part(
        all_normed[...],
        gradient_ref[...],
        in_ref[...],
        down_ref[...],
        turned_gradient[...],
        turned_normed[...],
        store,
    )

    @pl.when(step == pl.num_programs(0) - 1)
    def _():
        grad_out[...] = normed_grad[:rows]
        other_grad_out[...] = lowered(normed_grad[rows:])


def feed_back(
    above,
    back,
    other_gradients,
    other_back,
    normed,
    other_normed,
    in_weight,
    down_weight,
    hidden_size,
    steps,
    stage,
    bit,
    share,
):
    rows, features = above.shape
    width = hidden_size // (2 * steps)
    blocks = features // (2 * share)
    pieces = 1 << len(stage)
    far = blocks // pieces

    def whole(shape):
        return pl.BlockSpec(shape, lambda j, numbers: (0, 0))

    def chunk(start):
        return pl.BlockSpec(
            (features, width), lambda j, numbers: (0, start // width + numbers[0] * steps + j)
        )

    piece = pl.BlockSpec((far, share, 4 * width), lambda j, numbers: (0, 0, j))
    *results, grad, other_grad, gradient = pl.pallas_call(
        functools.partial(feed_back_kernel, share, pieces),
        grid_spec=pltpu.PrefetchScalarGridSpec(
            num_scalar_prefetch=1,
            grid=(steps,),
            in_specs=[
                whole(above.shape),
                whole(back.shape),
                whole(back.shape),
                whole(normed.shape),
                whole(normed.shape),
                chunk(in_weight[1]),
                chunk(down_weight[1]),
                *[whole(x.shape) for x in other_gradients],
            ],
            out_specs=[piece] * pieces + [whole(above.shape)] * 3,
            scratch_shapes=[
                pltpu.VMEM((2 * rows, features), jnp.bfloat16),
                pltpu.VMEM((2 * rows, features), jnp.bfloat16),
                pltpu.VMEM((features, 2 * rows), jnp.bfloat16),
                pltpu.VMEM((features, 2 * rows), jnp.bfloat16),
                pltpu.VMEM((2 * rows, features), jnp.float32),
                pltpu.VMEM((far, pieces, 2, share, width), jnp.bfloat16),
            ],
        ),
        out_shape=[pltpu.HBM((far, share, 2 * hidden_size), jnp.bfloat16)] * pieces
        + [
            jax.ShapeDtypeStruct(above.shape, jnp.float32),
            jax.ShapeDtypeStruct(above.shape, jnp.bfloat16),
            pltpu.HBM(above.shape, jnp.float32),
        ],
        compiler_params=pltpu.CompilerParams(vmem_limit_bytes=36 * megabyte),
        cost_estimate=cost(1, 1),
    )(
        jnp.stack([bit, own_number(stage)]),
        in_hbm(above),
        back,
        other_back,
        in_hbm(normed),
        other_normed,
        in_hbm(in_weight[0]),
        in_hbm(down_weight[0]),
        *other_gradients,
    )
    return results, grad, other_grad, gradient


def middle_kernel(
    share,
    members,
    bit_ref,
    query_ref,
    *refs,
):
    pair_refs, refs = refs[:members], refs[members:]
    (
        normed_ref,
        mixed_ref,
        low_ref,
        pooled_ref,
        hidden_grad_ref,
        above_ref,
        attend_ref,
        scale_ref,
        *outs,
        rows_out,
        left_out,
        right_out,
        back_out,
        scale_out,
    ) = refs
    sent_refs, kept_refs = outs[: len(outs) // 2], outs[len(outs) // 2 :]
    bit = bit_ref[0]
    features = query_ref.shape[1]
    pairs = pair_refs[0][...].astype(jnp.float32)
    for pair_ref in pair_refs[1:]:
        pairs = pairs + pair_ref[...].astype(jnp.float32)
    pairs = lowered(pairs)
    queries = query_ref[...]
    normed_grad = times(queries, attend_ref[:, :features], 1, 1) + times(
        pairs, attend_ref[:, features:], 1, 1
    )
    pooled = pooled_ref[...]
    pooled_grad, scaling_grad = norm_back(
        pooled, norm_scale(pooled), scale_ref[...], normed_grad
    )
    scale_out[...] = scaling_grad[None]
    pooled_grad = (pooled_grad + hidden_grad_ref[...]) * (1.0 / 3.0)
    back_out[...] = pooled_grad[0 : back_out.shape[0]]
    rows, shorts = rows_out.shape[0], pooled.shape[0]
    gap = (
        lax.broadcasted_iota(jnp.int32, (rows, shorts), 0)
        + 2
        - 3 * lax.broadcasted_iota(jnp.int32, (rows, shorts), 1)
    )
    spreading = jnp.where((gap >= 0) & (gap < 3), 1.0, 0.0)
    rows_grad = above_ref[...] + exact_times(spreading, pooled_grad)
    rows_out[...] = rows_grad
    left_out[...] = lowered(rows_grad[:, : features // 2])
    right_out[...] = lowered(rows_grad[:, features // 2 :])
    turned_normed = normed_ref[...].T
    products = (
        lambda: times(turned_normed, queries),
        lambda: times(turned_normed, pairs[:, :features]),
        lambda: times(turned_normed, pairs[:, features:]),
        lambda: times(mixed_ref[...], low_ref[...], 0, 0),
    )
    for product, sent_ref, kept_ref in zip(products, sent_refs, kept_refs):
        sent_ref[...], kept_ref[...] = halves(by_core(product(), share), bit)


def middle_gradients(
    bits,
    query_grad,
    pair_grads,
    normed,
    mixed_low,
    hidden_low,
    pooled,
    hidden_grad,
    above,
    weights,
    scaling,
    share,
):
    shorts, features = pooled.shape
    rows = above.shape[0]
    chips = features // (2 * share)

    def whole(shape):
        return pl.BlockSpec(shape, lambda j, bit: (0, 0))

    operands = [
        query_grad,
        *pair_grads,
        in_hbm(normed),
        in_hbm(mixed_low),
        hidden_low,
        in_hbm(pooled),
        hidden_grad,
        in_hbm(above),
        in_hbm(weights),
        scaling,
    ]
    specs = [whole(x.shape) for x in operands]
    specs[-2] = whole((features, 3 * features))
    buffer = pltpu.HBM((chips, share, features), jnp.bfloat16)
    piece = pl.BlockSpec((chips, share, features), lambda j, bit: (0, 0, 0))
    half = (rows, features // 2)
    return pl.pallas_call(
        functools.partial(middle_kernel, share, len(pair_grads)),
        grid_spec=pltpu.PrefetchScalarGridSpec(
            num_scalar_prefetch=1,
            grid=(1,),
            in_specs=specs,
            out_specs=[
                *[piece] * 8,
                whole(above.shape),
                whole(half),
                whole(half),
                whole((8, features)),
                whole((1, features)),
            ],
        ),
        out_shape=[
            *[buffer] * 8,
            pltpu.HBM(above.shape, jnp.float32),
            jax.ShapeDtypeStruct(half, jnp.bfloat16),
            jax.ShapeDtypeStruct(half, jnp.bfloat16),
            jax.ShapeDtypeStruct((8, features), jnp.float32),
            pltpu.HBM((1, features), jnp.float32),
        ],
        compiler_params=pltpu.CompilerParams(vmem_limit_bytes=24 * megabyte),
        cost_estimate=cost(1, 1),
    )(own_bit(bits[-1]).reshape(1), *operands)


def head_terms(stream, scaling, matrix, columns, factor):
    count = columns.shape[0] // 2
    columns = columns.T
    inverse = norm_scale(stream)
    normed_low = lowered(stream * inverse * scaling)
    logits = times(normed_low, matrix)
    vocabulary = logits.shape[1] // count
    letters = lax.broadcasted_iota(jnp.int32, (stream.shape[0], vocabulary), 1)
    gradients = []
    loss = None
    for place in range(count):
        some = logits[:, place * vocabulary : (place + 1) * vocabulary]
        highest = jnp.max(some, axis=-1, keepdims=True)
        exponent = jnp.exp(some - highest)
        denominator = jnp.sum(exponent, axis=-1, keepdims=True)
        matches = letters == columns[:, place : place + 1].astype(jnp.int32)
        picked = jnp.sum(jnp.where(matches, some, 0.0), axis=-1, keepdims=True)
        weight = columns[:, count + place : count + place + 1]
        term = weight * (highest + jnp.log(denominator) - picked)
        loss = term if loss is None else loss + term
        chance = exponent * (1.0 / denominator)
        gradients.append(lowered((chance - jnp.where(matches, 1.0, 0.0)) * (weight * factor)))
    logit_low = gradients[0] if len(gradients) == 1 else jnp.concatenate(gradients, axis=1)
    matrix_grad = times(normed_low, logit_low, 0, 0)
    stream_grad, scaling_grad = norm_back(
        stream, inverse, scaling, times(logit_low, matrix, 1, 1)
    )
    return jnp.sum(loss, axis=0, keepdims=True), stream_grad, scaling_grad, lowered(matrix_grad)


def heads_part(
    share,
    bit,
    total,
    first,
    short,
    scaling,
    readout,
    trigram,
    main_columns,
    triple_columns,
    sent_ref,
    kept_ref,
):
    inverse_total = 1.0 / jnp.maximum(total, 1.0)
    vocabulary = readout.shape[1]
    rows, shorts = first.shape[0], short.shape[0]
    gap = lax.broadcasted_iota(jnp.int32, (rows, shorts), 0) - 3 * lax.broadcasted_iota(
        jnp.int32, (rows, shorts), 1
    )
    thrice = jnp.where((gap >= 0) & (gap < 3), 1.0, 0.0)
    merged = first + exact_times(thrice, short)
    main_loss, merged_grad, main_scale, readout_grad = head_terms(
        merged, scaling[0:1], readout, main_columns, inverse_total
    )
    sent_ref[:, :, :vocabulary], kept_ref[:, :, :vocabulary] = halves(
        by_core(readout_grad, share), bit
    )
    extra_loss, short_grad, extra_scale, trigram_grad = head_terms(
        short, scaling[1:2], trigram, triple_columns, trigram_share * inverse_total
    )
    sent_ref[:, :, vocabulary:], kept_ref[:, :, vocabulary:] = halves(
        by_core(trigram_grad, share), bit
    )
    short_grad = short_grad + exact_times(thrice, merged_grad, 0, 0)
    loss = main_loss + trigram_share * extra_loss
    return loss, merged_grad, short_grad, main_scale[None], extra_scale[None]


def pair_rows(pair_refs, key_ref, value_ref):
    rows, both = pair_refs[0].shape
    for at, pair_ref in enumerate(pair_refs):
        here = slice(at * rows, (at + 1) * rows)
        key_ref[here], value_ref[here] = pair_ref[:, : both // 2], pair_ref[:, both // 2 :]


def upper_kernel(share, members, number_ref, total_ref, query_ref, *refs):
    pair_refs, refs = refs[:members], refs[members:]
    (
        pooled_ref,
        first_ref,
        scale_ref,
        project_ref,
        in_ref,
        down_ref,
        readout_ref,
        trigram_ref,
        main_ref,
        triple_ref,
        loss_ref,
        first_out,
        table_sent,
        table_kept,
        mixed_out,
        hidden_out,
        normed_out,
        gradient_out,
        low_out,
        share_out,
        scale_out,
        key_ref,
        value_ref,
        short_ref,
    ) = refs
    step = pl.program_id(0)
    bit, member = number_ref[0], number_ref[1]

    @pl.when(step == 0)
    def _():
        rows = query_ref.shape[0]
        row = lax.broadcasted_iota(jnp.int32, (rows, rows), 1)
        entry = lax.broadcasted_iota(jnp.int32, (rows, rows), 0)
        pair_rows(pair_refs, key_ref, value_ref)
        counts = [
            jnp.where(entry <= row + (member - (member ^ at)) * rows, 1.0, 0.0)
            for at in range(members)
        ]
        mixed = attend(
            query_ref[...], key_ref, value_ref, jnp.concatenate(counts, axis=0), share_out
        ).T
        mixed_out[...] = mixed
        hidden = pooled_ref[...] + times(mixed, project_ref[...])
        hidden_out[...] = hidden
        normed_out[...] = lowered(hidden * norm_scale(hidden) * scale_ref[0:1])
        short_ref[...] = hidden

    short_ref[...] += feed_forward_part(normed_out[...], in_ref, down_ref)

    @pl.when(step == pl.num_programs(0) - 1)
    def _():
        loss, merged_grad, short_grad, main_scale, extra_scale = heads_part(
            share,
            bit,
            total_ref[0, 0],
            first_ref[...],
            short_ref[...],
            scale_ref[1:3],
            readout_ref[...],
            trigram_ref[...],
            main_ref[...],
            triple_ref[...],
            table_sent,
            table_kept,
        )
        loss_ref[...] = loss
        first_out[...] = merged_grad
        gradient_out[...] = short_grad
        low_out[...] = lowered(short_grad)
        scale_out[0:1] = main_scale
        scale_out[1:2] = extra_scale


def upper_layer(
    numbers,
    mask_total,
    queries,
    pairs,
    pooled,
    first,
    scaling,
    weights,
    places,
    hidden_size,
    vocabulary,
    main_columns,
    triple_columns,
    share,
):
    shorts, features = pooled.shape
    rows = first.shape[0]
    members = len(pairs)
    entries = members * shorts
    steps = 1
    width = hidden_size // steps
    chips = features // (2 * share)
    project_at, in_at, down_at, tables_at = places

    def whole(shape, at=(0, 0)):
        return pl.BlockSpec(shape, lambda j, numbers: at)

    def chunk(start):
        return pl.BlockSpec((features, width), lambda j, numbers: (0, start // width + j))

    table_piece = pl.BlockSpec((chips, share, 4 * vocabulary), lambda j, numbers: (0, 0, 0))
    table_buffer = pltpu.HBM((chips, share, 4 * vocabulary), jnp.bfloat16)
    half = (entries, features)
    weights = in_hbm(weights)
    return pl.pallas_call(
        functools.partial(upper_kernel, share, members),
        grid_spec=pltpu.PrefetchScalarGridSpec(
            num_scalar_prefetch=1,
            grid=(steps,),
            in_specs=[
                pl.BlockSpec(memory_space=pltpu.SMEM),
                whole(queries.shape),
                *[whole(pair.shape) for pair in pairs],
                whole(pooled.shape),
                whole(first.shape),
                whole(scaling.shape),
                whole((features, features), (0, project_at // features)),
                chunk(in_at),
                chunk(down_at),
                whole((features, vocabulary), (0, tables_at // vocabulary + 3)),
                whole((features, 3 * vocabulary), (0, tables_at // (3 * vocabulary))),
                whole(main_columns.shape),
                whole(triple_columns.shape),
            ],
            out_specs=[
                whole((1, 1)),
                whole(first.shape),
                table_piece,
                table_piece,
                *[whole(pooled.shape)] * 5,
                pl.BlockSpec((HEADS, entries, shorts), lambda j, numbers: (0, 0, 0)),
                whole((2, features)),
            ],
            scratch_shapes=[
                pltpu.VMEM(half, jnp.bfloat16),
                pltpu.VMEM(half, jnp.bfloat16),
                pltpu.VMEM((shorts, features), jnp.float32),
            ],
        ),
        out_shape=[
            pltpu.HBM((1, 1), jnp.float32),
            pltpu.HBM((rows, features), jnp.float32),
            table_buffer,
            table_buffer,
            pltpu.HBM((shorts, features), jnp.bfloat16),
            pltpu.HBM((shorts, features), jnp.float32),
            jax.ShapeDtypeStruct((shorts, features), jnp.bfloat16),
            pltpu.HBM((shorts, features), jnp.float32),
            jax.ShapeDtypeStruct((shorts, features), jnp.bfloat16),
            pltpu.HBM((HEADS, entries, shorts), jnp.bfloat16),
            pltpu.HBM((2, features), jnp.float32),
        ],
        compiler_params=pltpu.CompilerParams(
            vmem_limit_bytes=(36 if entries <= 512 else 60) * megabyte
        ),
        cost_estimate=cost(
            6 * shorts * features * hidden_size + 6 * features * vocabulary * (rows + 3 * shorts),
            8 * features * hidden_size + 8 * rows * features,
            shorts * hidden_size,
        ),
    )(
        numbers,
        mask_total.reshape(1, 1),
        in_hbm(queries),
        in_hbm(pairs[0]),
        *pairs[1:],
        in_hbm(pooled),
        in_hbm(first),
        scaling,
        weights,
        weights,
        weights,
        weights,
        weights,
        main_columns,
        triple_columns,
    )


def upper_back_kernel(members, grad_ref, came_ref, hidden_ref, gradient_ref, *refs):
    scale_ref, project_ref, query_ref, share_ref, *refs = refs
    pair_refs, refs = refs[:members], refs[members:]
    low_out, hidden_out, query_out, *refs = refs
    pair_outs, refs = refs[:members], refs[members:]
    scale_out, key_ref, value_ref, key_out, value_out = refs
    pair_rows(pair_refs, key_ref, value_ref)
    hidden = hidden_ref[...]
    hidden_grad, scaling_grad = norm_back(
        hidden,
        norm_scale(hidden),
        scale_ref[...],
        grad_ref[...] + came_ref[...].astype(jnp.float32),
    )
    hidden_grad = hidden_grad + gradient_ref[...]
    hidden_low = lowered(hidden_grad)
    hidden_out[...] = hidden_grad
    low_out[...] = hidden_low
    scale_out[...] = scaling_grad[None]
    mixed_grad = lowered(times(hidden_low, project_ref[...], 1, 1))
    query_out[...] = attend_back(
        query_ref[...], key_ref, value_ref, share_ref, mixed_grad, key_out, value_out
    ).T
    rows, features = query_ref.shape
    for at, pair_out in enumerate(pair_outs):
        here = slice(at * rows, (at + 1) * rows)
        pair_out[:, :features], pair_out[:, features:] = key_out[here], value_out[here]


def upper_back(
    grad, came, hidden, gradient, scaling, weights, project_at, queries, shares, pairs
):
    shorts, features = hidden.shape
    members = len(pairs)
    half = (members * shorts, features)

    def whole(x):
        return pl.BlockSpec(x.shape, lambda j: (0,) * x.ndim)

    operands = [grad, came, hidden, gradient, scaling, weights, queries, shares, *pairs]
    specs = [whole(x) for x in operands]
    specs[5] = pl.BlockSpec((features, features), lambda j: (0, project_at // features))
    operands[2:4] = [in_hbm(hidden), in_hbm(gradient)]
    operands[5:] = [in_hbm(x) for x in operands[5:]]
    low, hidden_grad, query_grad, *pair_grads, scale_grad = pl.pallas_call(
        functools.partial(upper_back_kernel, members),
        grid=(1,),
        in_specs=specs,
        out_specs=[whole(hidden)] * 3 + [whole(pair) for pair in pairs] + [whole(scaling)],
        out_shape=[
            jax.ShapeDtypeStruct(hidden.shape, jnp.bfloat16),
            jax.ShapeDtypeStruct(hidden.shape, jnp.float32),
            jax.ShapeDtypeStruct(hidden.shape, jnp.bfloat16),
            *[jax.ShapeDtypeStruct(pair.shape, jnp.bfloat16) for pair in pairs],
            pltpu.HBM(scaling.shape, jnp.float32),
        ],
        scratch_shapes=[pltpu.VMEM(half, jnp.bfloat16)] * 4,
        compiler_params=pltpu.CompilerParams(
            vmem_limit_bytes=(20 if half[0] <= 512 else 60) * megabyte
        ),
        cost_estimate=cost(1, 1),
    )(*operands)
    return low, hidden_grad, query_grad, pair_grads, scale_grad


def lower_kernel(
    share,
    bit_ref,
    grad_ref,
    came_ref,
    hidden_ref,
    gradient_ref,
    feed_scale_ref,
    project_ref,
    query_ref,
    key_ref,
    value_ref,
    share_ref,
    token_ref,
    mixed_ref,
    table_ref,
    attend_ref,
    scale_ref,
    attend_one_ref,
    feed_one_ref,
    heads_ref,
    sent_ref,
    kept_ref,
    key_out,
    value_out,
):
    bit = bit_ref[0]
    features = grad_ref.shape[1]
    is_token = token_ref[...]
    hidden = hidden_ref[...]
    hidden_grad, feed_scale = norm_back(
        hidden,
        norm_scale(hidden),
        feed_scale_ref[...],
        grad_ref[...] + came_ref[...].astype(jnp.float32),
    )
    hidden_low = lowered(hidden_grad + gradient_ref[...])
    mixed_grad = lowered(times(hidden_low, project_ref[...], 1, 1))
    query_grad = attend_back(
        query_ref[...], key_ref, value_ref, share_ref, mixed_grad, key_out, value_out
    )
    query_grad = lowered(times(query_grad, is_token).T)
    table = table_ref[...].astype(jnp.float32).T
    inverse = norm_scale(table)
    turned_normed = lowered((table * inverse * scale_ref[...]).T)
    parts = (query_grad, key_out[...], value_out[...])
    normed_grad = None
    for place, part in enumerate(parts):
        span = slice(place * features, (place + 1) * features)
        product = times(part, attend_ref[:, span], 1, 1)
        normed_grad = product if normed_grad is None else normed_grad + product
    table_grad, scaling_grad = norm_back(table, inverse, scale_ref[...], normed_grad)
    table_grad = table_grad + times(is_token, hidden_low, 0, 0)
    known = (
        scaling_grad[None],
        feed_scale[None],
        attend_one_ref[...],
        feed_one_ref[...],
        heads_ref[...],
    )
    scale_rows = jnp.concatenate(
        [*known, jnp.zeros((lanes - 6, features), jnp.float32)], axis=0
    )
    products = (
        lambda: times(mixed_ref[...], hidden_low, 0, 0),
        *(lambda part=part: times(turned_normed, part) for part in parts),
        lambda: table_grad.T,
        lambda: scale_rows.T,
    )
    start = 0
    for product in products:
        product = product()
        span = slice(start, start + product.shape[1])
        sent_ref[:, :, span], kept_ref[:, :, span] = halves(by_core(product, share), bit)
        start += product.shape[1]


def lower_gradients(
    bit,
    grad,
    came,
    hidden,
    gradient,
    feed_scaling,
    project,
    queries,
    table_qkv,
    shares,
    is_token,
    mixed_low,
    embed_columns,
    attend,
    scaling,
    attend_one_scale,
    feed_one_scale,
    head_scales,
    share,
):
    rows, features = hidden.shape
    entries = table_qkv.shape[0]
    chips = features // (2 * share)
    width = 4 * features + entries + lanes

    def whole(x, at=(0, 0)):
        return pl.BlockSpec(x.shape, lambda j, bit: (0,) * x.ndim)

    def third(at):
        return pl.BlockSpec((entries, features), lambda j, bit: (0, at))

    operands = [
        grad,
        came,
        in_hbm(hidden),
        in_hbm(gradient),
        feed_scaling,
        project,
        queries,
        table_qkv,
        table_qkv,
        shares,
        is_token,
        mixed_low,
        embed_columns,
        attend,
        scaling,
        attend_one_scale,
        feed_one_scale,
        head_scales,
    ]
    specs = [whole(x) for x in operands]
    specs[7:9] = [third(1), third(2)]
    buffer = jax.ShapeDtypeStruct((chips, share, width), jnp.bfloat16)
    return pl.pallas_call(
        functools.partial(lower_kernel, share),
        grid_spec=pltpu.PrefetchScalarGridSpec(
            num_scalar_prefetch=1,
            grid=(1,),
            in_specs=specs,
            out_specs=[pl.BlockSpec((chips, share, width), lambda j, bit: (0, 0, 0))] * 2,
            scratch_shapes=[pltpu.VMEM((entries, features), jnp.bfloat16)] * 2,
        ),
        out_shape=[buffer, buffer],
        compiler_params=pltpu.CompilerParams(vmem_limit_bytes=36 * megabyte),
        cost_estimate=cost(1, 1),
    )(bit, *operands)


def adam_step(master, prior_first, prior_second, gradient, factor, rate, decay):
    clipped = gradient * factor
    moment = beta_first * prior_first + (1.0 - beta_first) * clipped
    variance = beta_second * prior_second + (1.0 - beta_second) * clipped * clipped
    ratio = (
        moment
        / (1.0 - beta_first**STEP)
        / (jnp.sqrt(variance / (1.0 - beta_second**STEP)) + adam_epsilon)
    )
    return (master - rate * (ratio + decay * master), moment, variance)


def adam_kernel(layout, group_count, bit_ref, total_ref, *refs):
    bit = bit_ref[0, 0]
    weights = len(layout)
    group_refs, refs = refs[:group_count], refs[group_count:]
    masters, firsts, seconds = (refs[k * weights : (k + 1) * weights] for k in range(3))
    loss_ref, norm_ref = refs[3 * weights : 3 * weights + 2]
    outs = refs[3 * weights + 2 :]
    share = total_ref.shape[0] - 8
    loss_ref[...] = total_ref[share : share + 1, 0:1]
    square_total = jnp.sum(
        jnp.sum(total_ref[0:share], axis=1, keepdims=True), axis=0, keepdims=True
    )
    norm_value = jnp.sqrt(square_total)
    norm_ref[...] = norm_value
    factor = clip_limit / jnp.maximum(norm_value, clip_limit)
    for place, layers in enumerate(layout):
        for at, pieces in enumerate(layers):
            for group, start, here, width in pieces:
                span = (slice(None), slice(here, here + width))
                span = (at, *span) if len(layers) > 1 else span
                there = (slice(None), slice(start, start + width))
                if isinstance(group, tuple):
                    first, half = group
                    gradient = jnp.where(
                        bit == half, group_refs[first][there], group_refs[first + 1][there]
                    )
                else:
                    gradient = group_refs[group][there]
                new = adam_step(
                    masters[place][span],
                    firsts[place][span],
                    seconds[place][span],
                    gradient,
                    factor,
                    learning_rates[place],
                    weight_decays[place],
                )
                for kind in range(3):
                    outs[kind * weights + place][span] = new[kind]


def adam_all(layout, bit, totals, groups, masters, firsts, seconds):
    arrays = [*masters, *firsts, *seconds]
    shapes = [jax.ShapeDtypeStruct(array.shape, jnp.float32) for array in arrays]
    scalar = jax.ShapeDtypeStruct((1, 1), jnp.float32)
    moved = sum(8 * array.size for array in arrays)
    return pl.pallas_call(
        functools.partial(adam_kernel, layout, len(groups)),
        in_specs=[pl.BlockSpec(memory_space=pltpu.SMEM)]
        + whole_in_vmem(1 + len(groups) + len(arrays)),
        out_specs=whole_in_vmem(2 + len(arrays)),
        out_shape=[scalar, scalar, *shapes],
        compiler_params=pltpu.CompilerParams(vmem_limit_bytes=16 * megabyte),
        cost_estimate=cost(2 * moved, moved),
    )(bit.reshape(1, 1), totals, *groups, *arrays)


def pad_columns(array, width):
    return jnp.pad(array, ((0, 0), (0, width - array.shape[1])))


def local(
    tokens,
    next_targets,
    triple_targets,
    loss_mask,
    embedding,
    attention,
    projection,
    expansion,
    contraction,
    readout,
    trigram,
    scales,
    *moments,
):
    masters = (embedding, attention, projection, expansion, contraction, readout, trigram, scales)
    firsts = moments[:8]
    seconds = moments[8:]
    bits = index_bits()
    seq_size, dp_size = lax.axis_size("seq"), lax.axis_size("dp")
    devices = seq_size * dp_size
    held, piece = tokens.shape
    length = piece * seq_size
    sequences = held * dp_size
    members = devices // sequences
    vocabulary, share = embedding.shape
    features = share * devices
    hidden_size = expansion.shape[2]
    rows = length // members
    shorts = rows // 3
    member_bits = [("dp", b) for b in reversed(bits_of("dp")) if b < members]
    member = lax.axis_index("dp") % members
    group = (lax.axis_index("seq") * dp_size + lax.axis_index("dp")) // members

    integers = jnp.stack(
        [tokens, next_targets, triple_targets.reshape(held, piece), loss_mask]
    ).astype(jnp.bfloat16)
    integers = integers.reshape(share, -1)
    integer_width = integers.shape[1]
    integer_room = -(-integer_width // 128) * 128
    down_low = jnp.swapaxes(lowered(contraction), 1, 2)
    attention_low, projection_low, expansion_low = map(lowered, (attention, projection, expansion))
    stages = stages_of(bits)

    def packed(parts):
        return jnp.concatenate(parts, axis=1)[None]

    first_parts = [
        pad_columns(integers, integer_room),
        pad_columns(lowered(scales).T, 128),
        lowered(embedding).T,
        attention_low[0],
    ]
    second_parts = [projection_low[0], expansion_low[0], down_low[0]]
    third_parts = [
        attention_low[1],
        projection_low[1],
        expansion_low[1],
        down_low[1],
        lowered(trigram),
        lowered(readout),
    ]
    third = lax.all_gather(jnp.concatenate(third_parts, axis=1), ("seq", "dp"), axis=0, tiled=True)
    first, second = packed(first_parts), packed(second_parts)
    behind = None
    for stage in reversed(stages):
        first = stage_blocks(first, stage)
        if behind is not None:
            second = stage_blocks(second, behind)
            terms = together(*first, *second)
            first, second = terms[: len(first)], jnp.concatenate(terms[len(first) :])
        behind = stage
        if stage is not stages[0]:
            first, second = together(jnp.concatenate(first), second)
    first_other = [swapped(piece, bits[-1]) for piece in first]
    second = stage_blocks(second, behind)
    all_integers, scale_columns, embed_columns, attend_zero = merge_blocks(
        first, first_other, [part.shape[1] for part in first_parts], bits
    )
    project_one_at = 3 * features
    expand_one_at = 4 * features
    down_one_at = expand_one_at + hidden_size
    tables_at = down_one_at + hidden_size
    scale_rows = scale_columns[:, :6].astype(jnp.float32).T
    all_integers = all_integers[:, :integer_width].reshape(
        seq_size, dp_size, 4, held, piece
    )
    mask_total = jnp.sum(all_integers[:, :, 3].astype(jnp.float32))
    inverse_total = 1.0 / jnp.maximum(mask_total, 1.0)
    sequence = lax.dynamic_slice(
        all_integers,
        (0, group // held, 0, group % held, 0),
        (seq_size, 1, 4, 1, piece),
    )
    sequence = jnp.swapaxes(sequence.reshape(seq_size, 4, piece), 0, 1).reshape(4, length)
    own = lax.dynamic_slice_in_dim(sequence, member * rows, rows, 1).astype(jnp.int32)
    sequence_tokens = sequence[0].astype(jnp.int32)
    own_tokens = own[0]
    main_columns = own[1:4:2].astype(jnp.float32)
    triple_columns = jnp.concatenate(
        [own[2].reshape(shorts, 3), own[3].reshape(shorts, 3)], 1
    ).T.astype(jnp.float32)

    letters = jnp.arange(vocabulary, dtype=jnp.int32)
    is_token = (own_tokens[:, None] == letters).astype(jnp.bfloat16)
    place = member * rows + jnp.arange(rows, dtype=jnp.int32)
    earlier = (jnp.arange(length, dtype=jnp.int32)[None, :] <= place[:, None]).astype(jnp.bfloat16)
    counts = contract(
        (sequence_tokens[:, None] == letters).astype(jnp.bfloat16), earlier, "tv,rt->vr"
    )
    table = embed_columns.astype(jnp.float32).T
    table_inverse = norm_scale(table)
    table_normed = lowered(table * table_inverse * scale_rows[0])
    table_qkv = lowered(contract(table_normed, attend_zero, "vd,dc->vc"))
    queries = lowered(contract(is_token, table_qkv[:, :features], "rv,vc->rc"))
    counts, main_columns, triple_columns, mask_total, scale_rows = together(
        counts, main_columns, triple_columns, mask_total, scale_rows
    )
    mixed_low, shares = weighted_attention(queries, table_qkv, counts)
    second_other = [swapped(piece, bits[-1]) for piece in second[:-1]]
    mixed_low, last_piece = together(mixed_low, second[-1])
    second = [*second[:-1], last_piece]
    second_other.append(swapped(last_piece, bits[-1]))
    project_zero, expand_zero, down_zero = merge_blocks(
        second, second_other, [part.shape[1] for part in second_parts], bits
    )
    first_stream, normed_zero, hidden, last = first_layer_end(
        is_token,
        embed_columns,
        mixed_low,
        project_zero,
        expand_zero,
        down_zero,
        scale_rows[1:2],
    )

    normed_other = swapped(normed_zero, bits[-1])

    along = [(i, i + 1) for i in range(dp_size - 1) if (i + 1) % members]
    back = [(i + 1, i) for i, _ in along]
    previous = lax.ppermute(last, "dp", along)
    pooled, pooled_normed, short_queries, pairs = pooled_rows(
        first_stream, previous, third, scale_rows[2:3], shorts
    )
    pairs = stage_blocks(pairs, member_bits)
    (
        loss_local,
        merged_grad,
        table_sent,
        table_kept,
        short_mixed_low,
        short_hidden,
        short_normed,
        short_grad,
        short_low,
        short_shares,
        head_scales,
    ) = upper_layer(
        jnp.stack([own_bit(bits[-1]), member]),
        mask_total,
        short_queries,
        pairs,
        pooled,
        first_stream,
        scale_rows[3:6],
        third,
        (project_one_at, expand_one_at, down_one_at, tables_at),
        hidden_size,
        vocabulary,
        main_columns,
        triple_columns,
        share,
    )

    bit = own_bit(bits[-1])
    none = jnp.zeros((8, features), jnp.float32)
    upper, grad, other_grad, gradient = feed_back(
        short_grad,
        none,
        [swapped(short_low, bits[-1])],
        none,
        short_normed,
        swapped(short_normed, bits[-1]),
        (third, expand_one_at),
        (third, down_one_at),
        hidden_size,
        upper_steps,
        stages[0],
        bit,
        share,
    )
    grad, other_grad, gradient, *upper = together(grad, other_grad, gradient, *upper)
    upper = stage_sums(upper, stages[0])
    count = len(upper)
    short_hidden_low, short_hidden_grad, query_grad, pair_grads, feed_one_scale = upper_back(
        grad,
        swapped(other_grad, bits[-1]),
        short_hidden,
        gradient,
        scale_rows[3:4],
        third,
        project_one_at,
        short_queries,
        short_shares,
        pairs,
    )
    pair_grads = stage_sums(pair_grads, member_bits)
    *middle, rows_grad, rows_left, rows_right, returned, attend_one_scale = middle_gradients(
        bits,
        query_grad,
        pair_grads,
        pooled_normed,
        short_mixed_low,
        short_hidden_low,
        pooled,
        short_hidden_grad,
        merged_grad,
        third,
        scale_rows[2:3],
        share,
    )

    rows_left, rows_right = swapped(rows_left, bits[-1]), swapped(rows_right, bits[-1])
    middle = [[middle[4 + k], swapped(middle[k], bits[-1])] for k in range(4)]
    tables = [table_kept, swapped(table_sent, bits[-1])]
    middle = add_and_split([tables, *middle], stages[0])
    after_next = [(i + 2, i) for i in range(dp_size - 2) if i % members < members - 2]
    if after_next:
        later = lax.ppermute(returned, "dp", after_next)
    else:
        later = jnp.zeros_like(returned)
    other_back = jnp.where(member % 2 == 1, returned, later)
    returned = lax.ppermute(returned, "dp", back)
    rows_grad, rows_left, rows_right, returned, other_back, *terms = together(
        rows_grad, rows_left, rows_right, returned, other_back, *middle, *upper
    )
    middle, upper = stage_sums(terms[:count], stages[0]), terms[count:]
    fed, grad, other_grad, gradient = feed_back(
        rows_grad,
        returned,
        [rows_left, rows_right],
        other_back,
        normed_zero,
        normed_other,
        (expand_zero, 0),
        (down_zero, 0),
        hidden_size,
        feed_steps,
        stages[0],
        bit,
        share,
    )
    grad, other_grad, gradient, *terms = together(grad, other_grad, gradient, *fed, *middle)
    fed, middle = stage_sums(terms[:count], stages[0]), terms[count:]
    came = swapped(other_grad, bits[-1])
    came, *upper = together(came, *add_and_split([upper, middle], stages[1]))
    upper = stage_sums(upper, stages[1])
    lower = lower_gradients(
        own_bit(bits[-1]).reshape(1),
        grad,
        came,
        hidden,
        gradient,
        scale_rows[1:2],
        project_zero,
        queries,
        table_qkv,
        shares,
        is_token,
        mixed_low,
        embed_columns,
        attend_zero,
        scale_rows[0:1],
        attend_one_scale,
        feed_one_scale,
        head_scales,
        share,
    )

    *upper, later = upper
    sent, kept, *terms = together(*lower, *fed, *upper)
    fed, upper = terms[:count], terms[count:]
    lower = [kept, swapped(sent, bits[-1])]
    lower, *fed = together(tuple(add_and_split([lower], stages[0], False)), *fed)
    lower = stage_sums(lower, stages[0])
    fed = stage_sums(add_and_split([fed], stages[1]), stages[1])
    terms = together(*fed, *lower, later)
    upper, fed = [*upper, terms[-1]], terms[: len(fed)]
    lower = stage_sums(add_and_split([terms[len(fed) : -1]], stages[1]), stages[1])
    groups = (upper, fed, lower)
    for stage in stages[2:]:
        groups = [stage_sums(add_and_split([terms], stage), stage) for terms in groups]
    both = 2 * hidden_size
    upper, fed, lower = groups
    upper_rest, upper_mine, upper_other, square = add_and_square(
        bit, loss_local, [], upper, upper_steps, both
    )
    fed_mine, fed_other, square = add_and_square(
        bit, loss_local, [square], fed, feed_steps, both
    )
    upper_came, fed_came = swapped(upper_other, bits[-1]), swapped(fed_other, bits[-1])
    lower_sum, totals = add_and_square(bit, loss_local, [square], lower, 0, 0)
    for stage in [[bits[-1]], stages[0]]:
        totals = sum(stage_sums([totals] * (1 << len(stage)), stage))
    for stage in stages[1:]:
        totals = sum(stage_sums([totals] * (1 << len(stage)), stage))
    def fed_at(group, kind, steps):
        width = hidden_size // (2 * steps)
        return [
            ((group, half), (2 * j + kind) * width, (half * steps + j) * width, width)
            for half in range(2)
            for j in range(steps)
        ]

    groups = [upper_rest, lower_sum, upper_mine, upper_came, fed_mine, fed_came]
    scale_at = 4 * features + vocabulary
    groups.append(lower_sum[:, scale_at : scale_at + 6].T)
    attend_at = 4 * vocabulary
    layout = (
        ([(1, 4 * features, 0, vocabulary)],),
        ([(1, features, 0, 3 * features)], [(0, attend_at, 0, 3 * features)]),
        ([(1, 0, 0, features)], [(0, attend_at + 3 * features, 0, features)]),
        (fed_at(4, 1, feed_steps), fed_at(2, 1, upper_steps)),
        (fed_at(4, 0, feed_steps), fed_at(2, 0, upper_steps)),
        ([(0, 0, 0, vocabulary)],),
        ([(0, vocabulary, 0, 3 * vocabulary)],),
        ([(6, 0, 0, share)],),
    )

    def turned(arrays):
        embed, attend, project, expand, down, *rest = arrays
        return (embed.T, attend, project, expand, jnp.swapaxes(down, 1, 2), *rest)

    late = lax.optimization_barrier(
        (turned(masters), turned(firsts), turned(seconds), lower[0])
    )
    loss_total, norm_value, *results = adam_all(
        layout, bit, totals, groups, *late[:3]
    )
    return (
        loss_total.reshape(()),
        mask_total,
        norm_value.reshape(()),
        *turned(results[:8]),
        *turned(results[8:16]),
        *turned(results[16:]),
    )


def solution(mesh):
    weight_specs = (
        P(None, ("seq", "dp")),
        P(None, ("seq", "dp"), None),
        P(None, ("seq", "dp"), None),
        P(None, ("seq", "dp"), None),
        P(None, None, ("seq", "dp")),
        P(("seq", "dp"), None),
        P(("seq", "dp"), None),
        P(None, ("seq", "dp")),
    )
    in_specs = (
        P("dp", "seq"),
        P("dp", "seq"),
        P("dp", "seq", None),
        P("dp", "seq"),
    ) + weight_specs * 3
    out_specs = (P(), P(), P()) + weight_specs * 3
    return jax.shard_map(local, mesh=mesh, in_specs=in_specs, out_specs=out_specs, check_vma=False)
```

```python
import functools

import jax
import jax.numpy as jnp
from jax import lax
from jax.experimental import pallas as pl
from jax.experimental.pallas import tpu as pltpu
from jax.sharding import PartitionSpec as P

HEADS = 8
STEP = 10


norm_epsilon = 1e-06
trigram_share = 0.5
clip_limit = 0.1
beta_first = 0.9
beta_second = 0.95
adam_epsilon = 1e-08
learning_rates = (0.6, 0.05, 0.2, 0.05, 0.03, 0.05, 0.05, 0.6)
weight_decays = (0.0, 0.1, 0.1, 0.1, 0.1, 0.1, 0.1, 0.0)
megabyte = 1024 * 1024
lanes = 128


def lowered(array):
    return array.astype(jnp.bfloat16)


def contract(left, right, form):
    return jnp.einsum(form, left, right, preferred_element_type=jnp.float32)


def bits_of(axis):
    return [1 << k for k in range((lax.axis_size(axis) - 1).bit_length())]


def index_bits():
    return [("seq", b) for b in reversed(bits_of("seq"))] + [
        ("dp", b) for b in reversed(bits_of("dp"))
    ]


def own_bit(step):
    axis, weight = step
    return (lax.axis_index(axis) // weight) % 2


def swapped(x, step):
    axis, weight = step
    return lax.ppermute(x, axis, [(i, i ^ weight) for i in range(lax.axis_size(axis))])


def stages_of(bits):
    rest = bits[:-1]
    return [rest[max(0, end - 2) : end] for end in range(len(rest), 0, -2)]


def exchanged(x, steps):
    masks = {"seq": 0, "dp": 0}
    for axis, weight in steps:
        masks[axis] |= weight
    if not masks["seq"]:
        pairs = [(i, i ^ masks["dp"]) for i in range(lax.axis_size("dp"))]
        return lax.ppermute(x, "dp", pairs)
    if not masks["dp"]:
        pairs = [(i, i ^ masks["seq"]) for i in range(lax.axis_size("seq"))]
        return lax.ppermute(x, "seq", pairs)
    width = lax.axis_size("dp")
    pairs = [
        (i * width + j, (i ^ masks["seq"]) * width + (j ^ masks["dp"]))
        for i in range(lax.axis_size("seq"))
        for j in range(width)
    ]
    return lax.ppermute(x, ("seq", "dp"), pairs)


def chosen_steps(stage, number):
    return [step for at, step in enumerate(stage) if number >> (len(stage) - 1 - at) & 1]


def own_number(stage):
    number = jnp.int32(0)
    for step in stage:
        number = 2 * number + own_bit(step)
    return number


def stage_blocks(x, stage):
    return [x] + [exchanged(x, chosen_steps(stage, m)) for m in range(1, 1 << len(stage))]


def merge_kernel(widths, pieces, number_ref, *refs):
    mine, others, outs = refs[:pieces], refs[pieces : 2 * pieces], refs[2 * pieces :]
    bit, number = number_ref[0], number_ref[1]
    for piece in range(pieces):
        start = 0
        at = pl.ds(number ^ piece, 1)
        for width, out in zip(widths, outs):
            span = slice(start, start + width)
            out[at, pl.ds(bit, 1)] = mine[piece][:, :, span][None]
            out[at, pl.ds(1 - bit, 1)] = others[piece][:, :, span][None]
            start += width


def merge_blocks(mine, others, widths, bits):
    blocks, share, width = mine[0].shape
    pieces = len(mine)
    stages = stages_of(bits)
    block = jnp.arange(blocks, dtype=jnp.int32)
    place = jnp.zeros((blocks,), jnp.int32)
    low = 0
    for stage in stages[1:]:
        high = len(bits) - 1 - len(stages[0]) - low - len(stage)
        number = (block >> high) % (1 << len(stage)) ^ own_number(stage)
        place = place + (number << low)
        low += len(stage)
    numbers = jnp.concatenate(
        [jnp.stack([own_bit(bits[-1]), own_number(stages[0])]), place]
    )
    taken = pl.BlockSpec((1, share, width), lambda i, numbers: (i, 0, 0))
    outs = pl.pallas_call(
        functools.partial(merge_kernel, widths, pieces),
        grid_spec=pltpu.PrefetchScalarGridSpec(
            num_scalar_prefetch=1,
            grid=(blocks,),
            in_specs=[taken] * (2 * pieces),
            out_specs=[
                pl.BlockSpec(
                    (pieces, 2, share, w), lambda i, numbers: (numbers[2 + i], 0, 0, 0)
                )
                for w in widths
            ],
        ),
        out_shape=[
            pltpu.HBM((pieces * blocks, 2, share, w), mine[0].dtype) for w in widths
        ],
        compiler_params=pltpu.CompilerParams(vmem_limit_bytes=12 * megabyte),
        cost_estimate=cost(0, 8 * pieces * blocks * share * width),
    )(numbers, *[in_hbm(x) for x in mine], *others)
    return [out.reshape(2 * pieces * blocks * share, out.shape[-1]) for out in outs]


def together(*arrays):
    return lax.optimization_barrier(arrays)


def whole_in_vmem(count):
    return [pl.BlockSpec(memory_space=pltpu.VMEM)] * count


def in_hbm(array):
    return pltpu.with_memory_space_constraint(array, pltpu.HBM)


def cost(flops, moved, exponentials=0):
    return pl.CostEstimate(
        flops=int(flops), bytes_accessed=int(moved), transcendentals=int(exponentials)
    )


def halves(product, bit):
    low, high = product[:, 0], product[:, 1]
    return jnp.where(bit == 0, high, low), jnp.where(bit == 0, low, high)


def by_core(product, share):
    return lowered(product).reshape(-1, 2, share, product.shape[-1])


def split_kernel(widths, summands, pieces, number_ref, *refs):
    sources, outs = refs[: len(widths) * summands], refs[len(widths) * summands :]
    number = number_ref[0]
    start = 0
    for at, width in enumerate(widths):
        terms = sources[at * summands : (at + 1) * summands]
        for m in range(pieces):
            place = pl.ds(number ^ m, 1)
            total = terms[0][:, place].astype(jnp.float32)
            for term in terms[1:]:
                total = total + term[:, place].astype(jnp.float32)
            outs[m][:, :, start : start + width] = lowered(total)[:, 0]
        start += width


def add_and_split(sources, stage, settled=True):
    blocks, share, _ = sources[0][0].shape
    pieces = 1 << len(stage)
    widths = [terms[0].shape[-1] for terms in sources]
    total = sum(widths)
    arrays = []
    for terms in sources:
        for at, term in enumerate(terms):
            term = term.reshape(blocks // pieces, pieces, share, term.shape[-1])
            stays = settled and (at == 0 or len(sources) > 2)
            arrays.append(in_hbm(term) if stays else term)
    return pl.pallas_call(
        functools.partial(split_kernel, widths, len(sources[0]), pieces),
        grid_spec=pltpu.PrefetchScalarGridSpec(
            num_scalar_prefetch=1,
            grid=(blocks // pieces,),
            in_specs=[
                pl.BlockSpec((1, *x.shape[1:]), lambda i, number: (i, 0, 0, 0)) for x in arrays
            ],
            out_specs=[pl.BlockSpec((1, share, total), lambda i, number: (i, 0, 0))] * pieces,
        ),
        out_shape=[jax.ShapeDtypeStruct((blocks // pieces, share, total), jnp.bfloat16)] * pieces,
        compiler_params=pltpu.CompilerParams(vmem_limit_bytes=16 * megabyte),
        cost_estimate=cost(1, 1),
    )(own_number(stage).reshape(1), *arrays)


def add_and_square_kernel(earlier, terms_count, steps, both, bit_ref, loss_ref, *refs):
    befores, refs = refs[:earlier], refs[earlier:]
    terms, outs = refs[:terms_count], list(refs[terms_count:])
    total = terms[0][...].astype(jnp.float32)
    for term in terms[1:]:
        total = total + term[...].astype(jnp.float32)
    if total.shape[1] > both:
        outs.pop(0)[...] = total[:, both:]
    if both:
        mine_ref, other_ref = outs[:2]
        width = both // (2 * steps)
        for step in range(steps):
            here = slice(step * width, (step + 1) * width)
            first = total[:, 2 * step * width : (2 * step + 1) * width]
            second = total[:, (2 * step + 1) * width : (2 * step + 2) * width]
            mine_ref[:, here] = jnp.where(bit_ref[0, 0] == 0, first, second)
            other_ref[:, here] = jnp.where(bit_ref[0, 0] == 0, second, first)
    square_ref = outs[-1]
    share = total.shape[0]
    squares = jnp.zeros((share, lanes), jnp.float32)
    for before in befores:
        squares = squares + before[0:share]
    for start in range(0, total.shape[1], lanes):
        piece = total[:, start : start + lanes]
        squares = squares + piece * piece
    square_ref[0:share] = squares
    square_ref[share:] = jnp.broadcast_to(loss_ref[...], (8, lanes))


def add_and_square(bit, loss, befores, terms, steps, both):
    share, width = terms[0].shape[-2:]
    shapes = [(share, width - both)] if width > both else []
    shapes += [(share, both // 2)] * 2 if both else []
    shapes += [(share + 8, lanes)]
    return pl.pallas_call(
        functools.partial(
            add_and_square_kernel, len(befores), len(terms), steps, both
        ),
        in_specs=[pl.BlockSpec(memory_space=pltpu.SMEM)]
        + whole_in_vmem(1 + len(befores) + len(terms)),
        out_specs=whole_in_vmem(len(shapes)),
        out_shape=[jax.ShapeDtypeStruct(shape, jnp.float32) for shape in shapes],
        compiler_params=pltpu.CompilerParams(vmem_limit_bytes=8 * megabyte),
        cost_estimate=cost(3 * share * width, 12 * share * width),
    )(bit.reshape(1, 1), loss, *befores, *[term.reshape(share, width) for term in terms])


def stage_sums(pieces, stage):
    return [pieces[0]] + [
        exchanged(pieces[m], chosen_steps(stage, m)) for m in range(1, 1 << len(stage))
    ]


def norm_scale(stream):
    return lax.rsqrt(jnp.mean(stream * stream, axis=-1, keepdims=True) + norm_epsilon)


def norm_back(stream, inverse, scaling, gradient):
    unit = stream * inverse
    scaled = gradient * scaling
    scaling_grad = jnp.sum(gradient * unit, axis=0)
    stream_grad = inverse * (scaled - unit * jnp.mean(scaled * unit, axis=-1, keepdims=True))
    return stream_grad, scaling_grad


def times(left, right, left_side=1, right_side=0):
    return lax.dot_general(
        left, right, (((left_side,), (right_side,)), ((), ())), preferred_element_type=jnp.float32
    )


def exact_times(chooser, right, left_side=1, right_side=0):
    chooser = lowered(chooser)
    total = None
    for _ in range(3):
        part = lowered(right)
        product = times(chooser, part, left_side, right_side)
        total = product if total is None else total + product
        right = right - part.astype(jnp.float32)
    return total


def head_groups(features):
    depth = features // HEADS
    together = max(1, lanes // depth)
    return depth, [
        (first * depth, together * depth, range(first, first + together))
        for first in range(0, HEADS, together)
    ]


def own_lanes(width, depth, at):
    lane = lax.broadcasted_iota(jnp.int32, (1, width), 1)
    return (lane >= at * depth) & (lane < (at + 1) * depth)


def attend(queries, key_ref, value_ref, counts, share_ref):
    features = queries.shape[1]
    depth, groups = head_groups(features)
    queries = queries * jnp.asarray(depth ** (-0.5), queries.dtype)
    turned_values = value_ref[...].T
    mixed = []
    for start, width, places in groups:
        span = slice(start, start + width)
        keys = key_ref[:, span]
        for at, place in enumerate(places):
            own = own_lanes(width, depth, at)
            scores = times(jnp.where(own, keys, jnp.zeros_like(keys)), queries[:, span], 1, 1)
            scores = jnp.where(counts > 0.0, scores, -1e30)
            exponent = counts * jnp.exp(scores - jnp.max(scores, axis=0, keepdims=True))
            shares = lowered(exponent * (1.0 / jnp.sum(exponent, axis=0, keepdims=True)))
            share_ref[place] = shares
            here = slice(start + at * depth, start + (at + 1) * depth)
            mixed.append(lowered(times(turned_values[here], shares)))
    return jnp.concatenate(mixed, axis=0)


def attend_back(queries, key_ref, value_ref, share_ref, gradient, key_out, value_out):
    features = queries.shape[1]
    depth, groups = head_groups(features)
    scaled = depth ** (-0.5)
    turned_keys = key_ref[...].T
    query_grads = []
    for start, width, places in groups:
        span = slice(start, start + width)
        values = value_ref[:, span]
        key_sum = value_sum = None
        for at, place in enumerate(places):
            own = own_lanes(width, depth, at)
            low = share_ref[place]
            shares = low.astype(jnp.float32)
            share_grad = times(
                jnp.where(own, values, jnp.zeros_like(values)), gradient[:, span], 1, 1
            )
            dots = jnp.sum(shares * share_grad, axis=0, keepdims=True)
            score_grad = lowered(shares * (share_grad - dots))
            here = slice(start + at * depth, start + (at + 1) * depth)
            query_grads.append(lowered(times(turned_keys[here], score_grad) * scaled))
            key_part = times(score_grad, queries[:, span])
            value_part = times(low, gradient[:, span])
            if key_sum is None:
                key_sum, value_sum = key_part, value_part
            else:
                key_sum = jnp.where(own, key_part, key_sum)
                value_sum = jnp.where(own, value_part, value_sum)
        key_out[:, span] = lowered(key_sum * scaled)
        value_out[:, span] = lowered(value_sum)
    return jnp.concatenate(query_grads, axis=0)


def attend_kernel(query_ref, key_ref, value_ref, count_ref, mixed_ref, share_ref):
    mixed_ref[...] = attend(
        query_ref[...], key_ref, value_ref, count_ref[...], share_ref
    ).T


def weighted_attention(queries, table_qkv, counts):
    rows, features = queries.shape
    entries = table_qkv.shape[0]
    return pl.pallas_call(
        attend_kernel,
        grid=(1,),
        in_specs=[
            pl.BlockSpec((rows, features), lambda i: (0, 0)),
            pl.BlockSpec((entries, features), lambda i: (0, 1)),
            pl.BlockSpec((entries, features), lambda i: (0, 2)),
            pl.BlockSpec((entries, rows), lambda i: (0, 0)),
        ],
        out_specs=[
            pl.BlockSpec((rows, features), lambda i: (0, 0)),
            pl.BlockSpec((HEADS, entries, rows), lambda i: (0, 0, 0)),
        ],
        out_shape=[
            jax.ShapeDtypeStruct((rows, features), jnp.bfloat16),
            pltpu.HBM((HEADS, entries, rows), jnp.bfloat16),
        ],
        compiler_params=pltpu.CompilerParams(vmem_limit_bytes=24 * megabyte),
        cost_estimate=cost(
            4 * rows * entries * features,
            4 * rows * features + 4 * entries * features + (2 * HEADS + 4) * rows * entries,
            HEADS * rows * entries,
        ),
    )(queries, table_qkv, table_qkv, counts)


gelu_rate = 0.7978845608
gelu_cube = 0.044715


feed_steps = 2
feed_parts = 2
upper_steps = 2


def gelu_terms(before):
    square = before * before
    bent = jnp.tanh(before * (gelu_rate + gelu_rate * gelu_cube * square))
    half = 0.5 + 0.5 * bent
    return square, bent, half


def feed_forward_part(normed, in_ref, down_ref):
    width = in_ref.shape[1] // feed_parts
    total = None
    for part in range(feed_parts):
        span = slice(part * width, (part + 1) * width)
        before = times(normed, in_ref[:, span])
        _, _, half = gelu_terms(before)
        product = times(lowered(before * half), down_ref[:, span], 1, 1)
        total = product if total is None else total + product
    return total


def feed_forward_kernel(
    token_ref,
    embed_ref,
    mixed_ref,
    project_ref,
    in_ref,
    down_ref,
    scale_ref,
    result_ref,
    normed_ref,
    hidden_ref,
    last_ref,
):
    @pl.when(pl.program_id(0) == 0)
    def _():
        hidden = times(token_ref[...], embed_ref[...], 1, 1) + times(
            mixed_ref[...], project_ref[...]
        )
        hidden_ref[...] = hidden
        normed_ref[...] = lowered(hidden * norm_scale(hidden) * scale_ref[...])
        result_ref[...] = hidden

    result_ref[...] += feed_forward_part(normed_ref[...], in_ref, down_ref)
    last_ref[...] = result_ref[result_ref.shape[0] - last_ref.shape[0] :]


def first_layer_end(is_token, embed_columns, mixed_low, project, in_weight, down_weight, scaling):
    rows, features = mixed_low.shape
    hidden_size = in_weight.shape[1]
    width = hidden_size // feed_steps

    def whole(shape):
        return pl.BlockSpec(shape, lambda j: (0, 0))

    chunk = pl.BlockSpec((features, width), lambda j: (0, j))
    return pl.pallas_call(
        feed_forward_kernel,
        grid=(feed_steps,),
        in_specs=[
            whole(is_token.shape),
            whole(embed_columns.shape),
            whole(mixed_low.shape),
            whole(project.shape),
            chunk,
            chunk,
            whole(scaling.shape),
        ],
        out_specs=[whole((rows, features))] * 3 + [whole((8, features))],
        out_shape=[
            pltpu.HBM((rows, features), jnp.float32),
            pltpu.HBM((rows, features), jnp.bfloat16),
            pltpu.HBM((rows, features), jnp.float32),
            jax.ShapeDtypeStruct((8, features), jnp.float32),
        ],
        compiler_params=pltpu.CompilerParams(vmem_limit_bytes=20 * megabyte),
        cost_estimate=cost(
            4 * rows * features * hidden_size,
            4 * features * hidden_size + 14 * rows * features,
            rows * hidden_size,
        ),
    )(
        in_hbm(is_token),
        in_hbm(embed_columns),
        mixed_low,
        in_hbm(project),
        in_hbm(in_weight),
        in_hbm(down_weight),
        scaling,
    )


def pool_kernel(
    first_ref, last_ref, attend_ref, scale_ref, pooled_ref, normed_ref, query_ref, pair_ref
):
    rows, shorts = first_ref.shape[0], pooled_ref.shape[0]
    gap = (
        lax.broadcasted_iota(jnp.int32, (shorts, rows), 1)
        + 2
        - 3 * lax.broadcasted_iota(jnp.int32, (shorts, rows), 0)
    )
    pooling = jnp.where((gap >= 0) & (gap < 3), 1.0, 0.0)
    pooled = exact_times(pooling, first_ref[...])
    row = lax.broadcasted_iota(jnp.int32, (shorts, 1), 0)
    pooled = (
        pooled + jnp.where(row == 0, jnp.sum(last_ref[6:8], axis=0, keepdims=True), 0.0)
    ) * (1.0 / 3.0)
    pooled_ref[...] = pooled
    normed = lowered(pooled * norm_scale(pooled) * scale_ref[...])
    normed_ref[...] = normed
    features = first_ref.shape[1]
    query_ref[...] = lowered(times(normed, attend_ref[:, :features]))
    pair_ref[...] = lowered(times(normed, attend_ref[:, features:]))


def pooled_rows(first, previous, weights, scaling, shorts):
    rows, features = first.shape

    def whole(shape):
        return pl.BlockSpec(shape, lambda j: (0, 0))

    return pl.pallas_call(
        pool_kernel,
        grid=(1,),
        in_specs=[
            whole(first.shape),
            whole(previous.shape),
            whole((features, 3 * features)),
            whole(scaling.shape),
        ],
        out_specs=[
            whole((shorts, features)),
            whole((shorts, features)),
            whole((shorts, features)),
            whole((shorts, 2 * features)),
        ],
        out_shape=[
            pltpu.HBM((shorts, features), jnp.float32),
            pltpu.HBM((shorts, features), jnp.bfloat16),
            pltpu.HBM((shorts, features), jnp.bfloat16),
            jax.ShapeDtypeStruct((shorts, 2 * features), jnp.bfloat16),
        ],
        compiler_params=pltpu.CompilerParams(vmem_limit_bytes=12 * megabyte),
        cost_estimate=cost(
            6 * shorts * features * features + 12 * rows * shorts * features,
            6 * features * features + 4 * rows * features,
        ),
    )(in_hbm(first), previous, in_hbm(weights), scaling)


def feed_back_part(normed, gradient, in_weight, down_weight, turned_gradient, turned_normed, store):
    before = times(normed, in_weight)
    square, bent, half = gelu_terms(before)
    slope = half + half * (1.0 - bent) * before * (
        gelu_rate + 3.0 * gelu_rate * gelu_cube * square
    )
    before_grad = lowered(times(gradient, down_weight) * slope)
    store(0, times(turned_gradient, lowered(before * half)))
    store(1, times(turned_normed, before_grad))
    return times(before_grad, in_weight, 1, 1)


def feed_back_kernel(share, pieces, number_ref, *refs):
    (
        above_ref,
        back_ref,
        other_back_ref,
        normed_ref,
        other_normed_ref,
        in_ref,
        down_ref,
        *outs,
        grad_out,
        other_grad_out,
        gradient_out,
        gradient_ref,
        all_normed,
        turned_gradient,
        turned_normed,
        normed_grad,
        product_ref,
    ) = refs
    other_gradients, outs = outs[:-pieces], outs[-pieces:]
    step = pl.program_id(0)
    number = number_ref[1]
    rows = above_ref.shape[0]

    @pl.when(step == 0)
    def _():
        row = lax.broadcasted_iota(jnp.int32, (rows, 1), 0)
        gradient = above_ref[...] + jnp.where(row >= rows - 2, back_ref[0:1], 0.0)
        gradient_out[...] = gradient
        gradient_ref[:rows] = lowered(gradient)
        start = 0
        for other in other_gradients:
            span = slice(start, start + other.shape[1])
            gradient_ref[rows:, span] = lowered(
                other[...].astype(jnp.float32)
                + jnp.where(row >= rows - 2, other_back_ref[0:1, span], 0.0)
            )
            start += other.shape[1]
        all_normed[:rows] = normed_ref[...]
        all_normed[rows:] = other_normed_ref[...]
        turned_gradient[...] = gradient_ref[...].T
        turned_normed[...] = all_normed[...].T
        normed_grad[...] = jnp.zeros_like(normed_grad)

    width = in_ref.shape[1]

    def store(place, product):
        product_ref[...] = lowered(product).reshape(product_ref.shape)
        for core in range(2):
            span = slice((2 * core + place) * width, (2 * core + place + 1) * width)
            for m in range(pieces):
                outs[m][:, :, span] = product_ref[:, pl.ds(number ^ m, 1), core][:, 0]

    normed_grad[...] += feed_back_part(
        all_normed[...],
        gradient_ref[...],
        in_ref[...],
        down_ref[...],
        turned_gradient[...],
        turned_normed[...],
        store,
    )

    @pl.when(step == pl.num_programs(0) - 1)
    def _():
        grad_out[...] = normed_grad[:rows]
        other_grad_out[...] = lowered(normed_grad[rows:])


def feed_back(
    above,
    back,
    other_gradients,
    other_back,
    normed,
    other_normed,
    in_weight,
    down_weight,
    hidden_size,
    steps,
    stage,
    bit,
    share,
):
    rows, features = above.shape
    width = hidden_size // (2 * steps)
    blocks = features // (2 * share)
    pieces = 1 << len(stage)
    far = blocks // pieces

    def whole(shape):
        return pl.BlockSpec(shape, lambda j, numbers: (0, 0))

    def chunk(start):
        return pl.BlockSpec(
            (features, width), lambda j, numbers: (0, start // width + numbers[0] * steps + j)
        )

    piece = pl.BlockSpec((far, share, 4 * width), lambda j, numbers: (0, 0, j))
    *results, grad, other_grad, gradient = pl.pallas_call(
        functools.partial(feed_back_kernel, share, pieces),
        grid_spec=pltpu.PrefetchScalarGridSpec(
            num_scalar_prefetch=1,
            grid=(steps,),
            in_specs=[
                whole(above.shape),
                whole(back.shape),
                whole(back.shape),
                whole(normed.shape),
                whole(normed.shape),
                chunk(in_weight[1]),
                chunk(down_weight[1]),
                *[whole(x.shape) for x in other_gradients],
            ],
            out_specs=[piece] * pieces + [whole(above.shape)] * 3,
            scratch_shapes=[
                pltpu.VMEM((2 * rows, features), jnp.bfloat16),
                pltpu.VMEM((2 * rows, features), jnp.bfloat16),
                pltpu.VMEM((features, 2 * rows), jnp.bfloat16),
                pltpu.VMEM((features, 2 * rows), jnp.bfloat16),
                pltpu.VMEM((2 * rows, features), jnp.float32),
                pltpu.VMEM((far, pieces, 2, share, width), jnp.bfloat16),
            ],
        ),
        out_shape=[pltpu.HBM((far, share, 2 * hidden_size), jnp.bfloat16)] * pieces
        + [
            jax.ShapeDtypeStruct(above.shape, jnp.float32),
            jax.ShapeDtypeStruct(above.shape, jnp.bfloat16),
            pltpu.HBM(above.shape, jnp.float32),
        ],
        compiler_params=pltpu.CompilerParams(vmem_limit_bytes=36 * megabyte),
        cost_estimate=cost(1, 1),
    )(
        jnp.stack([bit, own_number(stage)]),
        in_hbm(above),
        back,
        other_back,
        in_hbm(normed),
        other_normed,
        in_hbm(in_weight[0]),
        in_hbm(down_weight[0]),
        *other_gradients,
    )
    return results, grad, other_grad, gradient


def middle_kernel(
    share,
    members,
    bit_ref,
    query_ref,
    *refs,
):
    pair_refs, refs = refs[:members], refs[members:]
    (
        normed_ref,
        mixed_ref,
        low_ref,
        pooled_ref,
        hidden_grad_ref,
        above_ref,
        attend_ref,
        scale_ref,
        *outs,
        rows_out,
        left_out,
        right_out,
        back_out,
        scale_out,
    ) = refs
    sent_refs, kept_refs = outs[: len(outs) // 2], outs[len(outs) // 2 :]
    bit = bit_ref[0]
    features = query_ref.shape[1]
    pairs = pair_refs[0][...].astype(jnp.float32)
    for pair_ref in pair_refs[1:]:
        pairs = pairs + pair_ref[...].astype(jnp.float32)
    pairs = lowered(pairs)
    queries = query_ref[...]
    normed_grad = times(queries, attend_ref[:, :features], 1, 1) + times(
        pairs, attend_ref[:, features:], 1, 1
    )
    pooled = pooled_ref[...]
    pooled_grad, scaling_grad = norm_back(
        pooled, norm_scale(pooled), scale_ref[...], normed_grad
    )
    scale_out[...] = scaling_grad[None]
    pooled_grad = (pooled_grad + hidden_grad_ref[...]) * (1.0 / 3.0)
    back_out[...] = pooled_grad[0 : back_out.shape[0]]
    rows, shorts = rows_out.shape[0], pooled.shape[0]
    gap = (
        lax.broadcasted_iota(jnp.int32, (rows, shorts), 0)
        + 2
        - 3 * lax.broadcasted_iota(jnp.int32, (rows, shorts), 1)
    )
    spreading = jnp.where((gap >= 0) & (gap < 3), 1.0, 0.0)
    rows_grad = above_ref[...] + exact_times(spreading, pooled_grad)
    rows_out[...] = rows_grad
    left_out[...] = lowered(rows_grad[:, : features // 2])
    right_out[...] = lowered(rows_grad[:, features // 2 :])
    turned_normed = normed_ref[...].T
    products = (
        lambda: times(turned_normed, queries),
        lambda: times(turned_normed, pairs[:, :features]),
        lambda: times(turned_normed, pairs[:, features:]),
        lambda: times(mixed_ref[...], low_ref[...], 0, 0),
    )
    for product, sent_ref, kept_ref in zip(products, sent_refs, kept_refs):
        sent_ref[...], kept_ref[...] = halves(by_core(product(), share), bit)


def middle_gradients(
    bits,
    query_grad,
    pair_grads,
    normed,
    mixed_low,
    hidden_low,
    pooled,
    hidden_grad,
    above,
    weights,
    scaling,
    share,
):
    shorts, features = pooled.shape
    rows = above.shape[0]
    chips = features // (2 * share)

    def whole(shape):
        return pl.BlockSpec(shape, lambda j, bit: (0, 0))

    operands = [
        query_grad,
        *pair_grads,
        in_hbm(normed),
        in_hbm(mixed_low),
        hidden_low,
        in_hbm(pooled),
        hidden_grad,
        in_hbm(above),
        in_hbm(weights),
        scaling,
    ]
    specs = [whole(x.shape) for x in operands]
    specs[-2] = whole((features, 3 * features))
    buffer = pltpu.HBM((chips, share, features), jnp.bfloat16)
    piece = pl.BlockSpec((chips, share, features), lambda j, bit: (0, 0, 0))
    half = (rows, features // 2)
    return pl.pallas_call(
        functools.partial(middle_kernel, share, len(pair_grads)),
        grid_spec=pltpu.PrefetchScalarGridSpec(
            num_scalar_prefetch=1,
            grid=(1,),
            in_specs=specs,
            out_specs=[
                *[piece] * 8,
                whole(above.shape),
                whole(half),
                whole(half),
                whole((8, features)),
                whole((1, features)),
            ],
        ),
        out_shape=[
            *[buffer] * 8,
            pltpu.HBM(above.shape, jnp.float32),
            jax.ShapeDtypeStruct(half, jnp.bfloat16),
            jax.ShapeDtypeStruct(half, jnp.bfloat16),
            jax.ShapeDtypeStruct((8, features), jnp.float32),
            pltpu.HBM((1, features), jnp.float32),
        ],
        compiler_params=pltpu.CompilerParams(vmem_limit_bytes=24 * megabyte),
        cost_estimate=cost(1, 1),
    )(own_bit(bits[-1]).reshape(1), *operands)


def head_terms(stream, scaling, matrix, columns, factor):
    count = columns.shape[0] // 2
    columns = columns.T
    inverse = norm_scale(stream)
    normed_low = lowered(stream * inverse * scaling)
    logits = times(normed_low, matrix)
    vocabulary = logits.shape[1] // count
    letters = lax.broadcasted_iota(jnp.int32, (stream.shape[0], vocabulary), 1)
    gradients = []
    loss = None
    for place in range(count):
        some = logits[:, place * vocabulary : (place + 1) * vocabulary]
        highest = jnp.max(some, axis=-1, keepdims=True)
        exponent = jnp.exp(some - highest)
        denominator = jnp.sum(exponent, axis=-1, keepdims=True)
        matches = letters == columns[:, place : place + 1].astype(jnp.int32)
        picked = jnp.sum(jnp.where(matches, some, 0.0), axis=-1, keepdims=True)
        weight = columns[:, count + place : count + place + 1]
        term = weight * (highest + jnp.log(denominator) - picked)
        loss = term if loss is None else loss + term
        chance = exponent * (1.0 / denominator)
        gradients.append(lowered((chance - jnp.where(matches, 1.0, 0.0)) * (weight * factor)))
    logit_low = gradients[0] if len(gradients) == 1 else jnp.concatenate(gradients, axis=1)
    matrix_grad = times(normed_low, logit_low, 0, 0)
    stream_grad, scaling_grad = norm_back(
        stream, inverse, scaling, times(logit_low, matrix, 1, 1)
    )
    return jnp.sum(loss, axis=0, keepdims=True), stream_grad, scaling_grad, lowered(matrix_grad)


def heads_part(
    share,
    bit,
    total,
    first,
    short,
    scaling,
    readout,
    trigram,
    main_columns,
    triple_columns,
    sent_ref,
    kept_ref,
):
    inverse_total = 1.0 / jnp.maximum(total, 1.0)
    vocabulary = readout.shape[1]
    rows, shorts = first.shape[0], short.shape[0]
    gap = lax.broadcasted_iota(jnp.int32, (rows, shorts), 0) - 3 * lax.broadcasted_iota(
        jnp.int32, (rows, shorts), 1
    )
    thrice = jnp.where((gap >= 0) & (gap < 3), 1.0, 0.0)
    merged = first + exact_times(thrice, short)
    main_loss, merged_grad, main_scale, readout_grad = head_terms(
        merged, scaling[0:1], readout, main_columns, inverse_total
    )
    sent_ref[:, :, :vocabulary], kept_ref[:, :, :vocabulary] = halves(
        by_core(readout_grad, share), bit
    )
    extra_loss, short_grad, extra_scale, trigram_grad = head_terms(
        short, scaling[1:2], trigram, triple_columns, trigram_share * inverse_total
    )
    sent_ref[:, :, vocabulary:], kept_ref[:, :, vocabulary:] = halves(
        by_core(trigram_grad, share), bit
    )
    short_grad = short_grad + exact_times(thrice, merged_grad, 0, 0)
    loss = main_loss + trigram_share * extra_loss
    return loss, merged_grad, short_grad, main_scale[None], extra_scale[None]


def pair_rows(pair_refs, key_ref, value_ref):
    rows, both = pair_refs[0].shape
    for at, pair_ref in enumerate(pair_refs):
        here = slice(at * rows, (at + 1) * rows)
        key_ref[here], value_ref[here] = pair_ref[:, : both // 2], pair_ref[:, both // 2 :]


def upper_kernel(share, members, number_ref, total_ref, query_ref, *refs):
    pair_refs, refs = refs[:members], refs[members:]
    (
        pooled_ref,
        first_ref,
        scale_ref,
        project_ref,
        in_ref,
        down_ref,
        readout_ref,
        trigram_ref,
        main_ref,
        triple_ref,
        loss_ref,
        first_out,
        table_sent,
        table_kept,
        mixed_out,
        hidden_out,
        normed_out,
        gradient_out,
        low_out,
        share_out,
        scale_out,
        key_ref,
        value_ref,
        short_ref,
    ) = refs
    step = pl.program_id(0)
    bit, member = number_ref[0], number_ref[1]

    @pl.when(step == 0)
    def _():
        rows = query_ref.shape[0]
        row = lax.broadcasted_iota(jnp.int32, (rows, rows), 1)
        entry = lax.broadcasted_iota(jnp.int32, (rows, rows), 0)
        pair_rows(pair_refs, key_ref, value_ref)
        counts = [
            jnp.where(entry <= row + (member - (member ^ at)) * rows, 1.0, 0.0)
            for at in range(members)
        ]
        mixed = attend(
            query_ref[...], key_ref, value_ref, jnp.concatenate(counts, axis=0), share_out
        ).T
        mixed_out[...] = mixed
        hidden = pooled_ref[...] + times(mixed, project_ref[...])
        hidden_out[...] = hidden
        normed_out[...] = lowered(hidden * norm_scale(hidden) * scale_ref[0:1])
        short_ref[...] = hidden

    short_ref[...] += feed_forward_part(normed_out[...], in_ref, down_ref)

    @pl.when(step == pl.num_programs(0) - 1)
    def _():
        loss, merged_grad, short_grad, main_scale, extra_scale = heads_part(
            share,
            bit,
            total_ref[0, 0],
            first_ref[...],
            short_ref[...],
            scale_ref[1:3],
            readout_ref[...],
            trigram_ref[...],
            main_ref[...],
            triple_ref[...],
            table_sent,
            table_kept,
        )
        loss_ref[...] = loss
        first_out[...] = merged_grad
        gradient_out[...] = short_grad
        low_out[...] = lowered(short_grad)
        scale_out[0:1] = main_scale
        scale_out[1:2] = extra_scale


def upper_layer(
    numbers,
    mask_total,
    queries,
    pairs,
    pooled,
    first,
    scaling,
    weights,
    places,
    hidden_size,
    vocabulary,
    main_columns,
    triple_columns,
    share,
):
    shorts, features = pooled.shape
    rows = first.shape[0]
    members = len(pairs)
    entries = members * shorts
    steps = 1
    width = hidden_size // steps
    chips = features // (2 * share)
    project_at, in_at, down_at, tables_at = places

    def whole(shape, at=(0, 0)):
        return pl.BlockSpec(shape, lambda j, numbers: at)

    def chunk(start):
        return pl.BlockSpec((features, width), lambda j, numbers: (0, start // width + j))

    table_piece = pl.BlockSpec((chips, share, 4 * vocabulary), lambda j, numbers: (0, 0, 0))
    table_buffer = pltpu.HBM((chips, share, 4 * vocabulary), jnp.bfloat16)
    half = (entries, features)
    weights = in_hbm(weights)
    return pl.pallas_call(
        functools.partial(upper_kernel, share, members),
        grid_spec=pltpu.PrefetchScalarGridSpec(
            num_scalar_prefetch=1,
            grid=(steps,),
            in_specs=[
                pl.BlockSpec(memory_space=pltpu.SMEM),
                whole(queries.shape),
                *[whole(pair.shape) for pair in pairs],
                whole(pooled.shape),
                whole(first.shape),
                whole(scaling.shape),
                whole((features, features), (0, project_at // features)),
                chunk(in_at),
                chunk(down_at),
                whole((features, vocabulary), (0, tables_at // vocabulary + 3)),
                whole((features, 3 * vocabulary), (0, tables_at // (3 * vocabulary))),
                whole(main_columns.shape),
                whole(triple_columns.shape),
            ],
            out_specs=[
                whole((1, 1)),
                whole(first.shape),
                table_piece,
                table_piece,
                *[whole(pooled.shape)] * 5,
                pl.BlockSpec((HEADS, entries, shorts), lambda j, numbers: (0, 0, 0)),
                whole((2, features)),
            ],
            scratch_shapes=[
                pltpu.VMEM(half, jnp.bfloat16),
                pltpu.VMEM(half, jnp.bfloat16),
                pltpu.VMEM((shorts, features), jnp.float32),
            ],
        ),
        out_shape=[
            pltpu.HBM((1, 1), jnp.float32),
            pltpu.HBM((rows, features), jnp.float32),
            table_buffer,
            table_buffer,
            pltpu.HBM((shorts, features), jnp.bfloat16),
            pltpu.HBM((shorts, features), jnp.float32),
            jax.ShapeDtypeStruct((shorts, features), jnp.bfloat16),
            pltpu.HBM((shorts, features), jnp.float32),
            jax.ShapeDtypeStruct((shorts, features), jnp.bfloat16),
            pltpu.HBM((HEADS, entries, shorts), jnp.bfloat16),
            pltpu.HBM((2, features), jnp.float32),
        ],
        compiler_params=pltpu.CompilerParams(
            vmem_limit_bytes=(36 if entries <= 512 else 60) * megabyte
        ),
        cost_estimate=cost(
            6 * shorts * features * hidden_size + 6 * features * vocabulary * (rows + 3 * shorts),
            8 * features * hidden_size + 8 * rows * features,
            shorts * hidden_size,
        ),
    )(
        numbers,
        mask_total.reshape(1, 1),
        in_hbm(queries),
        in_hbm(pairs[0]),
        *pairs[1:],
        in_hbm(pooled),
        in_hbm(first),
        scaling,
        weights,
        weights,
        weights,
        weights,
        weights,
        main_columns,
        triple_columns,
    )


def upper_back_kernel(members, grad_ref, came_ref, hidden_ref, gradient_ref, *refs):
    scale_ref, project_ref, query_ref, share_ref, *refs = refs
    pair_refs, refs = refs[:members], refs[members:]
    low_out, hidden_out, query_out, *refs = refs
    pair_outs, refs = refs[:members], refs[members:]
    scale_out, key_ref, value_ref, key_out, value_out = refs
    pair_rows(pair_refs, key_ref, value_ref)
    hidden = hidden_ref[...]
    hidden_grad, scaling_grad = norm_back(
        hidden,
        norm_scale(hidden),
        scale_ref[...],
        grad_ref[...] + came_ref[...].astype(jnp.float32),
    )
    hidden_grad = hidden_grad + gradient_ref[...]
    hidden_low = lowered(hidden_grad)
    hidden_out[...] = hidden_grad
    low_out[...] = hidden_low
    scale_out[...] = scaling_grad[None]
    mixed_grad = lowered(times(hidden_low, project_ref[...], 1, 1))
    query_out[...] = attend_back(
        query_ref[...], key_ref, value_ref, share_ref, mixed_grad, key_out, value_out
    ).T
    rows, features = query_ref.shape
    for at, pair_out in enumerate(pair_outs):
        here = slice(at * rows, (at + 1) * rows)
        pair_out[:, :features], pair_out[:, features:] = key_out[here], value_out[here]


def upper_back(
    grad, came, hidden, gradient, scaling, weights, project_at, queries, shares, pairs
):
    shorts, features = hidden.shape
    members = len(pairs)
    half = (members * shorts, features)

    def whole(x):
        return pl.BlockSpec(x.shape, lambda j: (0,) * x.ndim)

    operands = [grad, came, hidden, gradient, scaling, weights, queries, shares, *pairs]
    specs = [whole(x) for x in operands]
    specs[5] = pl.BlockSpec((features, features), lambda j: (0, project_at // features))
    operands[2:4] = [in_hbm(hidden), in_hbm(gradient)]
    operands[5:] = [in_hbm(x) for x in operands[5:]]
    low, hidden_grad, query_grad, *pair_grads, scale_grad = pl.pallas_call(
        functools.partial(upper_back_kernel, members),
        grid=(1,),
        in_specs=specs,
        out_specs=[whole(hidden)] * 3 + [whole(pair) for pair in pairs] + [whole(scaling)],
        out_shape=[
            jax.ShapeDtypeStruct(hidden.shape, jnp.bfloat16),
            jax.ShapeDtypeStruct(hidden.shape, jnp.float32),
            jax.ShapeDtypeStruct(hidden.shape, jnp.bfloat16),
            *[jax.ShapeDtypeStruct(pair.shape, jnp.bfloat16) for pair in pairs],
            pltpu.HBM(scaling.shape, jnp.float32),
        ],
        scratch_shapes=[pltpu.VMEM(half, jnp.bfloat16)] * 4,
        compiler_params=pltpu.CompilerParams(
            vmem_limit_bytes=(20 if half[0] <= 512 else 60) * megabyte
        ),
        cost_estimate=cost(1, 1),
    )(*operands)
    return low, hidden_grad, query_grad, pair_grads, scale_grad


def lower_kernel(
    share,
    bit_ref,
    grad_ref,
    came_ref,
    hidden_ref,
    gradient_ref,
    feed_scale_ref,
    project_ref,
    query_ref,
    key_ref,
    value_ref,
    share_ref,
    token_ref,
    mixed_ref,
    table_ref,
    attend_ref,
    scale_ref,
    attend_one_ref,
    feed_one_ref,
    heads_ref,
    sent_ref,
    kept_ref,
    key_out,
    value_out,
):
    bit = bit_ref[0]
    features = grad_ref.shape[1]
    is_token = token_ref[...]
    hidden = hidden_ref[...]
    hidden_grad, feed_scale = norm_back(
        hidden,
        norm_scale(hidden),
        feed_scale_ref[...],
        grad_ref[...] + came_ref[...].astype(jnp.float32),
    )
    hidden_low = lowered(hidden_grad + gradient_ref[...])
    mixed_grad = lowered(times(hidden_low, project_ref[...], 1, 1))
    query_grad = attend_back(
        query_ref[...], key_ref, value_ref, share_ref, mixed_grad, key_out, value_out
    )
    query_grad = lowered(times(query_grad, is_token).T)
    table = table_ref[...].astype(jnp.float32).T
    inverse = norm_scale(table)
    turned_normed = lowered((table * inverse * scale_ref[...]).T)
    parts = (query_grad, key_out[...], value_out[...])
    normed_grad = None
    for place, part in enumerate(parts):
        span = slice(place * features, (place + 1) * features)
        product = times(part, attend_ref[:, span], 1, 1)
        normed_grad = product if normed_grad is None else normed_grad + product
    table_grad, scaling_grad = norm_back(table, inverse, scale_ref[...], normed_grad)
    table_grad = table_grad + times(is_token, hidden_low, 0, 0)
    known = (
        scaling_grad[None],
        feed_scale[None],
        attend_one_ref[...],
        feed_one_ref[...],
        heads_ref[...],
    )
    scale_rows = jnp.concatenate(
        [*known, jnp.zeros((lanes - 6, features), jnp.float32)], axis=0
    )
    products = (
        lambda: times(mixed_ref[...], hidden_low, 0, 0),
        *(lambda part=part: times(turned_normed, part) for part in parts),
        lambda: table_grad.T,
        lambda: scale_rows.T,
    )
    start = 0
    for product in products:
        product = product()
        span = slice(start, start + product.shape[1])
        sent_ref[:, :, span], kept_ref[:, :, span] = halves(by_core(product, share), bit)
        start += product.shape[1]


def lower_gradients(
    bit,
    grad,
    came,
    hidden,
    gradient,
    feed_scaling,
    project,
    queries,
    table_qkv,
    shares,
    is_token,
    mixed_low,
    embed_columns,
    attend,
    scaling,
    attend_one_scale,
    feed_one_scale,
    head_scales,
    share,
):
    rows, features = hidden.shape
    entries = table_qkv.shape[0]
    chips = features // (2 * share)
    width = 4 * features + entries + lanes

    def whole(x, at=(0, 0)):
        return pl.BlockSpec(x.shape, lambda j, bit: (0,) * x.ndim)

    def third(at):
        return pl.BlockSpec((entries, features), lambda j, bit: (0, at))

    operands = [
        grad,
        came,
        in_hbm(hidden),
        in_hbm(gradient),
        feed_scaling,
        project,
        queries,
        table_qkv,
        table_qkv,
        shares,
        is_token,
        mixed_low,
        embed_columns,
        attend,
        scaling,
        attend_one_scale,
        feed_one_scale,
        head_scales,
    ]
    specs = [whole(x) for x in operands]
    specs[7:9] = [third(1), third(2)]
    buffer = jax.ShapeDtypeStruct((chips, share, width), jnp.bfloat16)
    return pl.pallas_call(
        functools.partial(lower_kernel, share),
        grid_spec=pltpu.PrefetchScalarGridSpec(
            num_scalar_prefetch=1,
            grid=(1,),
            in_specs=specs,
            out_specs=[pl.BlockSpec((chips, share, width), lambda j, bit: (0, 0, 0))] * 2,
            scratch_shapes=[pltpu.VMEM((entries, features), jnp.bfloat16)] * 2,
        ),
        out_shape=[buffer, buffer],
        compiler_params=pltpu.CompilerParams(vmem_limit_bytes=36 * megabyte),
        cost_estimate=cost(1, 1),
    )(bit, *operands)


def adam_step(master, prior_first, prior_second, gradient, factor, rate, decay):
    clipped = gradient * factor
    moment = beta_first * prior_first + (1.0 - beta_first) * clipped
    variance = beta_second * prior_second + (1.0 - beta_second) * clipped * clipped
    ratio = (
        moment
        / (1.0 - beta_first**STEP)
        / (jnp.sqrt(variance / (1.0 - beta_second**STEP)) + adam_epsilon)
    )
    return (master - rate * (ratio + decay * master), moment, variance)


def adam_kernel(layout, group_count, bit_ref, total_ref, *refs):
    bit = bit_ref[0, 0]
    weights = len(layout)
    group_refs, refs = refs[:group_count], refs[group_count:]
    masters, firsts, seconds = (refs[k * weights : (k + 1) * weights] for k in range(3))
    loss_ref, norm_ref = refs[3 * weights : 3 * weights + 2]
    outs = refs[3 * weights + 2 :]
    share = total_ref.shape[0] - 8
    loss_ref[...] = total_ref[share : share + 1, 0:1]
    square_total = jnp.sum(
        jnp.sum(total_ref[0:share], axis=1, keepdims=True), axis=0, keepdims=True
    )
    norm_value = jnp.sqrt(square_total)
    norm_ref[...] = norm_value
    factor = clip_limit / jnp.maximum(norm_value, clip_limit)
    for place, layers in enumerate(layout):
        for at, pieces in enumerate(layers):
            for group, start, here, width in pieces:
                span = (slice(None), slice(here, here + width))
                span = (at, *span) if len(layers) > 1 else span
                there = (slice(None), slice(start, start + width))
                if isinstance(group, tuple):
                    first, half = group
                    gradient = jnp.where(
                        bit == half, group_refs[first][there], group_refs[first + 1][there]
                    )
                else:
                    gradient = group_refs[group][there]
                new = adam_step(
                    masters[place][span],
                    firsts[place][span],
                    seconds[place][span],
                    gradient,
                    factor,
                    learning_rates[place],
                    weight_decays[place],
                )
                for kind in range(3):
                    outs[kind * weights + place][span] = new[kind]


def adam_all(layout, bit, totals, groups, masters, firsts, seconds):
    arrays = [*masters, *firsts, *seconds]
    shapes = [jax.ShapeDtypeStruct(array.shape, jnp.float32) for array in arrays]
    scalar = jax.ShapeDtypeStruct((1, 1), jnp.float32)
    moved = sum(8 * array.size for array in arrays)
    return pl.pallas_call(
        functools.partial(adam_kernel, layout, len(groups)),
        in_specs=[pl.BlockSpec(memory_space=pltpu.SMEM)]
        + whole_in_vmem(1 + len(groups) + len(arrays)),
        out_specs=whole_in_vmem(2 + len(arrays)),
        out_shape=[scalar, scalar, *shapes],
        compiler_params=pltpu.CompilerParams(vmem_limit_bytes=16 * megabyte),
        cost_estimate=cost(2 * moved, moved),
    )(bit.reshape(1, 1), totals, *groups, *arrays)


def pad_columns(array, width):
    return jnp.pad(array, ((0, 0), (0, width - array.shape[1])))


def local(
    tokens,
    next_targets,
    triple_targets,
    loss_mask,
    embedding,
    attention,
    projection,
    expansion,
    contraction,
    readout,
    trigram,
    scales,
    *moments,
):
    masters = (embedding, attention, projection, expansion, contraction, readout, trigram, scales)
    firsts = moments[:8]
    seconds = moments[8:]
    bits = index_bits()
    seq_size, dp_size = lax.axis_size("seq"), lax.axis_size("dp")
    devices = seq_size * dp_size
    held, piece = tokens.shape
    length = piece * seq_size
    sequences = held * dp_size
    members = devices // sequences
    vocabulary, share = embedding.shape
    features = share * devices
    hidden_size = expansion.shape[2]
    rows = length // members
    shorts = rows // 3
    member_bits = [("dp", b) for b in reversed(bits_of("dp")) if b < members]
    member = lax.axis_index("dp") % members
    group = (lax.axis_index("seq") * dp_size + lax.axis_index("dp")) // members

    integers = jnp.stack(
        [tokens, next_targets, triple_targets.reshape(held, piece), loss_mask]
    ).astype(jnp.bfloat16)
    integers = integers.reshape(share, -1)
    integer_width = integers.shape[1]
    integer_room = -(-integer_width // 128) * 128
    down_low = jnp.swapaxes(lowered(contraction), 1, 2)
    attention_low, projection_low, expansion_low = map(lowered, (attention, projection, expansion))
    stages = stages_of(bits)

    def packed(parts):
        return jnp.concatenate(parts, axis=1)[None]

    first_parts = [
        pad_columns(integers, integer_room),
        pad_columns(lowered(scales).T, 128),
        lowered(embedding).T,
        attention_low[0],
    ]
    second_parts = [projection_low[0], expansion_low[0], down_low[0]]
    third_parts = [
        attention_low[1],
        projection_low[1],
        expansion_low[1],
        down_low[1],
        lowered(trigram),
        lowered(readout),
    ]
    third = lax.all_gather(jnp.concatenate(third_parts, axis=1), ("seq", "dp"), axis=0, tiled=True)
    first, second = packed(first_parts), packed(second_parts)
    behind = None
    for stage in reversed(stages):
        first = stage_blocks(first, stage)
        if behind is not None:
            second = stage_blocks(second, behind)
            terms = together(*first, *second)
            first, second = terms[: len(first)], jnp.concatenate(terms[len(first) :])
        behind = stage
        if stage is not stages[0]:
            first, second = together(jnp.concatenate(first), second)
    first_other = [swapped(piece, bits[-1]) for piece in first]
    second = stage_blocks(second, behind)
    all_integers, scale_columns, embed_columns, attend_zero = merge_blocks(
        first, first_other, [part.shape[1] for part in first_parts], bits
    )
    project_one_at = 3 * features
    expand_one_at = 4 * features
    down_one_at = expand_one_at + hidden_size
    tables_at = down_one_at + hidden_size
    scale_rows = scale_columns[:, :6].astype(jnp.float32).T
    all_integers = all_integers[:, :integer_width].reshape(
        seq_size, dp_size, 4, held, piece
    )
    mask_total = jnp.sum(all_integers[:, :, 3].astype(jnp.float32))
    inverse_total = 1.0 / jnp.maximum(mask_total, 1.0)
    sequence = lax.dynamic_slice(
        all_integers,
        (0, group // held, 0, group % held, 0),
        (seq_size, 1, 4, 1, piece),
    )
    sequence = jnp.swapaxes(sequence.reshape(seq_size, 4, piece), 0, 1).reshape(4, length)
    own = lax.dynamic_slice_in_dim(sequence, member * rows, rows, 1).astype(jnp.int32)
    sequence_tokens = sequence[0].astype(jnp.int32)
    own_tokens = own[0]
    main_columns = own[1:4:2].astype(jnp.float32)
    triple_columns = jnp.concatenate(
        [own[2].reshape(shorts, 3), own[3].reshape(shorts, 3)], 1
    ).T.astype(jnp.float32)

    letters = jnp.arange(vocabulary, dtype=jnp.int32)
    is_token = (own_tokens[:, None] == letters).astype(jnp.bfloat16)
    place = member * rows + jnp.arange(rows, dtype=jnp.int32)
    earlier = (jnp.arange(length, dtype=jnp.int32)[None, :] <= place[:, None]).astype(jnp.bfloat16)
    counts = contract(
        (sequence_tokens[:, None] == letters).astype(jnp.bfloat16), earlier, "tv,rt->vr"
    )
    table = embed_columns.astype(jnp.float32).T
    table_inverse = norm_scale(table)
    table_normed = lowered(table * table_inverse * scale_rows[0])
    table_qkv = lowered(contract(table_normed, attend_zero, "vd,dc->vc"))
    queries = lowered(contract(is_token, table_qkv[:, :features], "rv,vc->rc"))
    counts, main_columns, triple_columns, mask_total, scale_rows = together(
        counts, main_columns, triple_columns, mask_total, scale_rows
    )
    mixed_low, shares = weighted_attention(queries, table_qkv, counts)
    second_other = [swapped(piece, bits[-1]) for piece in second[:-1]]
    mixed_low, last_piece = together(mixed_low, second[-1])
    second = [*second[:-1], last_piece]
    second_other.append(swapped(last_piece, bits[-1]))
    project_zero, expand_zero, down_zero = merge_blocks(
        second, second_other, [part.shape[1] for part in second_parts], bits
    )
    first_stream, normed_zero, hidden, last = first_layer_end(
        is_token,
        embed_columns,
        mixed_low,
        project_zero,
        expand_zero,
        down_zero,
        scale_rows[1:2],
    )

    normed_other = swapped(normed_zero, bits[-1])

    along = [(i, i + 1) for i in range(dp_size - 1) if (i + 1) % members]
    back = [(i + 1, i) for i, _ in along]
    previous = lax.ppermute(last, "dp", along)
    pooled, pooled_normed, short_queries, pairs = pooled_rows(
        first_stream, previous, third, scale_rows[2:3], shorts
    )
    pairs = stage_blocks(pairs, member_bits)
    (
        loss_local,
        merged_grad,
        table_sent,
        table_kept,
        short_mixed_low,
        short_hidden,
        short_normed,
        short_grad,
        short_low,
        short_shares,
        head_scales,
    ) = upper_layer(
        jnp.stack([own_bit(bits[-1]), member]),
        mask_total,
        short_queries,
        pairs,
        pooled,
        first_stream,
        scale_rows[3:6],
        third,
        (project_one_at, expand_one_at, down_one_at, tables_at),
        hidden_size,
        vocabulary,
        main_columns,
        triple_columns,
        share,
    )

    bit = own_bit(bits[-1])
    none = jnp.zeros((8, features), jnp.float32)
    upper, grad, other_grad, gradient = feed_back(
        short_grad,
        none,
        [swapped(short_low, bits[-1])],
        none,
        short_normed,
        swapped(short_normed, bits[-1]),
        (third, expand_one_at),
        (third, down_one_at),
        hidden_size,
        upper_steps,
        stages[0],
        bit,
        share,
    )
    grad, other_grad, gradient, *upper = together(grad, other_grad, gradient, *upper)
    upper = stage_sums(upper, stages[0])
    count = len(upper)
    short_hidden_low, short_hidden_grad, query_grad, pair_grads, feed_one_scale = upper_back(
        grad,
        swapped(other_grad, bits[-1]),
        short_hidden,
        gradient,
        scale_rows[3:4],
        third,
        project_one_at,
        short_queries,
        short_shares,
        pairs,
    )
    pair_grads = stage_sums(pair_grads, member_bits)
    *middle, rows_grad, rows_left, rows_right, returned, attend_one_scale = middle_gradients(
        bits,
        query_grad,
        pair_grads,
        pooled_normed,
        short_mixed_low,
        short_hidden_low,
        pooled,
        short_hidden_grad,
        merged_grad,
        third,
        scale_rows[2:3],
        share,
    )

    rows_left, rows_right = swapped(rows_left, bits[-1]), swapped(rows_right, bits[-1])
    middle = [[middle[4 + k], swapped(middle[k], bits[-1])] for k in range(4)]
    tables = [table_kept, swapped(table_sent, bits[-1])]
    middle = add_and_split([tables, *middle], stages[0])
    after_next = [(i + 2, i) for i in range(dp_size - 2) if i % members < members - 2]
    if after_next:
        later = lax.ppermute(returned, "dp", after_next)
    else:
        later = jnp.zeros_like(returned)
    other_back = jnp.where(member % 2 == 1, returned, later)
    returned = lax.ppermute(returned, "dp", back)
    rows_grad, rows_left, rows_right, returned, other_back, *terms = together(
        rows_grad, rows_left, rows_right, returned, other_back, *middle, *upper
    )
    middle, upper = stage_sums(terms[:count], stages[0]), terms[count:]
    fed, grad, other_grad, gradient = feed_back(
        rows_grad,
        returned,
        [rows_left, rows_right],
        other_back,
        normed_zero,
        normed_other,
        (expand_zero, 0),
        (down_zero, 0),
        hidden_size,
        feed_steps,
        stages[0],
        bit,
        share,
    )
    grad, other_grad, gradient, *terms = together(grad, other_grad, gradient, *fed, *middle)
    fed, middle = stage_sums(terms[:count], stages[0]), terms[count:]
    came = swapped(other_grad, bits[-1])
    came, *upper = together(came, *add_and_split([upper, middle], stages[1]))
    upper = stage_sums(upper, stages[1])
    lower = lower_gradients(
        own_bit(bits[-1]).reshape(1),
        grad,
        came,
        hidden,
        gradient,
        scale_rows[1:2],
        project_zero,
        queries,
        table_qkv,
        shares,
        is_token,
        mixed_low,
        embed_columns,
        attend_zero,
        scale_rows[0:1],
        attend_one_scale,
        feed_one_scale,
        head_scales,
        share,
    )

    *upper, later = upper
    sent, kept, *terms = together(*lower, *fed, *upper)
    fed, upper = terms[:count], terms[count:]
    lower = [kept, swapped(sent, bits[-1])]
    lower, *fed = together(tuple(add_and_split([lower], stages[0], False)), *fed)
    lower = stage_sums(lower, stages[0])
    fed = stage_sums(add_and_split([fed], stages[1]), stages[1])
    terms = together(*fed, *lower, later)
    upper, fed = [*upper, terms[-1]], terms[: len(fed)]
    lower = stage_sums(add_and_split([terms[len(fed) : -1]], stages[1]), stages[1])
    groups = (upper, fed, lower)
    for stage in stages[2:]:
        groups = [stage_sums(add_and_split([terms], stage), stage) for terms in groups]
    both = 2 * hidden_size
    upper, fed, lower = groups
    upper_rest, upper_mine, upper_other, square = add_and_square(
        bit, loss_local, [], upper, upper_steps, both
    )
    fed_mine, fed_other, square = add_and_square(
        bit, loss_local, [square], fed, feed_steps, both
    )
    upper_came, fed_came = swapped(upper_other, bits[-1]), swapped(fed_other, bits[-1])
    lower_sum, totals = add_and_square(bit, loss_local, [square], lower, 0, 0)
    for stage in [[bits[-1]], stages[0]]:
        totals = sum(stage_sums([totals] * (1 << len(stage)), stage))
    for stage in stages[1:]:
        totals = sum(stage_sums([totals] * (1 << len(stage)), stage))
    def fed_at(group, kind, steps):
        width = hidden_size // (2 * steps)
        return [
            ((group, half), (2 * j + kind) * width, (half * steps + j) * width, width)
            for half in range(2)
            for j in range(steps)
        ]

    groups = [upper_rest, lower_sum, upper_mine, upper_came, fed_mine, fed_came]
    scale_at = 4 * features + vocabulary
    groups.append(lower_sum[:, scale_at : scale_at + 6].T)
    attend_at = 4 * vocabulary
    layout = (
        ([(1, 4 * features, 0, vocabulary)],),
        ([(1, features, 0, 3 * features)], [(0, attend_at, 0, 3 * features)]),
        ([(1, 0, 0, features)], [(0, attend_at + 3 * features, 0, features)]),
        (fed_at(4, 1, feed_steps), fed_at(2, 1, upper_steps)),
        (fed_at(4, 0, feed_steps), fed_at(2, 0, upper_steps)),
        ([(0, 0, 0, vocabulary)],),
        ([(0, vocabulary, 0, 3 * vocabulary)],),
        ([(6, 0, 0, share)],),
    )

    def turned(arrays):
        embed, attend, project, expand, down, *rest = arrays
        return (embed.T, attend, project, expand, jnp.swapaxes(down, 1, 2), *rest)

    late = lax.optimization_barrier(
        (turned(masters), turned(firsts), turned(seconds), lower[0])
    )
    loss_total, norm_value, *results = adam_all(
        layout, bit, totals, groups, *late[:3]
    )
    return (
        loss_total.reshape(()),
        mask_total,
        norm_value.reshape(()),
        *turned(results[:8]),
        *turned(results[8:16]),
        *turned(results[16:]),
    )


def solution(mesh):
    weight_specs = (
        P(None, ("seq", "dp")),
        P(None, ("seq", "dp"), None),
        P(None, ("seq", "dp"), None),
        P(None, ("seq", "dp"), None),
        P(None, None, ("seq", "dp")),
        P(("seq", "dp"), None),
        P(("seq", "dp"), None),
        P(None, ("seq", "dp")),
    )
    in_specs = (
        P("dp", "seq"),
        P("dp", "seq"),
        P("dp", "seq", None),
        P("dp", "seq"),
    ) + weight_specs * 3
    out_specs = (P(), P(), P()) + weight_specs * 3
    return jax.shard_map(local, mesh=mesh, in_specs=in_specs, out_specs=out_specs, check_vma=False)
```
